32 devices in a mesh: batch: 8 (over z, x), tm: 4 (over y, core).
Axes of the slice: x: 2, y: 2, z: 4, core: 2. Of those that a mesh axis runs over, the one named last changes fastest.
Arguments:
- phonemes: bfloat16 [8192, 512], P('batch'), may hold values from -6 to 6
- durations: int32 [8, 1024], P('batch'), may hold values from 1 to 16, 4096 in all within a row
- utt_frames: int32 [8, 4], P('batch'), may hold values from 192 to 3328, as said below
- style_codes: float32 [32, 128], P('batch'), may hold values from -3 to 3
- fc_weight: float32 [4, 128, 1024], replicated, may hold values from -0.5 to 0.5
- fc_bias: float32 [4, 1024], replicated, may hold values from -1.5 to 1.5
- conv_weight: bfloat16 [4, 1536, 512], replicated, may hold values from -0.15625 to 0.15625
- conv_bias: float32 [2, 512], replicated, may hold values from -1.5 to 1.5
- cotangent: bfloat16 [32768, 512], P(('batch', 'tm')), may hold values from -6 to 6
Outputs:
- frames_out: bfloat16 [32768, 512], P(('batch', 'tm'))
- phoneme_grad: float32 [8192, 512], P('batch')
- style_grad: float32 [32, 128], P('batch')
- fc_weight_grad: float32 [4, 128, 1024], replicated
- fc_bias_grad: float32 [4, 1024], replicated
- conv_weight_grad: float32 [4, 1536, 512], replicated
- conv_bias_grad: float32 [2, 512], replicated
The draws below stay inside these ranges and needn't reach their ends.
Inputs may be any that keep to these rules, and one draw needn't show every extreme that they name: `utt_frames`: the lengths of a group sum to 4096.
All inputs are finite; a program needn't handle non-finite values.
Results may differ from the reference program's by a relative error of at most 0.009.
Values may be sent and summed in bfloat16 or wider, within the bound.
A program may use at most 192 MiB of HBM per device.

```python
import math
import jax
import jax.numpy as jnp
import numpy as np
from jax import lax

D = 512
STY = 128
FR_DEV = 1024
UTT = 4
DMAX = 16
GROUP_FRAMES = 4096
GROUP_PHONES = 1024
FRAMES = 32768
PHONES = 8192
UTTS = 32
N_BATCH = 8
N_TM = 4


def draw_utt_frames(key, part):
    key = jax.random.fold_in(key, 7)
    quarter = FR_DEV // 4
    step_size = FR_DEV // 16
    lengths = jnp.array([GROUP_FRAMES - 3 * quarter, quarter - step_size, quarter, quarter + step_size], dtype=jnp.int32)
    row_keys = jax.random.split(key, N_BATCH)
    return jax.vmap(lambda row_key: jax.random.permutation(row_key, lengths))(row_keys)


def levels(rng, extent, shards, low, largest):
    def one(dim, parts):
        steps = jax.random.uniform(jax.random.fold_in(jax.random.fold_in(rng, 6), dim), (parts,), jnp.float32, low / len(shards), largest / len(shards))
        return jnp.repeat(jnp.exp(steps), extent[dim] // parts).reshape((-1,) + (1,) * (len(extent) - dim - 1))

    factor_of = one(*shards[0])
    for cut in shards[1:]:
        factor_of = factor_of * one(*cut)
    return factor_of


def profile(amount, total, limit, slope):
    weights = [(1 << 20) // math.isqrt(standing ** slope) + 1 for standing in range(2, amount + 1)]
    rest, given = total - limit - (amount - 1), [1] * (amount - 1)
    while rest > 0:
        free = [i for i in range(amount - 1) if given[i] < limit]
        pool, remaining = sum([weights[i] for i in free]), rest
        for i in free:
            extra = min(limit - given[i], max(1, remaining * weights[i] // pool), rest)
            given[i] = given[i] + extra
            rest = rest - extra
    return np.array([limit] + given)


def ragged(stream_key, count, total, reach, lean):
    if count == 2:
        one = jax.random.randint(stream_key, (), max(1, total - reach), min(reach, total - 1) + 1)
        return jnp.stack([one, total - one])
    tallies = jnp.asarray(profile(count, total, reach, lean), jnp.int32)
    couples = (count - 1) // 2
    source_of, sink = tallies[1:1 + 2 * couples:2], tallies[2:2 + 2 * couples:2]
    room = jnp.minimum(source_of - 1, reach - sink)
    moved = jax.random.randint(jax.random.fold_in(stream_key, 1), (couples,), 0, 1 << 20) % (room + 1)
    tallies = tallies.at[1:1 + 2 * couples:2].set(source_of - moved).at[2:2 + 2 * couples:2].set(sink + moved)
    return tallies[jax.random.permutation(jax.random.fold_in(stream_key, 2), count)]


def noise(own_key, extent, width, most, cuts=(), held_as=jnp.bfloat16):
    values = jax.random.normal(own_key, extent, jnp.float32) * width
    if len(cuts) > 0:
        values = levels(own_key, extent, cuts, -0.22, 0.18) * values
    return jnp.clip(values, min=-most, max=most).astype(held_as)


def setup_inputs(seed: int = 0) -> dict:
    arg_keys = jax.random.split(jax.random.key(seed), 10)
    phonemes = noise(arg_keys[0], (PHONES, D), 1.0, 6.0, ((0, 8),))
    durations = jax.vmap(lambda own: ragged(own, GROUP_PHONES, GROUP_FRAMES, DMAX, 2))(jax.random.split(arg_keys[1], N_BATCH)).reshape((N_BATCH, GROUP_PHONES)).astype(jnp.int32)
    utt_frames = draw_utt_frames(jax.random.fold_in(arg_keys[9], 71), 0)
    style_codes = noise(arg_keys[3], (UTTS, STY), 0.5, 3.0, ((0, 8),), jnp.float32)
    fc_weight = noise(arg_keys[4], (4, STY, 2 * D), STY ** -0.5, 0.5, (), jnp.float32)
    fc_bias = noise(arg_keys[5], (4, 2 * D), 0.3, 1.5, (), jnp.float32)
    conv_weight = noise(arg_keys[6], (4, 3 * D, D), (3 * D) ** -0.5, 0.15625)
    conv_bias = noise(arg_keys[7], (2, D), 0.3, 1.5, (), jnp.float32)
    cotangent = noise(arg_keys[8], (FRAMES, D), 1.0, 6.0, ((0, 32),))
    return {"phonemes": phonemes, "durations": durations, "utt_frames": utt_frames, "style_codes": style_codes, "fc_weight": fc_weight, "fc_bias": fc_bias, "conv_weight": conv_weight, "conv_bias": conv_bias, "cotangent": cotangent}


@jax.custom_vjp
def low(v):
    return lax.optimization_barrier(v.astype(jnp.bfloat16)).astype(jnp.float32)

@jax.custom_vjp
def low_back(v):
    return v

def low_keep(v):
    return (low(v), None)

def low_pass(kept, grad):
    return (grad,)

def back_keep(v):
    return (v, None)

def back_low(kept, grad):
    return (low(grad),)
low.defvjp(low_keep, low_pass)
low_back.defvjp(back_keep, back_low)
highest = lax.Precision.HIGHEST
norm_eps = 1e-05
root_half = 0.7071067811865476

def adain(stream, member, counts, styles, weight, biases):
    channels = stream.shape[1]
    modulation = jnp.dot(styles, weight, precision=highest) + biases
    averages = jnp.dot(member.T, stream, precision=highest) / counts[:, None]
    centered = stream - jnp.dot(member, averages, precision=highest)
    spread = jnp.dot(member.T, centered * centered, precision=highest) / counts[:, None]
    scales = lax.rsqrt(spread + norm_eps)
    normed = centered * jnp.dot(member, scales, precision=highest)
    per_frame = jnp.dot(member, modulation, precision=highest)
    return (1.0 + per_frame[:, :channels]) * normed + per_frame[:, channels:]

def convolve(activated, weight, before_mask, after_mask):
    channels = activated.shape[1]
    zeros_row = jnp.zeros((1, channels), jnp.float32)
    preceding = jnp.concatenate([zeros_row, activated[:-1]], 0) * before_mask[:, None]
    following = jnp.concatenate([activated[1:], zeros_row], 0) * after_mask[:, None]
    return jnp.dot(preceding, weight[:channels], precision=highest) + jnp.dot(activated, weight[channels:2 * channels], precision=highest) + jnp.dot(following, weight[2 * channels:], precision=highest)

def group_forward(phone_rows, styles, fc_w, fc_b, conv_w, conv_b, phone_index, member, counts, before_mask, after_mask):
    stream = low_back(jnp.take(phone_rows, phone_index, axis=0))
    for blocks in range(2):
        first = low(jax.nn.silu(adain(stream, member, counts, styles, fc_w[2 * blocks], fc_b[2 * blocks])))
        middle = low_back(convolve(first, conv_w[2 * blocks], before_mask, after_mask))
        second = low(jax.nn.silu(adain(middle, member, counts, styles, fc_w[2 * blocks + 1], fc_b[2 * blocks + 1])))
        branch = low_back(convolve(second, conv_w[2 * blocks + 1], before_mask, after_mask))
        stream = (branch + conv_b[blocks] + stream) * root_half
    return stream

def reference(phonemes, durations, utt_frames, style_codes, fc_weight, fc_bias, conv_weight, conv_bias, cotangent):
    group_frames = FR_DEV * N_TM
    phone_groups = phonemes.astype(jnp.float32).reshape(N_BATCH, -1, D)
    style_groups = style_codes.reshape(N_BATCH, UTT, STY)
    cot_groups = cotangent.astype(jnp.float32).reshape(N_BATCH, group_frames, D)
    conv_float = conv_weight.astype(jnp.float32)
    positions = jnp.arange(group_frames, dtype=jnp.int32)

    def one_group(running, inputs):
        phone_rows, styles, cot_rows, duration_row, length_row = inputs
        phone_ends = jnp.cumsum(duration_row, dtype=jnp.int32)
        phone_index = jnp.searchsorted(phone_ends, positions, side='right').astype(jnp.int32)
        bounds = jnp.cumsum(length_row, dtype=jnp.int32)
        utterance = jnp.searchsorted(bounds, positions, side='right').astype(jnp.int32)
        member = (utterance[:, None] == jnp.arange(UTT, dtype=jnp.int32)[None, :]).astype(jnp.float32)
        counts = length_row.astype(jnp.float32)
        shifted_down = jnp.concatenate([utterance[:1], utterance[:-1]], 0)
        shifted_up = jnp.concatenate([utterance[1:], utterance[-1:] + 1], 0)
        before_mask = ((positions >= 1) & (shifted_down == utterance)).astype(jnp.float32)
        after_mask = (shifted_up == utterance).astype(jnp.float32)

        def forward(phone_in, styles_in, fcw, fcb, convw, convb):
            return group_forward(phone_in, styles_in, fcw, fcb, convw, convb, phone_index, member, counts, before_mask, after_mask)
        result, pullback = jax.vjp(forward, phone_rows, styles, fc_weight, fc_bias, conv_float, conv_bias)
        grads = pullback(cot_rows)
        running = tuple((total_sum + grad_part for total_sum, grad_part in zip(running, grads[2:])))
        return (running, (result, grads[0], grads[1]))
    start_sums = (jnp.zeros_like(fc_weight), jnp.zeros_like(fc_bias), jnp.zeros_like(conv_float), jnp.zeros_like(conv_bias))
    sums_out, per_group = lax.scan(one_group, start_sums, (phone_groups, style_groups, cot_groups, durations, utt_frames))
    frames_out = per_group[0].reshape(-1, D).astype(jnp.bfloat16)
    phoneme_grad = per_group[1].reshape(-1, D)
    style_grad = per_group[2].reshape(-1, STY)
    return (frames_out, phoneme_grad, style_grad, sums_out[0], sums_out[1], sums_out[2], sums_out[3])
```

```python
import functools
import jax
import jax.numpy as jnp
from jax import lax
from jax.experimental import pallas as pl
from jax.experimental.pallas import tpu as pltpu
from jax.sharding import PartitionSpec as P

F32, BF16 = jnp.float32, jnp.bfloat16
MESH = pl.DeviceIdType.MESH
highest = lax.Precision.HIGHEST
norm_eps = 1e-05
root_half = 0.7071067811865476
UTT = 4
CORES = 2
OUTER = 4
WIDE = 128


def dot(left, right):
    return jnp.dot(left, right, preferred_element_type=F32)


def dot_rows(left, right):
    return lax.dot_general(left, right, (((0,), (0,)), ((), ())), preferred_element_type=F32)


def dot_back(left, right, precision=None):
    return lax.dot_general(
        left, right, (((1,), (1,)), ((), ())), precision=precision, preferred_element_type=F32
    )


def split3(values):
    high = values.astype(BF16).astype(F32)
    rest = values - high
    mid = rest.astype(BF16).astype(F32)
    return jnp.concatenate([high, mid, rest - mid, jnp.zeros_like(values)], axis=0).astype(BF16)


def kernel(
    inner,
    members,
    phon_hbm,
    dur_ref,
    utt_ref,
    style_ref,
    fcw_hbm,
    fcb_ref,
    cw_hbm,
    cb_ref,
    cot_hbm,
    frames_ref,
    pg_ref,
    styleg_ref,
    gat_ref,
    wg_ref,
    phon,
    fcw,
    cw,
    cot,
    pick,
    mem,
    memt,
    amask,
    bmask,
    x0,
    vs,
    piv,
    asave,
    sh,
    x3,
    dyb,
    mod,
    sv,
    coef,
    st,
    brow,
    fx,
    bx,
    prcv0,
    wsnd,
    wkeep,
    wrcv0,
    rcv1,
    acc2,
    rcv2,
    acc3,
    rcv3,
    acc4,
    lsem,
    csem,
    xs_sem,
    xr_sem,
    gs_sem,
    gr_sem,
    ps_sem,
    pr_sem,
    ws_sem,
    wr_sem,
):
    T, C = cot_hbm.shape
    PH = phon_hbm.shape[0]
    yn = members // CORES
    batch = lax.axis_index("batch")
    time = lax.axis_index("tm")
    bo, bi = batch // inner, batch % inner
    ty, core = time // CORES, time % CORES
    R = 256
    t0 = time * T

    loads = [
        pltpu.make_async_copy(phon_hbm, phon, lsem.at[0]),
        pltpu.make_async_copy(fcw_hbm, fcw, lsem.at[1]),
        pltpu.make_async_copy(cot_hbm, cot, lsem.at[2]),
    ] + [pltpu.make_async_copy(cw_hbm.at[n], cw.at[n], lsem.at[3 + n]) for n in range(4)]
    for load in loads:
        load.start()

    def on_tm(o):
        return (batch, lax.rem(time + o, members))

    def on_core():
        return (batch, ty * CORES + (1 - core))

    def on_y(o):
        return (batch, lax.rem(ty + o, yn) * CORES + core)

    def on_inner(o):
        return (bo * inner + lax.rem(bi + o, inner), time)

    def on_outer(o):
        return (lax.rem(bo + o, OUTER) * inner + bi, time)

    partners = (
        [on_tm(o) for o in range(1, members)]
        + [on_inner(o) for o in range(1, inner)]
        + [on_outer(o) for o in range(1, OUTER)]
    )
    barrier = pltpu.get_barrier_semaphore()
    for partner in partners:
        pl.semaphore_signal(barrier, inc=1, device_id=partner, device_id_type=MESH)

    def remote(src, dst, ssem, rsem, device):
        return pltpu.make_async_remote_copy(
            src_ref=src,
            dst_ref=dst,
            send_sem=ssem,
            recv_sem=rsem,
            device_id=device,
            device_id_type=MESH,
        )

    unsent = []

    def send(src, dst, ssem, rsem, device):
        copy = remote(src, dst, ssem, rsem, device)
        copy.start()
        unsent.append(copy)

    def drain():
        for copy in unsent:
            copy.wait_send()
        unsent.clear()

    lens = [utt_ref[0, u] for u in range(UTT)]
    starts, ends, total = [], [], 0
    for u in range(UTT):
        starts.append(total)
        total = total + lens[u]
        ends.append(total)
    row8 = lax.broadcasted_iota(jnp.int32, (8, C), 0)

    def by_utt(values, other):
        out = jnp.full((8, C), other, F32)
        for u in range(UTT):
            out = jnp.where(row8 == u, values[u], out)
        return out

    def local_counts(j):
        return by_utt(
            [
                jnp.maximum(jnp.minimum(ends[u], (j + 1) * T) - jnp.maximum(starts[u], j * T), 0)
                .astype(F32)
                for u in range(UTT)
            ],
            0.0,
        )

    totals = by_utt([n.astype(F32) for n in lens], 1.0)
    inv_totals = 1.0 / totals
    mine = local_counts(time)
    inv_mine = 1.0 / jnp.maximum(mine, 1.0)

    def owner_rows(t):
        return [
            jnp.logical_and(t >= starts[u], t < ends[u]).astype(F32) for u in range(UTT)
        ]

    first_own, last_own = owner_rows(t0), owner_rows(t0 + T - 1)

    def pick_row(values, own):
        out = own[0] * values[0:1]
        for u in range(1, UTT):
            out = out + own[u] * values[u : u + 1]
        return out

    coef[...] = jnp.zeros_like(coef)

    @pl.loop(0, T // WIDE)
    def _(i):
        r0 = pl.multiple_of(i * WIDE, WIDE)
        t = lax.broadcasted_iota(jnp.int32, (WIDE, WIDE), 0) + r0 + t0
        lane = lax.broadcasted_iota(jnp.int32, (WIDE, WIDE), 1)
        before, after = t >= 1, t >= 0
        own = jnp.zeros((WIDE, WIDE), F32)
        slot = lax.rem(lane, 8)
        for u in range(UTT):
            before = jnp.logical_and(before, t != starts[u])
            after = jnp.logical_and(after, t + 1 != ends[u])
            inside = jnp.logical_and(t >= starts[u], t < ends[u])
            own = jnp.where(jnp.logical_and(inside, slot == u), 1.0, own)
        own = jnp.where(lane < 24, own, 0.0)
        mem[pl.ds(r0, WIDE), :] = own.astype(BF16)
        bmask[pl.ds(r0, WIDE), :] = before.astype(F32)
        amask[pl.ds(r0, WIDE), :] = after.astype(F32)
        tt = lax.broadcasted_iota(jnp.int32, (16, WIDE), 1) + r0 + t0
        row = lax.broadcasted_iota(jnp.int32, (16, WIDE), 0)
        ownt = jnp.zeros((16, WIDE), F32)
        for u in range(UTT):
            inside = jnp.logical_and(tt >= starts[u], tt < ends[u])
            ownt = jnp.where(jnp.logical_and(inside, row == u), 1.0, ownt)
        memt[:, pl.ds(r0, WIDE)] = ownt.astype(BF16)

    tiles = PH // WIDE
    durs = jnp.concatenate(
        [dur_ref[0:1, j * WIDE : (j + 1) * WIDE] for j in range(tiles)], axis=0
    ).astype(F32)
    upper = (
        lax.broadcasted_iota(jnp.int32, (WIDE, WIDE), 0)
        <= lax.broadcasted_iota(jnp.int32, (WIDE, WIDE), 1)
    ).astype(BF16)
    within = dot(durs.astype(BF16), upper)
    so_far = jnp.zeros((1, 1), F32)
    for j in range(tiles):
        stop = within[j : j + 1] + so_far
        begin = (stop - durs[j : j + 1]).astype(jnp.int32)
        stop = stop.astype(jnp.int32)
        so_far = so_far + within[j : j + 1, WIDE - 1 : WIDE]
        t = lax.broadcasted_iota(jnp.int32, (T, WIDE), 0) + t0
        inside = jnp.logical_and(t >= begin, t < stop)
        pick[:, j * WIDE : (j + 1) * WIDE] = jnp.where(inside, 1.0, 0.0).astype(BF16)

    loads[0].wait()

    @pl.loop(0, T // R)
    def _(i):
        r0 = pl.multiple_of(i * R, R)
        x0[pl.ds(r0, R), :] = dot(pick[pl.ds(r0, R), :], phon[...]).astype(BF16)

    def value(n, rows):
        if n == 0:
            return x0[rows, :].astype(F32) - piv[0:1, :]
        return vs[n - 1, rows, :]

    def add_stats(rows, one, two):
        both = jnp.concatenate([one.astype(BF16), two.astype(BF16)], axis=1)
        st[...] += dot(memt[:, rows], both)

    st[...] = jnp.zeros_like(st)
    piv[0:8, :] = jnp.broadcast_to(x0[0:16, :].astype(F32)[0:1], (8, C))

    @pl.loop(0, T // R)
    def _(i):
        rows = pl.ds(pl.multiple_of(i * R, R), R)
        d = value(0, rows)
        add_stats(rows, d, d * d)

    loads[1].wait()
    style8 = jnp.concatenate(
        [style_ref[...], jnp.zeros((8 - UTT, style_ref.shape[1]), F32)], axis=0
    )
    for n in range(4):
        mod[n] = dot_general_exact(style8, fcw[n]) + fcb_ref[n : n + 1, :]

    loads[2].wait()
    cot_first = cot[0:16, :].astype(F32)[0:1]
    cot_last = cot[T - 16 : T, :].astype(F32)[15:16]

    pl.semaphore_wait(barrier, len(partners))

    def exchange(buf, phase, full):
        for o in range(1, members):
            rows = 16 if full or o in (1, members - 1) else 8
            send(
                buf.at[time, pl.ds(0, rows)],
                buf.at[time, pl.ds(0, rows)],
                xs_sem.at[phase, o],
                xr_sem.at[phase, o],
                on_tm(o),
            )

    def exchanged(buf, phase, full):
        for o in range(1, members):
            rows = 16 if full or o in (1, members - 1) else 8
            ref = buf.at[lax.rem(time + members - o, members), pl.ds(0, rows)]
            remote(ref, ref, xs_sem.at[phase, o], xr_sem.at[phase, o], on_tm(o)).wait_recv()

    before_me, after_me = lax.rem(time + members - 1, members), lax.rem(time + 1, members)

    def forward_send(n, first, last):
        p = piv[8 * n : 8 * n + 1, :]
        s1, s2 = st[0:8, 0:C], st[0:8, C : 2 * C]
        local = s1 * inv_mine
        fx[n, time, 0:4, :] = (local + p)[0:4]
        fx[n, time, 4:8, :] = (s2 - s1 * local)[0:4]
        fx[n, time, 8:9, :] = first + p
        fx[n, time, 9:10, :] = last + p
        fx[n, time, 10:11, :] = cot_first
        fx[n, time, 11:12, :] = cot_last
        fx[n, time, 12:16, :] = jnp.zeros((4, C), F32)
        exchange(fx.at[n], n, False)

    def forward_norm(n):
        exchanged(fx.at[n], n, False)
        p = piv[8 * n : 8 * n + 1, :]
        zero4 = jnp.zeros((4, C), F32)
        counts = [local_counts(j) for j in range(members)]
        means = [
            jnp.concatenate([fx[n, j, 0:4, :], zero4], axis=0) for j in range(members)
        ]
        mean = counts[0] * means[0]
        for j in range(1, members):
            mean = mean + counts[j] * means[j]
        mean = mean * inv_totals
        spread = jnp.zeros((8, C), F32)
        for j in range(members):
            off = means[j] - mean
            spread = spread + counts[j] * off * off + jnp.concatenate(
                [fx[n, j, 4:8, :], zero4], axis=0
            )
        scale = lax.rsqrt(jnp.maximum(spread * inv_totals, 0.0) + norm_eps)
        gain, shift = 1.0 + mod[n, :, 0:C], mod[n, :, C : 2 * C]
        slope = gain * scale
        mean = mean - p
        half_a, half_b = 0.5 * slope, 0.5 * (shift - slope * mean)
        sv[n, 0] = half_a
        sv[n, 1] = half_b
        sv[n, 2] = scale
        sv[n, 3] = mean
        sv[n, 4] = gain
        coef[0:32, 0 : 2 * C] = split3(jnp.concatenate([half_a, half_b], axis=1))

        def edge(raw, own):
            h = pick_row(half_a, own) * (raw - p) + pick_row(half_b, own)
            return h + h * jnp.tanh(h)

        sh[7:8, :] = edge(fx[n, before_me, 9:10, :], first_own)
        sh[T + 8 : T + 9, :] = edge(fx[n, after_me, 8:9, :], last_own)

        @pl.loop(0, T // R)
        def _(i):
            r0 = pl.multiple_of(i * R, R)
            rows = pl.ds(r0, R)
            spread_out = dot(mem[rows, :], coef[:, 0 : 2 * C])
            h = spread_out[:, 0:C] * value(n, rows) + spread_out[:, C : 2 * C]
            a = h + h * jnp.tanh(h)
            sh[pl.ds(pl.multiple_of(r0 + 8, 8), R), :] = a
            asave[n, rows, :] = a.astype(BF16)

    def shifted(r0):
        window = sh[pl.ds(r0, R + 16), :]
        rows = pl.ds(r0, R)
        bm = jnp.concatenate([bmask[rows, :]] * (C // WIDE), axis=1)
        am = jnp.concatenate([amask[rows, :]] * (C // WIDE), axis=1)
        return (
            (window[7 : 7 + R] * bm).astype(BF16),
            (window[9 : 9 + R] * am).astype(BF16),
            window[8 : 8 + R],
        )

    def forward_conv(n):
        loads[3 + n].wait()
        st[...] = jnp.zeros_like(st)

        @pl.loop(0, T // R)
        def _(i):
            r0 = pl.multiple_of(i * R, R)
            rows = pl.ds(r0, R)
            prev, following, _ = shifted(r0)
            c = dot(jnp.concatenate([prev, asave[n, rows, :], following], axis=1), cw[n])
            if n % 2 == 1:
                b = n // 2
                kept = x0[rows, :].astype(F32) if n == 1 else vs[1, rows, :] + piv[16:17, :]
                c = (c + cb_ref[b : b + 1, :] + kept) * root_half
            if n == 3:
                frames_ref[rows, :] = c.astype(BF16)
                return

            @pl.when(i == 0)
            def _():
                m = jnp.mean(c, axis=0, keepdims=True)
                piv[8 * (n + 1) : 8 * (n + 2), :] = jnp.broadcast_to(m, (8, C))

            d = c - piv[8 * (n + 1) : 8 * (n + 1) + 1, :]
            vs[n, rows, :] = d
            add_stats(rows, d, d * d)

    first16 = x0[0:16, :].astype(F32)
    last16 = x0[T - 16 : T, :].astype(F32)
    p0 = piv[0:1, :]
    forward_send(0, first16[0:1] - p0, last16[15:16] - p0)
    for n in range(4):
        forward_norm(n)
        forward_conv(n)
        if n < 3:
            forward_send(n + 1, vs[n, 0:1, :], vs[n, T - 1 : T, :])
    drain()

    axes = {
        "y": (yn, ty, on_y),
        "x": (inner, bi, on_inner),
        "z": (OUTER, bo, on_outer),
    }
    half = C // 2

    def plan(u):
        order = "xy" if u % 2 == 0 else "yx"
        return axes[order[0]], axes[order[1]], axes["z"]

    def out_rows(u, side, start, count):
        n, k = u // 3, u % 3
        base = k * C + side * half + start
        return wg_ref.at[n, pl.ds(pl.multiple_of(base, 16), count)]

    def slots(u):
        (k1, _, _), (k2, _, _), (k3, _, _) = plan(u)
        base = [0, 1, k1, k1 + k2 - 1]
        width = k1 + k2 + k3 - 2
        return base, width

    def reduce_step(u, s):
        (k1, m1, d1), (k2, m2, d2), (k3, m3, d3) = plan(u)
        base, width = slots(u)
        r1, r2, w3 = half // k1, half // k1 // k2, C // k3
        sems = lambda slot: (ws_sem.at[u, slot], wr_sem.at[u, slot])
        if s == 0:
            send(wsnd.at[u], wrcv0.at[u], *sems(0), on_core())
        elif s == 1:
            remote(wsnd.at[u], wrcv0.at[u], *sems(0), on_core()).wait_recv()
            wkeep[u] = (wkeep[u].astype(F32) + wrcv0[u].astype(F32)).astype(BF16)
            for o in range(1, k1):
                piece = wkeep.at[u, pl.ds(pl.multiple_of(lax.rem(m1 + o, k1) * r1, 16), r1)]
                send(piece, rcv1.at[u, m1], *sems(base[1] + o - 1), d1(o))
        elif s == 2:
            own = wkeep[u, pl.ds(pl.multiple_of(m1 * r1, 16), r1), :].astype(F32)
            for o in range(1, k1):
                got = rcv1.at[u, lax.rem(m1 + k1 - o, k1)]
                remote(got, got, *sems(base[1] + o - 1), d1(o)).wait_recv()
                own = own + got[...].astype(F32)
            acc2[u] = own.astype(BF16)
            for o in range(1, k2):
                piece = acc2.at[u, pl.ds(pl.multiple_of(lax.rem(m2 + o, k2) * r2, 16), r2)]
                send(piece, rcv2.at[u, m2], *sems(base[2] + o - 1), d2(o))
        elif s == 3:
            own = acc2[u, pl.ds(pl.multiple_of(m2 * r2, 16), r2), :].astype(F32)
            for o in range(1, k2):
                got = rcv2.at[u, lax.rem(m2 + k2 - o, k2)]
                remote(got, got, *sems(base[2] + o - 1), d2(o)).wait_recv()
                own = own + got[...].astype(F32)
            acc3[u] = own.astype(BF16)
            for o in range(1, k3):
                lanes = pl.ds(pl.multiple_of(lax.rem(m3 + o, k3) * w3, WIDE), w3)
                send(
                    acc3.at[u, :, lanes], rcv3.at[u, m3], *sems(base[3] + o - 1), d3(o)
                )
        elif s == 4:
            own = acc3[u, :, pl.ds(pl.multiple_of(m3 * w3, WIDE), w3)].astype(F32)
            for o in range(1, k3):
                got = rcv3.at[u, lax.rem(m3 + k3 - o, k3)]
                remote(got, got, *sems(base[3] + o - 1), d3(o)).wait_recv()
                own = own + got[...].astype(F32)
            spot = out_rows(u, core, m1 * r1 + m2 * r2, r2).at[
                :, pl.ds(pl.multiple_of(m3 * w3, WIDE), w3)
            ]
            acc4[u] = own.astype(BF16)
            pltpu.make_async_copy(acc4.at[u], spot, csem.at[u]).start()
            for o in range(1, k3):
                send(acc4.at[u], spot, *sems(width + base[3] + o - 1), d3(o))
        elif s == 5:
            for o in range(1, k3):
                lanes = pl.ds(pl.multiple_of(lax.rem(m3 + k3 - o, k3) * w3, WIDE), w3)
                got = out_rows(u, core, m1 * r1 + m2 * r2, r2).at[:, lanes]
                remote(got, got, *sems(width + base[3] + o - 1), d3(o)).wait_recv()
            spot = out_rows(u, core, m1 * r1 + m2 * r2, r2)
            mine = spot.at[:, pl.ds(pl.multiple_of(m3 * w3, WIDE), w3)]
            pltpu.make_async_copy(acc4.at[u], mine, csem.at[u]).wait()
            for o in range(1, k2):
                send(spot, spot, *sems(width + base[2] + o - 1), d2(o))
        elif s == 6:
            for o in range(1, k2):
                got = out_rows(u, core, m1 * r1 + lax.rem(m2 + k2 - o, k2) * r2, r2)
                remote(got, got, *sems(width + base[2] + o - 1), d2(o)).wait_recv()
            spot = out_rows(u, core, m1 * r1, r1)
            for o in range(1, k1):
                send(spot, spot, *sems(width + base[1] + o - 1), d1(o))
        elif s == 7:
            for o in range(1, k1):
                got = out_rows(u, core, lax.rem(m1 + k1 - o, k1) * r1, r1)
                remote(got, got, *sems(width + base[1] + o - 1), d1(o)).wait_recv()
            spot = out_rows(u, core, 0, half)
            send(spot, spot, *sems(width), on_core())
        else:
            got = out_rows(u, 1 - core, 0, half)
            remote(got, got, *sems(width), on_core()).wait_recv()

    progress = {}

    def advance(units=None):
        for u in list(progress) if units is None else units:
            if u in progress:
                reduce_step(u, progress[u])
                progress[u] += 1
                if progress[u] > 8:
                    del progress[u]

    def gather_step(n, s):
        sems = lambda slot: (gs_sem.at[n, slot], gr_sem.at[n, slot])
        if s == 0:
            own = gat_ref.at[n, bo, bi]
            for o in range(1, inner):
                send(own, own, *sems(o - 1), on_inner(o))
        elif s == 1:
            for o in range(1, inner):
                got = gat_ref.at[n, bo, lax.rem(bi + inner - o, inner)]
                remote(got, got, *sems(o - 1), on_inner(o)).wait_recv()
            own = gat_ref.at[n, bo]
            for o in range(1, OUTER):
                send(own, own, *sems(inner - 1 + o - 1), on_outer(o))
        else:
            for o in range(1, OUTER):
                got = gat_ref.at[n, lax.rem(bo + OUTER - o, OUTER)]
                remote(got, got, *sems(inner - 1 + o - 1), on_outer(o)).wait_recv()

    def backward_conv(n):
        st[...] = jnp.zeros_like(st)
        coef[0:32, 0 : 2 * C] = split3(jnp.concatenate([sv[n, 0], sv[n, 1]], axis=1))

        @pl.loop(0, T // R)
        def _(i):
            r0 = pl.multiple_of(i * R, R)
            rows = pl.ds(r0, R)
            prev, following, mid = shifted(r0)
            mid = mid.astype(BF16)
            x3[rows, 0:C] = following
            x3[rows, C : 2 * C] = mid
            x3[rows, 2 * C : 3 * C] = prev
            da = (
                dot_back(following, cw[n, 0:C, :])
                + dot_back(mid, cw[n, C : 2 * C, :])
                + dot_back(prev, cw[n, 2 * C : 3 * C, :])
            )
            spread_out = dot(mem[rows, :], coef[:, 0 : 2 * C])
            d = value(n, rows)
            h = spread_out[:, 0:C] * d + spread_out[:, C : 2 * C]
            th = jnp.tanh(h)
            dy = da * ((0.5 + 0.5 * th) * (1.0 + h - h * th))
            dyb[rows, :] = dy
            add_stats(rows, dy, dy * d)

    def backward_send(n):
        scale, mean = sv[n, 2], sv[n, 3]
        s1, s2 = st[0:8, 0:C], st[0:8, C : 2 * C]
        bx[n, time, 0:4, :] = (scale * (s2 - mean * s1))[0:4]
        bx[n, time, 4:8, :] = s1[0:4]
        bx[n, time, 8:9, :] = dyb[0:1, :]
        bx[n, time, 9:10, :] = dyb[T - 1 : T, :]
        bx[n, time, 10:11, :] = brow[0:1, :]
        bx[n, time, 11:16, :] = jnp.zeros((5, C), F32)
        exchange(bx.at[n], 4 + n, n % 2 == 1)

    def weight_grad(n):
        for side in range(2):
            lane = (core if side else 1 - core) * half
            left = asave[n, :, pl.ds(pl.multiple_of(lane, half), half)]
            for k in range(3):
                u = 3 * n + k
                g = dot_rows(left, x3[:, k * C : (k + 1) * C]).astype(BF16)
                if side:
                    wkeep[u] = g
                else:
                    wsnd[u] = g
                    progress[u] = 0
                    advance([u])

    def backward_norm(n):
        exchanged(bx.at[n], 4 + n, n % 2 == 1)
        zero4 = jnp.zeros((4, C), F32)
        dgain, dshift = jnp.zeros((4, C), F32), jnp.zeros((4, C), F32)
        bias_row = jnp.zeros((1, C), F32)
        for j in range(members):
            dgain = dgain + bx[n, j, 0:4, :]
            dshift = dshift + bx[n, j, 4:8, :]
            if n % 2 == 1:
                bias_row = bias_row + bx[n, j, 10:11, :]
        dmod = jnp.concatenate([dgain, dshift], axis=1)
        quarter = C // 2
        packet = [dmod[:, q * quarter : (q + 1) * quarter] for q in range(4)]
        packet += [bias_row[:, 0:quarter], bias_row[:, quarter:C]]
        packet += [
            jnp.concatenate([style_ref[0:1, :], style_ref[1:2, :]], axis=1),
            jnp.concatenate([style_ref[2:3, :], style_ref[3:4, :]], axis=1),
            jnp.zeros((12, quarter), F32),
        ]
        gat_ref[n, bo, bi] = jnp.concatenate(packet, axis=0).astype(BF16)
        gather_step(n, 0)
        dmod8 = jnp.concatenate([dmod, jnp.zeros((4, 2 * C), F32)], axis=0)
        part = dot_back(dmod8, fcw[n], highest)[0:UTT]
        if n == 3:
            styleg_ref[...] = part
        else:
            styleg_ref[...] += part
        scale, mean, gain = sv[n, 2], sv[n, 3], sv[n, 4]
        mean_dn = gain * jnp.concatenate([dshift, zero4], axis=0) * inv_totals
        mean_x = gain * jnp.concatenate([dgain, zero4], axis=0) * inv_totals
        alpha = scale * gain
        kappa = -(scale * scale) * mean_x
        delta = -scale * mean_dn - kappa * mean
        coef[0:32, 0 : 3 * C] = split3(jnp.concatenate([alpha, kappa, delta], axis=1))
        p = piv[8 * n : 8 * n + 1, :]

        def edge(dy, raw, own, cot_edge):
            out = (
                pick_row(alpha, own) * dy
                + pick_row(kappa, own) * (raw - p)
                + pick_row(delta, own)
            )
            if n == 2:
                out = (out + cot_edge * root_half) * root_half
            return out

        if n > 0:
            sh[7:8, :] = edge(
                bx[n, before_me, 9:10, :],
                fx[n, before_me, 9:10, :],
                first_own,
                fx[0, before_me, 11:12, :],
            )
            sh[T + 8 : T + 9, :] = edge(
                bx[n, after_me, 8:9, :],
                fx[n, after_me, 8:9, :],
                last_own,
                fx[0, after_me, 10:11, :],
            )
        if n == 2:
            brow[...] = jnp.zeros_like(brow)

        @pl.loop(0, T // R)
        def _(i):
            r0 = pl.multiple_of(i * R, R)
            rows = pl.ds(r0, R)
            spread_out = dot(mem[rows, :], coef[...])
            dv = (
                spread_out[:, 0:C] * dyb[rows, :]
                + spread_out[:, C : 2 * C] * value(n, rows)
                + spread_out[:, 2 * C : 3 * C]
            )
            mid = pl.ds(pl.multiple_of(r0 + 8, 8), R)
            if n % 2 == 1:
                sh[mid, :] = dv
            elif n == 2:
                carried = (dv + cot[rows, :].astype(F32) * root_half) * root_half
                vs[2, rows, :] = carried
                sh[mid, :] = carried
                brow[0:1, :] += jnp.sum(carried, axis=0, keepdims=True)
            else:
                phon[rows, :] = (dv + vs[2, rows, :]).astype(BF16)

    brow[...] = jnp.zeros_like(brow)

    @pl.loop(0, T // R)
    def _(i):
        r0 = pl.multiple_of(i * R, R)
        g = cot[pl.ds(r0, R), :].astype(F32) * root_half
        sh[pl.ds(pl.multiple_of(r0 + 8, 8), R), :] = g
        brow[0:1, :] += jnp.sum(g, axis=0, keepdims=True)

    sh[7:8, :] = fx[0, before_me, 11:12, :] * root_half
    sh[T + 8 : T + 9, :] = fx[0, after_me, 10:11, :] * root_half

    for n in (3, 2, 1, 0):
        backward_conv(n)
        backward_send(n)
        advance()
        weight_grad(n)
        backward_norm(n)
        advance()
        gather_step(n, 1)

    ph = PH // 2
    psnd, pkeep = x3.at[pl.ds(0, ph), 0:C], x3.at[pl.ds(0, ph), C : 2 * C]
    prcv1 = [asave.at[o, pl.ds(0, ph)] for o in range(1, yn)]
    psems = lambda slot: (ps_sem.at[slot], pr_sem.at[slot])
    for side in range(2):
        lane = pl.multiple_of((core if side else 1 - core) * ph, WIDE)
        step = 256

        @pl.loop(0, ph // step)
        def _(i):
            at = pl.multiple_of(i * step, step)
            lanes = pl.ds(pl.multiple_of(lane + at, WIDE), step)
            g = dot_rows(pick[:, lanes], phon[pl.ds(0, T), :])
            (pkeep if side else psnd)[pl.ds(at, step), :] = g.astype(BF16)

        if side == 0:
            send(psnd, prcv0, *psems(0), on_core())
    advance()
    remote(psnd, prcv0, *psems(0), on_core()).wait_recv()
    pkeep[...] = (pkeep[...].astype(F32) + prcv0[...].astype(F32)).astype(BF16)
    for o in range(1, yn):
        send(pkeep, prcv1[o - 1], *psems(o), on_y(o))
    advance()
    advance()
    spot = pg_ref.at[pl.ds(pl.multiple_of(core * ph, WIDE), ph)]
    whole = pkeep[...].astype(F32)
    for o in range(1, yn):
        remote(pkeep, prcv1[o - 1], *psems(o), on_y(o)).wait_recv()
        whole = whole + prcv1[o - 1][...].astype(F32)
    spot[...] = whole.astype(BF16)
    send(spot, spot, *psems(yn), on_core())
    while progress:
        advance()
    got = pg_ref.at[pl.ds(pl.multiple_of((1 - core) * ph, WIDE), ph)]
    remote(got, got, *psems(yn), on_core()).wait_recv()
    for n in range(4):
        gather_step(n, 2)
    drain()


def dot_general_exact(left, right):
    return jnp.dot(left, right, precision=highest, preferred_element_type=F32)


def on_device(
    n_batch,
    members,
    phonemes,
    durations,
    utt_frames,
    style_codes,
    fc_weight,
    fc_bias,
    conv_weight,
    conv_bias,
    cotangent,
):
    T, C = cotangent.shape
    PH = phonemes.shape[0]
    inner = n_batch // OUTER
    yn = members // CORES
    half = C // 2
    VM, ANY = pltpu.VMEM, pl.ANY
    vspec = pl.BlockSpec(memory_space=pltpu.VMEM)
    aspec = pl.BlockSpec(memory_space=pl.ANY)
    r1 = half // min(yn, inner)
    r2 = half // yn // inner
    most = max(yn, inner)
    nslots = 2 * (yn + inner + OUTER - 2)
    DMA = pltpu.SemaphoreType.DMA
    scratch = [
        VM((PH, C), BF16),
        VM(fc_weight.shape, F32),
        VM(conv_weight.shape, BF16),
        VM((T, C), BF16),
        VM((T, PH), BF16),
        VM((T, WIDE), BF16),
        VM((16, T), BF16),
        VM((T, WIDE), F32),
        VM((T, WIDE), F32),
        VM((T, C), BF16),
        VM((3, T, C), F32),
        VM((32, C), F32),
        VM((4, T, C), BF16),
        VM((T + 16, C), F32),
        VM((T, 3 * C), BF16),
        VM((T, C), F32),
        VM((4, 8, 2 * C), F32),
        VM((4, 5, 8, C), F32),
        VM((WIDE, 3 * C), BF16),
        VM((16, 2 * C), F32),
        VM((8, C), F32),
        VM((4, members, 16, C), F32),
        VM((4, members, 16, C), F32),
        VM((PH // 2, C), BF16),
        VM((12, half, C), BF16),
        VM((12, half, C), BF16),
        VM((12, half, C), BF16),
        VM((12, most, r1, C), BF16),
        VM((12, r1, C), BF16),
        VM((12, most, r2, C), BF16),
        VM((12, r2, C), BF16),
        VM((12, OUTER, r2, C // OUTER), BF16),
        VM((12, r2, C // OUTER), BF16),
        DMA((7,)),
        DMA((12,)),
        DMA((8, members)),
        DMA((8, members)),
        DMA((4, inner + OUTER)),
        DMA((4, inner + OUTER)),
        DMA((yn + 1,)),
        DMA((yn + 1,)),
        DMA((12, nslots)),
        DMA((12, nslots)),
    ]
    frames_out, pgrad, style_part, gathered, wgrad = pl.pallas_call(
        functools.partial(kernel, inner, members),
        out_shape=(
            jax.ShapeDtypeStruct((T, C), BF16),
            jax.ShapeDtypeStruct((PH, C), BF16),
            jax.ShapeDtypeStruct(style_codes.shape, F32),
            jax.ShapeDtypeStruct((4, OUTER, inner, 32, C // 2), BF16),
            jax.ShapeDtypeStruct(conv_weight.shape, BF16),
        ),
        in_specs=[
            aspec,
            vspec,
            pl.BlockSpec(memory_space=pltpu.SMEM),
            vspec,
            aspec,
            vspec,
            aspec,
            vspec,
            aspec,
        ],
        out_specs=[vspec, vspec, vspec, vspec, aspec],
        scratch_shapes=scratch,
        compiler_params=pltpu.CompilerParams(
            collective_id=0, has_side_effects=True, vmem_limit_bytes=63 * 1024 * 1024
        ),
    )(
        phonemes,
        durations,
        utt_frames,
        style_codes,
        fc_weight,
        fc_bias,
        conv_weight,
        conv_bias,
        cotangent,
    )
    gathered = gathered.reshape(4, n_batch, 32, C // 2).astype(F32)
    dmods = (
        gathered[:, :, 0:16].reshape(4, n_batch, 4, UTT, C // 2).transpose(0, 1, 3, 2, 4)
    ).reshape(4, n_batch * UTT, 2 * C)
    styles = gathered[0, :, 18:20].reshape(n_batch * UTT, -1)
    fc_grad = jnp.einsum("us,num->nsm", styles, dmods, precision=highest)
    fcb_grad = jnp.sum(dmods, axis=1)
    bias_grad = jnp.stack(
        [jnp.sum(gathered[n, :, 16:18].reshape(n_batch, C), axis=0) for n in (1, 3)], 0
    )
    return (
        frames_out,
        pgrad.astype(F32),
        style_part,
        fc_grad,
        fcb_grad,
        wgrad.astype(F32),
        bias_grad,
    )


def solution(mesh):
    return jax.shard_map(
        functools.partial(on_device, mesh.shape["batch"], mesh.shape["tm"]),
        mesh=mesh,
        in_specs=(
            P("batch", None),
            P("batch", None),
            P("batch", None),
            P("batch", None),
            P(),
            P(),
            P(),
            P(),
            P(("batch", "tm"), None),
        ),
        out_specs=(
            P(("batch", "tm"), None),
            P("batch", None),
            P("batch", None),
            P(),
            P(),
            P(),
            P(),
        ),
        check_vma=False,
    )
```

```python
import functools
import jax
import jax.numpy as jnp
from jax import lax
from jax.experimental import pallas as pl
from jax.experimental.pallas import tpu as pltpu
from jax.sharding import PartitionSpec as P

F32, BF16 = jnp.float32, jnp.bfloat16
MESH = pl.DeviceIdType.MESH
highest = lax.Precision.HIGHEST
norm_eps = 1e-05
root_half = 0.7071067811865476
UTT = 4
CORES = 2
OUTER = 4
WIDE = 128
SLOTS = ""
FREE = "BE"
ORDERS = ["xyz", "yxz"] * 6


def dot(left, right):
    return jnp.dot(left, right, preferred_element_type=F32)


def dot_rows(left, right):
    return lax.dot_general(left, right, (((0,), (0,)), ((), ())), preferred_element_type=F32)


def dot_back(left, right, precision=None):
    return lax.dot_general(
        left, right, (((1,), (1,)), ((), ())), precision=precision, preferred_element_type=F32
    )


def split3(values):
    high = values.astype(BF16).astype(F32)
    rest = values - high
    mid = rest.astype(BF16).astype(F32)
    return jnp.concatenate([high, mid, rest - mid, jnp.zeros_like(values)], axis=0).astype(BF16)


def kernel(
    inner,
    members,
    phon_hbm,
    dur_ref,
    utt_ref,
    style_ref,
    fcw_hbm,
    fcb_ref,
    cw_hbm,
    cb_ref,
    cot_hbm,
    frames_ref,
    pg_ref,
    styleg_ref,
    gat_ref,
    wg_ref,
    phon,
    fcw,
    cw,
    cot,
    pick,
    mem,
    memt,
    amask,
    bmask,
    x0,
    vs,
    piv,
    asave,
    sh,
    x3,
    dyb,
    mod,
    sv,
    coef,
    st,
    brow,
    fx,
    bx,
    prcv0,
    wsnd,
    wkeep,
    wrcv0,
    rcv1,
    acc2,
    rcv2,
    acc3,
    rcv3,
    acc4,
    lsem,
    csem,
    xs_sem,
    xr_sem,
    gs_sem,
    gr_sem,
    ps_sem,
    pr_sem,
    ws_sem,
    wr_sem,
):
    T, C = cot_hbm.shape
    PH = phon_hbm.shape[0]
    yn = members // CORES
    batch = lax.axis_index("batch")
    time = lax.axis_index("tm")
    bo, bi = batch // inner, batch % inner
    ty, core = time // CORES, time % CORES
    R = 512
    t0 = time * T

    loads = [
        pltpu.make_async_copy(phon_hbm, phon, lsem.at[0]),
        pltpu.make_async_copy(fcw_hbm, fcw, lsem.at[1]),
        pltpu.make_async_copy(cot_hbm, cot, lsem.at[2]),
    ] + [pltpu.make_async_copy(cw_hbm.at[n], cw.at[n], lsem.at[3 + n]) for n in range(4)]
    for load in loads:
        load.start()

    def on_tm(o):
        return (batch, lax.rem(time + o, members))

    def on_core():
        return (batch, ty * CORES + (1 - core))

    def on_y(o):
        return (batch, lax.rem(ty + o, yn) * CORES + core)

    def on_inner(o):
        return (bo * inner + lax.rem(bi + o, inner), time)

    def on_outer(o):
        return (lax.rem(bo + o, OUTER) * inner + bi, time)

    partners = (
        [on_tm(o) for o in range(1, members)]
        + [on_inner(o) for o in range(1, inner)]
        + [on_outer(o) for o in range(1, OUTER)]
    )
    barrier = pltpu.get_barrier_semaphore()
    for partner in partners:
        pl.semaphore_signal(barrier, inc=1, device_id=partner, device_id_type=MESH)

    def remote(src, dst, ssem, rsem, device):
        return pltpu.make_async_remote_copy(
            src_ref=src,
            dst_ref=dst,
            send_sem=ssem,
            recv_sem=rsem,
            device_id=device,
            device_id_type=MESH,
        )

    unsent = []

    def send(src, dst, ssem, rsem, device):
        copy = remote(src, dst, ssem, rsem, device)
        copy.start()
        unsent.append(copy)

    def drain():
        for copy in unsent:
            copy.wait_send()
        unsent.clear()

    lens = [utt_ref[0, u] for u in range(UTT)]
    starts, ends, total = [], [], 0
    for u in range(UTT):
        starts.append(total)
        total = total + lens[u]
        ends.append(total)
    row8 = lax.broadcasted_iota(jnp.int32, (8, C), 0)

    def by_utt(values, other):
        out = jnp.full((8, C), other, F32)
        for u in range(UTT):
            out = jnp.where(row8 == u, values[u], out)
        return out

    def local_counts(j):
        return by_utt(
            [
                jnp.maximum(jnp.minimum(ends[u], (j + 1) * T) - jnp.maximum(starts[u], j * T), 0)
                .astype(F32)
                for u in range(UTT)
            ],
            0.0,
        )

    totals = by_utt([n.astype(F32) for n in lens], 1.0)
    inv_totals = 1.0 / totals
    mine = local_counts(time)
    inv_mine = 1.0 / jnp.maximum(mine, 1.0)

    def owner_rows(t):
        return [
            jnp.logical_and(t >= starts[u], t < ends[u]).astype(F32) for u in range(UTT)
        ]

    first_own, last_own = owner_rows(t0), owner_rows(t0 + T - 1)

    def pick_row(values, own):
        out = own[0] * values[0:1]
        for u in range(1, UTT):
            out = out + own[u] * values[u : u + 1]
        return out

    coef[...] = jnp.zeros_like(coef)

    @pl.loop(0, T // WIDE)
    def _(i):
        r0 = pl.multiple_of(i * WIDE, WIDE)
        t = lax.broadcasted_iota(jnp.int32, (WIDE, WIDE), 0) + r0 + t0
        lane = lax.broadcasted_iota(jnp.int32, (WIDE, WIDE), 1)
        before, after = t >= 1, t >= 0
        own = jnp.zeros((WIDE, WIDE), F32)
        slot = lax.rem(lane, 8)
        for u in range(UTT):
            before = jnp.logical_and(before, t != starts[u])
            after = jnp.logical_and(after, t + 1 != ends[u])
            inside = jnp.logical_and(t >= starts[u], t < ends[u])
            own = jnp.where(jnp.logical_and(inside, slot == u), 1.0, own)
        own = jnp.where(lane < 24, own, 0.0)
        mem[pl.ds(r0, WIDE), :] = own.astype(BF16)
        bmask[pl.ds(r0, WIDE), :] = before.astype(F32)
        amask[pl.ds(r0, WIDE), :] = after.astype(F32)
        tt = lax.broadcasted_iota(jnp.int32, (16, WIDE), 1) + r0 + t0
        row = lax.broadcasted_iota(jnp.int32, (16, WIDE), 0)
        ownt = jnp.zeros((16, WIDE), F32)
        for u in range(UTT):
            inside = jnp.logical_and(tt >= starts[u], tt < ends[u])
            ownt = jnp.where(jnp.logical_and(inside, row == u), 1.0, ownt)
        memt[:, pl.ds(r0, WIDE)] = ownt.astype(BF16)

    tiles = PH // WIDE
    durs = jnp.concatenate(
        [dur_ref[0:1, j * WIDE : (j + 1) * WIDE] for j in range(tiles)], axis=0
    ).astype(F32)
    upper = (
        lax.broadcasted_iota(jnp.int32, (WIDE, WIDE), 0)
        <= lax.broadcasted_iota(jnp.int32, (WIDE, WIDE), 1)
    ).astype(BF16)
    within = dot(durs.astype(BF16), upper)
    so_far = jnp.zeros((1, 1), F32)
    for j in range(tiles):
        stop = within[j : j + 1] + so_far
        begin = (stop - durs[j : j + 1]).astype(jnp.int32)
        stop = stop.astype(jnp.int32)
        so_far = so_far + within[j : j + 1, WIDE - 1 : WIDE]
        t = lax.broadcasted_iota(jnp.int32, (T, WIDE), 0) + t0
        inside = jnp.logical_and(t >= begin, t < stop)
        pick[:, j * WIDE : (j + 1) * WIDE] = jnp.where(inside, 1.0, 0.0).astype(BF16)

    loads[0].wait()

    @pl.loop(0, T // R)
    def _(i):
        r0 = pl.multiple_of(i * R, R)
        x0[pl.ds(r0, R), :] = dot(pick[pl.ds(r0, R), :], phon[...]).astype(BF16)

    def value(n, rows):
        if n == 0:
            return x0[rows, :].astype(F32) - piv[0:1, :]
        return vs[n - 1, rows, :]

    def add_stats(rows, one, two):
        both = jnp.concatenate([one.astype(BF16), two.astype(BF16)], axis=1)
        st[...] += dot(memt[:, rows], both)

    st[...] = jnp.zeros_like(st)
    piv[0:8, :] = jnp.broadcast_to(x0[0:16, :].astype(F32)[0:1], (8, C))

    @pl.loop(0, T // R)
    def _(i):
        rows = pl.ds(pl.multiple_of(i * R, R), R)
        d = value(0, rows)
        add_stats(rows, d, d * d)

    loads[1].wait()
    style8 = jnp.concatenate(
        [style_ref[...], jnp.zeros((8 - UTT, style_ref.shape[1]), F32)], axis=0
    )
    for n in range(4):
        mod[n] = dot_general_exact(style8, fcw[n]) + fcb_ref[n : n + 1, :]

    loads[2].wait()
    cot_first = cot[0:16, :].astype(F32)[0:1]
    cot_last = cot[T - 16 : T, :].astype(F32)[15:16]

    pl.semaphore_wait(barrier, len(partners))

    def exchange(buf, phase, full):
        for o in range(1, members):
            rows = 16 if full or o in (1, members - 1) else 8
            send(
                buf.at[time, pl.ds(0, rows)],
                buf.at[time, pl.ds(0, rows)],
                xs_sem.at[phase, o],
                xr_sem.at[phase, o],
                on_tm(o),
            )

    def exchanged(buf, phase, full):
        for o in range(1, members):
            rows = 16 if full or o in (1, members - 1) else 8
            ref = buf.at[lax.rem(time + members - o, members), pl.ds(0, rows)]
            remote(ref, ref, xs_sem.at[phase, o], xr_sem.at[phase, o], on_tm(o)).wait_recv()

    before_me, after_me = lax.rem(time + members - 1, members), lax.rem(time + 1, members)

    def forward_send(n, first, last):
        p = piv[8 * n : 8 * n + 1, :]
        s1, s2 = st[0:8, 0:C], st[0:8, C : 2 * C]
        local = s1 * inv_mine
        fx[n, time, 0:4, :] = (local + p)[0:4]
        fx[n, time, 4:8, :] = (s2 - s1 * local)[0:4]
        fx[n, time, 8:9, :] = first + p
        fx[n, time, 9:10, :] = last + p
        fx[n, time, 10:11, :] = cot_first
        fx[n, time, 11:12, :] = cot_last
        fx[n, time, 12:16, :] = jnp.zeros((4, C), F32)
        exchange(fx.at[n], n, False)

    def forward_norm(n):
        exchanged(fx.at[n], n, False)
        p = piv[8 * n : 8 * n + 1, :]
        zero4 = jnp.zeros((4, C), F32)
        counts = [local_counts(j) for j in range(members)]
        means = [
            jnp.concatenate([fx[n, j, 0:4, :], zero4], axis=0) for j in range(members)
        ]
        mean = counts[0] * means[0]
        for j in range(1, members):
            mean = mean + counts[j] * means[j]
        mean = mean * inv_totals
        spread = jnp.zeros((8, C), F32)
        for j in range(members):
            off = means[j] - mean
            spread = spread + counts[j] * off * off + jnp.concatenate(
                [fx[n, j, 4:8, :], zero4], axis=0
            )
        scale = lax.rsqrt(jnp.maximum(spread * inv_totals, 0.0) + norm_eps)
        gain, shift = 1.0 + mod[n, :, 0:C], mod[n, :, C : 2 * C]
        slope = gain * scale
        mean = mean - p
        half_a, half_b = 0.5 * slope, 0.5 * (shift - slope * mean)
        sv[n, 0] = half_a
        sv[n, 1] = half_b
        sv[n, 2] = scale
        sv[n, 3] = mean
        sv[n, 4] = gain
        coef[0:32, 0 : 2 * C] = split3(jnp.concatenate([half_a, half_b], axis=1))

        def edge(raw, own):
            h = pick_row(half_a, own) * (raw - p) + pick_row(half_b, own)
            return h + h * jnp.tanh(h)

        sh[7:8, :] = edge(fx[n, before_me, 9:10, :], first_own)
        sh[T + 8 : T + 9, :] = edge(fx[n, after_me, 8:9, :], last_own)

        @pl.loop(0, T // R)
        def _(i):
            r0 = pl.multiple_of(i * R, R)
            rows = pl.ds(r0, R)
            spread_out = dot(mem[rows, :], coef[:, 0 : 2 * C])
            h = spread_out[:, 0:C] * value(n, rows) + spread_out[:, C : 2 * C]
            a = h + h * jnp.tanh(h)
            sh[pl.ds(pl.multiple_of(r0 + 8, 8), R), :] = a
            asave[n, rows, :] = a.astype(BF16)

    def shifted(r0):
        window = sh[pl.ds(r0, R + 16), :]
        rows = pl.ds(r0, R)
        bm = jnp.concatenate([bmask[rows, :]] * (C // WIDE), axis=1)
        am = jnp.concatenate([amask[rows, :]] * (C // WIDE), axis=1)
        return (
            (window[7 : 7 + R] * bm).astype(BF16),
            (window[9 : 9 + R] * am).astype(BF16),
            window[8 : 8 + R],
        )

    def forward_conv(n):
        if n < 3:
            loads[3 + n].wait()
        st[...] = jnp.zeros_like(st)

        @pl.loop(0, T // R)
        def _(i):
            r0 = pl.multiple_of(i * R, R)
            rows = pl.ds(r0, R)
            prev, following, _ = shifted(r0)
            c = dot(jnp.concatenate([prev, asave[n, rows, :], following], axis=1), cw[n])
            if n % 2 == 1:
                b = n // 2
                kept = x0[rows, :].astype(F32) if n == 1 else vs[1, rows, :] + piv[16:17, :]
                c = (c + cb_ref[b : b + 1, :] + kept) * root_half
            if n == 3:
                frames_ref[rows, :] = c.astype(BF16)
                return

            @pl.when(i == 0)
            def _():
                m = jnp.mean(c, axis=0, keepdims=True)
                piv[8 * (n + 1) : 8 * (n + 2), :] = jnp.broadcast_to(m, (8, C))

            d = c - piv[8 * (n + 1) : 8 * (n + 1) + 1, :]
            vs[n, rows, :] = d
            add_stats(rows, d, d * d)

    def shift_rows(i):
        r0 = pl.multiple_of(i * R, R)
        rows = pl.ds(r0, R)
        prev, following, mid = shifted(r0)
        x3[rows, 0:C] = following
        x3[rows, C : 2 * C] = mid.astype(BF16)
        x3[rows, 2 * C : 3 * C] = prev

    def cotangent_rows():
        brow[...] = jnp.zeros_like(brow)

        @pl.loop(0, T // R)
        def _(i):
            r0 = pl.multiple_of(i * R, R)
            g = cot[pl.ds(r0, R), :].astype(F32) * root_half
            sh[pl.ds(pl.multiple_of(r0 + 8, 8), R), :] = g
            brow[0:1, :] += jnp.sum(g, axis=0, keepdims=True)

        sh[7:8, :] = fx[0, before_me, 11:12, :] * root_half
        sh[T + 8 : T + 9, :] = fx[0, after_me, 10:11, :] * root_half
        pl.loop(0, T // R)(shift_rows)

    first16 = x0[0:16, :].astype(F32)
    last16 = x0[T - 16 : T, :].astype(F32)
    p0 = piv[0:1, :]
    forward_send(0, first16[0:1] - p0, last16[15:16] - p0)
    for n in range(3):
        forward_norm(n)
        forward_conv(n)
        forward_send(n + 1, vs[n, 0:1, :], vs[n, T - 1 : T, :])
        if n == 0:
            cotangent_rows()
    forward_norm(3)
    loads[6].wait()

    axes = {
        "y": (yn, ty, on_y),
        "x": (inner, bi, on_inner),
        "z": (OUTER, bo, on_outer),
    }
    half = C // 2

    def order_of(u):
        return ORDERS[u]

    def plan(u):
        return tuple(axes[name] for name in order_of(u))

    def out_rows(u, side, start, count):
        n, k = u // 3, u % 3
        base = k * C + side * half + start
        return wg_ref.at[n, pl.ds(pl.multiple_of(base, 16), count)]

    def slots(u):
        (k1, _, _), (k2, _, _), (k3, _, _) = plan(u)
        base = [0, 1, k1, k1 + k2 - 1]
        width = k1 + k2 + k3 - 2
        return base, width

    def reduce_step(u, s):
        (k1, m1, d1), (k2, m2, d2), (k3, m3, d3) = plan(u)
        base, width = slots(u)
        r1, r2, w3 = half // k1, half // k1 // k2, C // k3
        sems = lambda slot: (ws_sem.at[u, slot], wr_sem.at[u, slot])
        if s == 0:
            send(wsnd.at[u], wrcv0.at[u], *sems(0), on_core())
        elif s == 1:
            remote(wsnd.at[u], wrcv0.at[u], *sems(0), on_core()).wait_recv()
            wkeep[u] = (wkeep[u].astype(F32) + wrcv0[u].astype(F32)).astype(BF16)
            for o in range(1, k1):
                piece = wkeep.at[u, pl.ds(pl.multiple_of(lax.rem(m1 + o, k1) * r1, 16), r1)]
                send(piece, rcv1.at[u, o - 1], *sems(base[1] + o - 1), d1(o))
        elif s == 2:
            own = wkeep[u, pl.ds(pl.multiple_of(m1 * r1, 16), r1), :].astype(F32)
            for o in range(1, k1):
                got = rcv1.at[u, o - 1]
                remote(got, got, *sems(base[1] + o - 1), d1(o)).wait_recv()
                own = own + got[...].astype(F32)
            acc2[u] = own.astype(BF16)
            for o in range(1, k2):
                piece = acc2.at[u, pl.ds(pl.multiple_of(lax.rem(m2 + o, k2) * r2, 16), r2)]
                send(piece, rcv2.at[u, o - 1], *sems(base[2] + o - 1), d2(o))
        elif s == 3:
            own = acc2[u, pl.ds(pl.multiple_of(m2 * r2, 16), r2), :].astype(F32)
            for o in range(1, k2):
                got = rcv2.at[u, o - 1]
                remote(got, got, *sems(base[2] + o - 1), d2(o)).wait_recv()
                own = own + got[...].astype(F32)
            acc3[u] = own.astype(BF16)
            for o in range(1, k3):
                lanes = pl.ds(pl.multiple_of(lax.rem(m3 + o, k3) * w3, WIDE), w3)
                send(
                    acc3.at[u, :, lanes], rcv3.at[u, o - 1], *sems(base[3] + o - 1), d3(o)
                )
        elif s == 4:
            own = acc3[u, :, pl.ds(pl.multiple_of(m3 * w3, WIDE), w3)].astype(F32)
            for o in range(1, k3):
                got = rcv3.at[u, o - 1]
                remote(got, got, *sems(base[3] + o - 1), d3(o)).wait_recv()
                own = own + got[...].astype(F32)
            spot = out_rows(u, core, m1 * r1 + m2 * r2, r2).at[
                :, pl.ds(pl.multiple_of(m3 * w3, WIDE), w3)
            ]
            acc4[u] = own.astype(BF16)
            pltpu.make_async_copy(acc4.at[u], spot, csem.at[u]).start()
            for o in range(1, k3):
                send(acc4.at[u], spot, *sems(width + base[3] + o - 1), d3(o))
        elif s == 5:
            for o in range(1, k3):
                lanes = pl.ds(pl.multiple_of(lax.rem(m3 + k3 - o, k3) * w3, WIDE), w3)
                got = out_rows(u, core, m1 * r1 + m2 * r2, r2).at[:, lanes]
                remote(got, got, *sems(width + base[3] + o - 1), d3(o)).wait_recv()
            spot = out_rows(u, core, m1 * r1 + m2 * r2, r2)
            mine = spot.at[:, pl.ds(pl.multiple_of(m3 * w3, WIDE), w3)]
            pltpu.make_async_copy(acc4.at[u], mine, csem.at[u]).wait()
            for o in range(1, k2):
                send(spot, spot, *sems(width + base[2] + o - 1), d2(o))
        elif s == 6:
            for o in range(1, k2):
                got = out_rows(u, core, m1 * r1 + lax.rem(m2 + k2 - o, k2) * r2, r2)
                remote(got, got, *sems(width + base[2] + o - 1), d2(o)).wait_recv()
            spot = out_rows(u, core, m1 * r1, r1)
            for o in range(1, k1):
                send(spot, spot, *sems(width + base[1] + o - 1), d1(o))
        elif s == 7:
            for o in range(1, k1):
                got = out_rows(u, core, lax.rem(m1 + k1 - o, k1) * r1, r1)
                remote(got, got, *sems(width + base[1] + o - 1), d1(o)).wait_recv()
            spot = out_rows(u, core, 0, half)
            send(spot, spot, *sems(width), on_core())
        else:
            got = out_rows(u, 1 - core, 0, half)
            remote(got, got, *sems(width), on_core()).wait_recv()

    progress = {}

    def link(u):
        first = order_of(u)
        return ("c" + first + first[::-1] + "c ")[progress[u]]

    def advance(units=None, links="xyzc "):
        for u in list(progress) if units is None else units:
            if u in progress and link(u) in links:
                reduce_step(u, progress[u])
                progress[u] += 1
                if progress[u] > 8:
                    del progress[u]

    def slot(name):
        if name in FREE:
            advance()
        elif name in SLOTS:
            advance(links="xzc ")

    def gather_step(n, s):
        sems = lambda slot: (gs_sem.at[n, slot], gr_sem.at[n, slot])
        if s == 0:
            own = gat_ref.at[n, bo, bi]
            for o in range(1, inner):
                send(own, own, *sems(o - 1), on_inner(o))
        elif s == 1:
            for o in range(1, inner):
                got = gat_ref.at[n, bo, lax.rem(bi + inner - o, inner)]
                remote(got, got, *sems(o - 1), on_inner(o)).wait_recv()
            own = gat_ref.at[n, bo]
            for o in range(1, OUTER):
                send(own, own, *sems(inner - 1 + o - 1), on_outer(o))
        else:
            for o in range(1, OUTER):
                got = gat_ref.at[n, lax.rem(bo + OUTER - o, OUTER)]
                remote(got, got, *sems(inner - 1 + o - 1), on_outer(o)).wait_recv()

    def backward_conv(n):
        st[...] = jnp.zeros_like(st)
        coef[0:32, 0 : 2 * C] = split3(jnp.concatenate([sv[n, 0], sv[n, 1]], axis=1))

        @pl.loop(0, T // R)
        def _(i):
            r0 = pl.multiple_of(i * R, R)
            rows = pl.ds(r0, R)
            if n < 3:
                shift_rows(i)
            da = (
                dot_back(x3[rows, 0:C], cw[n, 0:C, :])
                + dot_back(x3[rows, C : 2 * C], cw[n, C : 2 * C, :])
                + dot_back(x3[rows, 2 * C : 3 * C], cw[n, 2 * C : 3 * C, :])
            )
            spread_out = dot(mem[rows, :], coef[:, 0 : 2 * C])
            d = value(n, rows)
            h = spread_out[:, 0:C] * d + spread_out[:, C : 2 * C]
            th = jnp.tanh(h)
            dy = da * ((0.5 + 0.5 * th) * (1.0 + h - h * th))
            dyb[rows, :] = dy
            add_stats(rows, dy, dy * d)

    def backward_send(n):
        scale, mean = sv[n, 2], sv[n, 3]
        s1, s2 = st[0:8, 0:C], st[0:8, C : 2 * C]
        bx[n, time, 0:4, :] = (scale * (s2 - mean * s1))[0:4]
        bx[n, time, 4:8, :] = s1[0:4]
        bx[n, time, 8:9, :] = dyb[0:1, :]
        bx[n, time, 9:10, :] = dyb[T - 1 : T, :]
        bx[n, time, 10:11, :] = brow[0:1, :]
        bx[n, time, 11:16, :] = jnp.zeros((5, C), F32)
        exchange(bx.at[n], 4 + n, n % 2 == 1)

    def weight_grad(n):
        for side in range(2):
            lane = (core if side else 1 - core) * half
            left = asave[n, :, pl.ds(pl.multiple_of(lane, half), half)]
            for k in range(3):
                u = 3 * n + k
                g = dot_rows(left, x3[:, k * C : (k + 1) * C]).astype(BF16)
                if side:
                    wkeep[u] = g
                else:
                    wsnd[u] = g
                    progress[u] = 0
                    advance([u])

    def backward_norm(n):
        exchanged(bx.at[n], 4 + n, n % 2 == 1)
        slot("D")
        zero4 = jnp.zeros((4, C), F32)
        dgain, dshift = jnp.zeros((4, C), F32), jnp.zeros((4, C), F32)
        bias_row = jnp.zeros((1, C), F32)
        for j in range(members):
            dgain = dgain + bx[n, j, 0:4, :]
            dshift = dshift + bx[n, j, 4:8, :]
            if n % 2 == 1:
                bias_row = bias_row + bx[n, j, 10:11, :]
        dmod = jnp.concatenate([dgain, dshift], axis=1)
        quarter = C // 2
        packet = [dmod[:, q * quarter : (q + 1) * quarter] for q in range(4)]
        packet += [bias_row[:, 0:quarter], bias_row[:, quarter:C]]
        packet += [
            jnp.concatenate([style_ref[0:1, :], style_ref[1:2, :]], axis=1),
            jnp.concatenate([style_ref[2:3, :], style_ref[3:4, :]], axis=1),
            jnp.zeros((12, quarter), F32),
        ]
        gat_ref[n, bo, bi] = jnp.concatenate(packet, axis=0).astype(BF16)
        gather_step(n, 0)
        dmod8 = jnp.concatenate([dmod, jnp.zeros((4, 2 * C), F32)], axis=0)
        part = dot_back(dmod8, fcw[n], highest)[0:UTT]
        if n == 3:
            styleg_ref[...] = part
        else:
            styleg_ref[...] += part
        scale, mean, gain = sv[n, 2], sv[n, 3], sv[n, 4]
        mean_dn = gain * jnp.concatenate([dshift, zero4], axis=0) * inv_totals
        mean_x = gain * jnp.concatenate([dgain, zero4], axis=0) * inv_totals
        alpha = scale * gain
        kappa = -(scale * scale) * mean_x
        delta = -scale * mean_dn - kappa * mean
        coef[0:32, 0 : 3 * C] = split3(jnp.concatenate([alpha, kappa, delta], axis=1))
        p = piv[8 * n : 8 * n + 1, :]

        def edge(dy, raw, own, cot_edge):
            out = (
                pick_row(alpha, own) * dy
                + pick_row(kappa, own) * (raw - p)
                + pick_row(delta, own)
            )
            if n == 2:
                out = (out + cot_edge * root_half) * root_half
            return out

        if n > 0:
            sh[7:8, :] = edge(
                bx[n, before_me, 9:10, :],
                fx[n, before_me, 9:10, :],
                first_own,
                fx[0, before_me, 11:12, :],
            )
            sh[T + 8 : T + 9, :] = edge(
                bx[n, after_me, 8:9, :],
                fx[n, after_me, 8:9, :],
                last_own,
                fx[0, after_me, 10:11, :],
            )
        if n == 2:
            brow[...] = jnp.zeros_like(brow)

        @pl.loop(0, T // R)
        def _(i):
            r0 = pl.multiple_of(i * R, R)
            rows = pl.ds(r0, R)
            spread_out = dot(mem[rows, :], coef[...])
            dv = (
                spread_out[:, 0:C] * dyb[rows, :]
                + spread_out[:, C : 2 * C] * value(n, rows)
                + spread_out[:, 2 * C : 3 * C]
            )
            mid = pl.ds(pl.multiple_of(r0 + 8, 8), R)
            if n % 2 == 1:
                sh[mid, :] = dv
            elif n == 2:
                carried = (dv + cot[rows, :].astype(F32) * root_half) * root_half
                vs[2, rows, :] = carried
                sh[mid, :] = carried
                brow[0:1, :] += jnp.sum(carried, axis=0, keepdims=True)
            else:
                phon[rows, :] = (dv + vs[2, rows, :]).astype(BF16)

    for n in (3, 2, 1, 0):
        if n == 3:
            weight_grad(n)
        backward_conv(n)
        slot("A")
        backward_send(n)
        slot("B")
        if n == 3:
            forward_conv(n)
        else:
            weight_grad(n)
        slot("C")
        backward_norm(n)
        slot("E")
        if n < 3:
            gather_step(n + 1, 1)

    ph = PH // 2
    psnd, pkeep = x3.at[pl.ds(0, ph), 0:C], x3.at[pl.ds(0, ph), C : 2 * C]
    prcv1 = [asave.at[o, pl.ds(0, ph)] for o in range(1, yn)]
    psems = lambda slot: (ps_sem.at[slot], pr_sem.at[slot])
    for side in range(2):
        lane = pl.multiple_of((core if side else 1 - core) * ph, WIDE)
        step = 256

        @pl.loop(0, ph // step)
        def _(i):
            at = pl.multiple_of(i * step, step)
            lanes = pl.ds(pl.multiple_of(lane + at, WIDE), step)
            g = dot_rows(pick[:, lanes], phon[pl.ds(0, T), :])
            (pkeep if side else psnd)[pl.ds(at, step), :] = g.astype(BF16)

        if side == 0:
            send(psnd, prcv0, *psems(0), on_core())
    advance()
    remote(psnd, prcv0, *psems(0), on_core()).wait_recv()
    pkeep[...] = (pkeep[...].astype(F32) + prcv0[...].astype(F32)).astype(BF16)
    for o in range(1, yn):
        send(pkeep, prcv1[o - 1], *psems(o), on_y(o))
    advance()
    advance()
    spot = pg_ref.at[pl.ds(pl.multiple_of(core * ph, WIDE), ph)]
    whole = pkeep[...].astype(F32)
    for o in range(1, yn):
        remote(pkeep, prcv1[o - 1], *psems(o), on_y(o)).wait_recv()
        whole = whole + prcv1[o - 1][...].astype(F32)
    spot[...] = whole.astype(BF16)
    send(spot, spot, *psems(yn), on_core())
    gather_step(0, 1)
    while progress:
        advance()
    got = pg_ref.at[pl.ds(pl.multiple_of((1 - core) * ph, WIDE), ph)]
    remote(got, got, *psems(yn), on_core()).wait_recv()
    for n in range(4):
        gather_step(n, 2)
    drain()


def dot_general_exact(left, right):
    return jnp.dot(left, right, precision=highest, preferred_element_type=F32)


def finish(
    frames_in,
    pg_in,
    style_in,
    gat_in,
    wg_in,
    frames_out,
    pg_out,
    style_out,
    fcg_out,
    fcb_out,
    wg_out,
    bias_out,
    whigh,
    phigh,
    fcg,
    dm,
    styles,
    rsem,
    wsem,
):
    C = frames_in.shape[1]
    half = C // 2
    n_batch = gat_in.shape[1]
    units = [(n, k) for n in range(4) for k in range(3)]
    whole = pltpu.make_async_copy(frames_in, frames_out, rsem.at[0])
    stores = [
        pltpu.make_async_copy(whigh.at[u], wg_out.at[n, pl.ds(k * C, C)], wsem.at[u])
        for u, (n, k) in enumerate(units)
    ]
    pstore = pltpu.make_async_copy(phigh, pg_out, wsem.at[12])
    fstore = pltpu.make_async_copy(fcg, fcg_out, wsem.at[13])
    for u in range(12):
        n, k = units[u]
        whigh[u] = wg_in[n, k * C : (k + 1) * C, :].astype(F32)
        stores[u].start()
    phigh[...] = pg_in[...].astype(F32)
    pstore.start()
    whole.start()
    style_out[...] = style_in[...]
    bias = [jnp.zeros((1, C), F32), jnp.zeros((1, C), F32)]
    for b in range(n_batch):
        pack = gat_in[0, b].astype(F32)
        for side in range(2):
            styles[b * UTT + 2 * side : b * UTT + 2 * side + 1, :] = pack[18 + side : 19 + side, 0:half // 2]
            styles[b * UTT + 2 * side + 1 : b * UTT + 2 * side + 2, :] = pack[18 + side : 19 + side, half // 2 : half]
    for n in range(4):
        for b in range(n_batch):
            pack = gat_in[n, b].astype(F32)
            dm[b * UTT : (b + 1) * UTT, :] = jnp.concatenate(
                [pack[q * UTT : (q + 1) * UTT] for q in range(4)], axis=1
            )
            if n % 2 == 1:
                bias[n // 2] = bias[n // 2] + jnp.concatenate(
                    [pack[16:17], pack[17:18]], axis=1
                )
        fcg[n] = dot_rows(styles[...].astype(BF16), dm[...].astype(BF16))
        fcb_out[n : n + 1, :] = jnp.sum(dm[...], axis=0, keepdims=True)
    bias_out[...] = jnp.concatenate(bias, axis=0)
    fstore.start()
    whole.wait()
    for store in stores + [pstore, fstore]:
        store.wait()


def on_device(
    n_batch,
    members,
    phonemes,
    durations,
    utt_frames,
    style_codes,
    fc_weight,
    fc_bias,
    conv_weight,
    conv_bias,
    cotangent,
):
    T, C = cotangent.shape
    PH = phonemes.shape[0]
    inner = n_batch // OUTER
    yn = members // CORES
    half = C // 2
    VM, ANY = pltpu.VMEM, pl.ANY
    vspec = pl.BlockSpec(memory_space=pltpu.VMEM)
    aspec = pl.BlockSpec(memory_space=pl.ANY)
    r1 = half // min(yn, inner)
    r2 = half // yn // inner
    most = max(yn, inner)
    nslots = 2 * (yn + inner + OUTER - 2)
    DMA = pltpu.SemaphoreType.DMA
    roomy = PH <= 1024 and members <= 4
    held = VM if roomy else jax.ShapeDtypeStruct
    scratch = [
        VM((PH, C), BF16),
        VM(fc_weight.shape, F32),
        VM(conv_weight.shape, BF16),
        VM((T, C), BF16),
        VM((T, PH), BF16),
        VM((T, WIDE), BF16),
        VM((16, T), BF16),
        VM((T, WIDE), F32),
        VM((T, WIDE), F32),
        VM((T, C), BF16),
        VM((3, T, C), F32),
        VM((32, C), F32),
        VM((4, T, C), BF16),
        VM((T + 16, C), F32),
        VM((T, 3 * C), BF16),
        VM((T, C), F32),
        VM((4, 8, 2 * C), F32),
        VM((4, 5, 8, C), F32),
        VM((WIDE, 3 * C), BF16),
        VM((16, 2 * C), F32),
        VM((8, C), F32),
        VM((4, members, 16, C), F32),
        VM((4, members, 16, C), F32),
        VM((PH // 2, C), BF16),
        VM((12, half, C), BF16),
        VM((12, half, C), BF16),
        VM((12, half, C), BF16),
        VM((12, most - 1, r1, C), BF16),
        VM((12, r1, C), BF16),
        VM((12, most - 1, r2, C), BF16),
        VM((12, r2, C), BF16),
        VM((12, OUTER - 1, r2, C // OUTER), BF16),
        VM((12, r2, C // OUTER), BF16),
        DMA((7,)),
        DMA((12,)),
        DMA((8, members)),
        DMA((8, members)),
        DMA((4, inner + OUTER)),
        DMA((4, inner + OUTER)),
        DMA((yn + 1,)),
        DMA((yn + 1,)),
        DMA((12, nslots)),
        DMA((12, nslots)),
    ]
    frames_out, pgrad, style_part, gathered, wgrad = pl.pallas_call(
        functools.partial(kernel, inner, members),
        out_shape=(
            held((T, C), BF16),
            held((PH, C), BF16),
            held(style_codes.shape, F32),
            held((4, OUTER, inner, 32, C // 2), BF16),
            held(conv_weight.shape, BF16),
        ),
        in_specs=[
            aspec,
            vspec,
            pl.BlockSpec(memory_space=pltpu.SMEM),
            vspec,
            aspec,
            vspec,
            aspec,
            vspec,
            aspec,
        ],
        out_specs=[vspec, vspec, vspec, vspec, vspec if roomy else aspec],
        scratch_shapes=scratch,
        compiler_params=pltpu.CompilerParams(
            collective_id=0, has_side_effects=True, vmem_limit_bytes=(54 if roomy else 63) * 1024 * 1024
        ),
    )(
        phonemes,
        durations,
        utt_frames,
        style_codes,
        fc_weight,
        fc_bias,
        conv_weight,
        conv_bias,
        cotangent,
    )
    utts = n_batch * UTT
    return pl.pallas_call(
        finish,
        out_shape=(
            jax.ShapeDtypeStruct((T, C), BF16),
            jax.ShapeDtypeStruct((PH, C), F32),
            jax.ShapeDtypeStruct(style_codes.shape, F32),
            jax.ShapeDtypeStruct(fc_weight.shape, F32),
            jax.ShapeDtypeStruct(fc_bias.shape, F32),
            jax.ShapeDtypeStruct(conv_weight.shape, F32),
            jax.ShapeDtypeStruct(conv_bias.shape, F32),
        ),
        in_specs=[vspec] * 5,
        out_specs=[aspec, aspec, vspec, aspec, vspec, aspec, vspec],
        scratch_shapes=[
            VM((12, C, C), F32),
            VM((PH, C), F32),
            VM(fc_weight.shape, F32),
            VM((utts, 2 * C), F32),
            VM((utts, style_codes.shape[1]), F32),
            DMA((1,)),
            DMA((14,)),
        ],
        compiler_params=pltpu.CompilerParams(vmem_limit_bytes=32 * 1024 * 1024),
    )(frames_out, pgrad, style_part, gathered.reshape(4, n_batch, 32, C // 2), wgrad)


def solution(mesh):
    return jax.shard_map(
        functools.partial(on_device, mesh.shape["batch"], mesh.shape["tm"]),
        mesh=mesh,
        in_specs=(
            P("batch", None),
            P("batch", None),
            P("batch", None),
            P("batch", None),
            P(),
            P(),
            P(),
            P(),
            P(("batch", "tm"), None),
        ),
        out_specs=(
            P(("batch", "tm"), None),
            P("batch", None),
            P("batch", None),
            P(),
            P(),
            P(),
            P(),
        ),
        check_vma=False,
    )
```

```python
import functools
import jax
import jax.numpy as jnp
from jax import lax
from jax.experimental import pallas as pl
from jax.experimental.pallas import tpu as pltpu
from jax.sharding import PartitionSpec as P

F32, BF16 = jnp.float32, jnp.bfloat16
MESH = pl.DeviceIdType.MESH
highest = lax.Precision.HIGHEST
norm_eps = 1e-05
root_half = 0.7071067811865476
UTT = 4
CORES = 2
OUTER = 4
WIDE = 128
ORDERS = ["xyz", "yxz", "yxz", "xyz", "xzy", "yxz", "xzy", "xzy", "yxz", "xzy", "xyz", "xzy"]
SCHEDULE = [
    [9, 10, 11],
    [],
    [],
    [9],
    [],
    [],
    [10],
    [],
    [],
    [11],
    [9],
    [10],
    [9],
    [],
    [6, 7, 8, 11, 10, 9],
    [],
    [],
    [],
    [],
    [6, 8, 10],
    [7, 11, 9],
    [],
    [3, 4, 5, 8, 11, 10],
    [6],
    [9],
    [7, 9],
    [],
    [3, 5, 8, 6],
    [4, 7, 11],
    [3, 6],
    [0, 1, 2, 5, 8, 7, 10],
    [],
    [11],
    [4, 10, 11],
    [3],
    [0],
    [1],
    [2, 0, 1, 2, 5, 4, 3, 8, 6, 7, 0, 1, 2, 5, 0, 4, -1, 1, 2, 3, 5, 6, 7, 8, 1, 0, 2, 4, 5, 3, 6, 7, 8, 5, 1, 0, 3, 1, 2, 4, 0, 2, 4],
]


def dot(left, right):
    return jnp.dot(left, right, preferred_element_type=F32)


def dot_rows(left, right):
    return lax.dot_general(left, right, (((0,), (0,)), ((), ())), preferred_element_type=F32)


def dot_back(left, right, precision=None):
    return lax.dot_general(
        left, right, (((1,), (1,)), ((), ())), precision=precision, preferred_element_type=F32
    )


def split3(values):
    high = values.astype(BF16).astype(F32)
    rest = values - high
    mid = rest.astype(BF16).astype(F32)
    return jnp.concatenate([high, mid, rest - mid, jnp.zeros_like(values)], axis=0).astype(BF16)


def kernel(
    inner,
    members,
    phon_hbm,
    dur_ref,
    utt_ref,
    style_ref,
    fcw_hbm,
    fcb_ref,
    cw_hbm,
    cb_ref,
    cot_hbm,
    frames_ref,
    pg_ref,
    styleg_ref,
    gat_ref,
    wg_ref,
    phon,
    fcw,
    cw,
    cot,
    pick,
    mem,
    memt,
    amask,
    bmask,
    x0,
    vs,
    piv,
    asave,
    sh,
    x3,
    dyb,
    mod,
    sv,
    coef,
    st,
    brow,
    fx,
    bx,
    prcv0,
    wsnd,
    wkeep,
    wrcv0,
    rcv1,
    acc2,
    rcv2,
    acc3,
    rcv3z,
    rcv3o,
    acc4z,
    acc4o,
    lsem,
    csem,
    xs_sem,
    xr_sem,
    gs_sem,
    gr_sem,
    ps_sem,
    pr_sem,
    ws_sem,
    wr_sem,
):
    T, C = cot_hbm.shape
    PH = phon_hbm.shape[0]
    yn = members // CORES
    batch = lax.axis_index("batch")
    time = lax.axis_index("tm")
    bo, bi = batch // inner, batch % inner
    ty, core = time // CORES, time % CORES
    R = 512
    t0 = time * T

    def at(i):
        return i * R if isinstance(i, int) else pl.multiple_of(i * R, R)

    loads = [
        pltpu.make_async_copy(phon_hbm, phon, lsem.at[0]),
        pltpu.make_async_copy(fcw_hbm, fcw, lsem.at[1]),
        pltpu.make_async_copy(cot_hbm, cot, lsem.at[2]),
    ] + [pltpu.make_async_copy(cw_hbm.at[n], cw.at[n], lsem.at[3 + n]) for n in range(4)]
    for load in loads:
        load.start()

    def on_tm(o):
        return (batch, lax.rem(time + o, members))

    def on_core():
        return (batch, ty * CORES + (1 - core))

    def on_y(o):
        return (batch, lax.rem(ty + o, yn) * CORES + core)

    def on_inner(o):
        return (bo * inner + lax.rem(bi + o, inner), time)

    def on_outer(o):
        return (lax.rem(bo + o, OUTER) * inner + bi, time)

    partners = (
        [on_tm(o) for o in range(1, members)]
        + [on_inner(o) for o in range(1, inner)]
        + [on_outer(o) for o in range(1, OUTER)]
    )
    barrier = pltpu.get_barrier_semaphore()
    for partner in partners:
        pl.semaphore_signal(barrier, inc=1, device_id=partner, device_id_type=MESH)

    def remote(src, dst, ssem, rsem, device):
        return pltpu.make_async_remote_copy(
            src_ref=src,
            dst_ref=dst,
            send_sem=ssem,
            recv_sem=rsem,
            device_id=device,
            device_id_type=MESH,
        )

    unsent = []

    def send(src, dst, ssem, rsem, device):
        copy = remote(src, dst, ssem, rsem, device)
        copy.start()
        unsent.append(copy)

    def drain():
        for copy in unsent:
            copy.wait_send()
        unsent.clear()

    lens = [utt_ref[0, u] for u in range(UTT)]
    starts, ends, total = [], [], 0
    for u in range(UTT):
        starts.append(total)
        total = total + lens[u]
        ends.append(total)
    row8 = lax.broadcasted_iota(jnp.int32, (8, C), 0)

    def by_utt(values, other):
        out = jnp.full((8, C), other, F32)
        for u in range(UTT):
            out = jnp.where(row8 == u, values[u], out)
        return out

    def local_counts(j):
        return by_utt(
            [
                jnp.maximum(jnp.minimum(ends[u], (j + 1) * T) - jnp.maximum(starts[u], j * T), 0)
                .astype(F32)
                for u in range(UTT)
            ],
            0.0,
        )

    totals = by_utt([n.astype(F32) for n in lens], 1.0)
    inv_totals = 1.0 / totals
    mine = local_counts(time)
    inv_mine = 1.0 / jnp.maximum(mine, 1.0)

    def owner_rows(t):
        return [
            jnp.logical_and(t >= starts[u], t < ends[u]).astype(F32) for u in range(UTT)
        ]

    first_own, last_own = owner_rows(t0), owner_rows(t0 + T - 1)

    def pick_row(values, own):
        out = own[0] * values[0:1]
        for u in range(1, UTT):
            out = out + own[u] * values[u : u + 1]
        return out

    coef[...] = jnp.zeros_like(coef)

    @pl.loop(0, T // WIDE)
    def _(i):
        r0 = pl.multiple_of(i * WIDE, WIDE)
        t = lax.broadcasted_iota(jnp.int32, (WIDE, WIDE), 0) + r0 + t0
        lane = lax.broadcasted_iota(jnp.int32, (WIDE, WIDE), 1)
        before, after = t >= 1, t >= 0
        own = jnp.zeros((WIDE, WIDE), F32)
        slot = lax.rem(lane, 8)
        for u in range(UTT):
            before = jnp.logical_and(before, t != starts[u])
            after = jnp.logical_and(after, t + 1 != ends[u])
            inside = jnp.logical_and(t >= starts[u], t < ends[u])
            own = jnp.where(jnp.logical_and(inside, slot == u), 1.0, own)
        own = jnp.where(lane < 24, own, 0.0)
        mem[pl.ds(r0, WIDE), :] = own.astype(BF16)
        bmask[pl.ds(r0, WIDE), :] = before.astype(F32)
        amask[pl.ds(r0, WIDE), :] = after.astype(F32)
        tt = lax.broadcasted_iota(jnp.int32, (16, WIDE), 1) + r0 + t0
        row = lax.broadcasted_iota(jnp.int32, (16, WIDE), 0)
        ownt = jnp.zeros((16, WIDE), F32)
        for u in range(UTT):
            inside = jnp.logical_and(tt >= starts[u], tt < ends[u])
            ownt = jnp.where(jnp.logical_and(inside, row == u), 1.0, ownt)
        memt[:, pl.ds(r0, WIDE)] = ownt.astype(BF16)

    tiles = PH // WIDE
    durs = jnp.concatenate(
        [dur_ref[0:1, j * WIDE : (j + 1) * WIDE] for j in range(tiles)], axis=0
    ).astype(F32)
    upper = (
        lax.broadcasted_iota(jnp.int32, (WIDE, WIDE), 0)
        <= lax.broadcasted_iota(jnp.int32, (WIDE, WIDE), 1)
    ).astype(BF16)
    within = dot(durs.astype(BF16), upper)
    so_far = jnp.zeros((1, 1), F32)
    for j in range(tiles):
        stop = within[j : j + 1] + so_far
        begin = (stop - durs[j : j + 1]).astype(jnp.int32)
        stop = stop.astype(jnp.int32)
        so_far = so_far + within[j : j + 1, WIDE - 1 : WIDE]
        t = lax.broadcasted_iota(jnp.int32, (T, WIDE), 0) + t0
        inside = jnp.logical_and(t >= begin, t < stop)
        pick[:, j * WIDE : (j + 1) * WIDE] = jnp.where(inside, 1.0, 0.0).astype(BF16)

    loads[0].wait()

    @pl.loop(0, T // R)
    def _(i):
        r0 = pl.multiple_of(i * R, R)
        x0[pl.ds(r0, R), :] = dot(pick[pl.ds(r0, R), :], phon[...]).astype(BF16)

    def value(n, rows):
        if n == 0:
            return x0[rows, :].astype(F32) - piv[0:1, :]
        return vs[n - 1, rows, :]

    def add_stats(rows, one, two):
        both = jnp.concatenate([one.astype(BF16), two.astype(BF16)], axis=1)
        st[...] += dot(memt[:, rows], both)

    st[...] = jnp.zeros_like(st)
    piv[0:8, :] = jnp.broadcast_to(x0[0:16, :].astype(F32)[0:1], (8, C))

    @pl.loop(0, T // R)
    def _(i):
        rows = pl.ds(pl.multiple_of(i * R, R), R)
        d = value(0, rows)
        add_stats(rows, d, d * d)

    loads[1].wait()
    style8 = jnp.concatenate(
        [style_ref[...], jnp.zeros((8 - UTT, style_ref.shape[1]), F32)], axis=0
    )
    for n in range(4):
        mod[n] = dot_general_exact(style8, fcw[n]) + fcb_ref[n : n + 1, :]

    loads[2].wait()
    cot_first = cot[0:16, :].astype(F32)[0:1]
    cot_last = cot[T - 16 : T, :].astype(F32)[15:16]

    pl.semaphore_wait(barrier, len(partners))

    def exchange(buf, phase, full):
        for o in range(1, members):
            rows = 16 if full or o in (1, members - 1) else 8
            send(
                buf.at[time, pl.ds(0, rows)],
                buf.at[time, pl.ds(0, rows)],
                xs_sem.at[phase, o],
                xr_sem.at[phase, o],
                on_tm(o),
            )

    def exchanged(buf, phase, full):
        for o in range(1, members):
            rows = 16 if full or o in (1, members - 1) else 8
            ref = buf.at[lax.rem(time + members - o, members), pl.ds(0, rows)]
            remote(ref, ref, xs_sem.at[phase, o], xr_sem.at[phase, o], on_tm(o)).wait_recv()

    before_me, after_me = lax.rem(time + members - 1, members), lax.rem(time + 1, members)

    def forward_send(n, first, last):
        p = piv[8 * n : 8 * n + 1, :]
        s1, s2 = st[0:8, 0:C], st[0:8, C : 2 * C]
        local = s1 * inv_mine
        fx[n, time, 0:4, :] = (local + p)[0:4]
        fx[n, time, 4:8, :] = (s2 - s1 * local)[0:4]
        fx[n, time, 8:9, :] = first + p
        fx[n, time, 9:10, :] = last + p
        fx[n, time, 10:11, :] = cot_first
        fx[n, time, 11:12, :] = cot_last
        fx[n, time, 12:16, :] = jnp.zeros((4, C), F32)
        exchange(fx.at[n], n, False)

    def forward_norm(n):
        exchanged(fx.at[n], n, False)
        p = piv[8 * n : 8 * n + 1, :]
        zero4 = jnp.zeros((4, C), F32)
        counts = [local_counts(j) for j in range(members)]
        means = [
            jnp.concatenate([fx[n, j, 0:4, :], zero4], axis=0) for j in range(members)
        ]
        mean = counts[0] * means[0]
        for j in range(1, members):
            mean = mean + counts[j] * means[j]
        mean = mean * inv_totals
        spread = jnp.zeros((8, C), F32)
        for j in range(members):
            off = means[j] - mean
            spread = spread + counts[j] * off * off + jnp.concatenate(
                [fx[n, j, 4:8, :], zero4], axis=0
            )
        scale = lax.rsqrt(jnp.maximum(spread * inv_totals, 0.0) + norm_eps)
        gain, shift = 1.0 + mod[n, :, 0:C], mod[n, :, C : 2 * C]
        slope = gain * scale
        mean = mean - p
        half_a, half_b = 0.5 * slope, 0.5 * (shift - slope * mean)
        sv[n, 0] = half_a
        sv[n, 1] = half_b
        sv[n, 2] = scale
        sv[n, 3] = mean
        sv[n, 4] = gain
        coef[0:32, 0 : 2 * C] = split3(jnp.concatenate([half_a, half_b], axis=1))

        def edge(raw, own):
            h = pick_row(half_a, own) * (raw - p) + pick_row(half_b, own)
            return h + h * jnp.tanh(h)

        sh[7:8, :] = edge(fx[n, before_me, 9:10, :], first_own)
        sh[T + 8 : T + 9, :] = edge(fx[n, after_me, 8:9, :], last_own)

        @pl.loop(0, T // R)
        def _(i):
            r0 = pl.multiple_of(i * R, R)
            rows = pl.ds(r0, R)
            spread_out = dot(mem[rows, :], coef[:, 0 : 2 * C])
            h = spread_out[:, 0:C] * value(n, rows) + spread_out[:, C : 2 * C]
            a = h + h * jnp.tanh(h)
            sh[pl.ds(pl.multiple_of(r0 + 8, 8), R), :] = a
            asave[n, rows, :] = a.astype(BF16)

    def shifted(r0):
        window = sh[pl.ds(r0, R + 16), :]
        rows = pl.ds(r0, R)
        bm = jnp.concatenate([bmask[rows, :]] * (C // WIDE), axis=1)
        am = jnp.concatenate([amask[rows, :]] * (C // WIDE), axis=1)
        return (
            (window[7 : 7 + R] * bm).astype(BF16),
            (window[9 : 9 + R] * am).astype(BF16),
            window[8 : 8 + R],
        )

    def forward_conv(n):
        st[...] = jnp.zeros_like(st)

        def chunk(i):
            r0 = at(i)
            rows = pl.ds(r0, R)
            prev, following, _ = shifted(r0)
            c = dot(jnp.concatenate([prev, asave[n, rows, :], following], axis=1), cw[n])
            if n % 2 == 1:
                b = n // 2
                kept = x0[rows, :].astype(F32) if n == 1 else vs[1, rows, :] + piv[16:17, :]
                c = (c + cb_ref[b : b + 1, :] + kept) * root_half
            if n == 3:
                frames_ref[rows, :] = c.astype(BF16)
                return

            @pl.when(i == 0)
            def _():
                m = jnp.mean(c, axis=0, keepdims=True)
                piv[8 * (n + 1) : 8 * (n + 2), :] = jnp.broadcast_to(m, (8, C))

            d = c - piv[8 * (n + 1) : 8 * (n + 1) + 1, :]
            vs[n, rows, :] = d
            add_stats(rows, d, d * d)

        if n < 3:
            loads[3 + n].wait()
            pl.loop(0, T // R)(chunk)
        else:
            for i in range(T // R):
                slot()
                chunk(i)

    def shift_rows(i):
        r0 = at(i)
        rows = pl.ds(r0, R)
        prev, following, mid = shifted(r0)
        x3[rows, 0:C] = following
        x3[rows, C : 2 * C] = mid.astype(BF16)
        x3[rows, 2 * C : 3 * C] = prev

    def cotangent_rows():
        brow[...] = jnp.zeros_like(brow)

        @pl.loop(0, T // R)
        def _(i):
            r0 = pl.multiple_of(i * R, R)
            g = cot[pl.ds(r0, R), :].astype(F32) * root_half
            sh[pl.ds(pl.multiple_of(r0 + 8, 8), R), :] = g
            brow[0:1, :] += jnp.sum(g, axis=0, keepdims=True)

        sh[7:8, :] = fx[0, before_me, 11:12, :] * root_half
        sh[T + 8 : T + 9, :] = fx[0, after_me, 10:11, :] * root_half
        pl.loop(0, T // R)(shift_rows)

    first16 = x0[0:16, :].astype(F32)
    last16 = x0[T - 16 : T, :].astype(F32)
    p0 = piv[0:1, :]
    forward_send(0, first16[0:1] - p0, last16[15:16] - p0)
    for n in range(3):
        forward_norm(n)
        forward_conv(n)
        forward_send(n + 1, vs[n, 0:1, :], vs[n, T - 1 : T, :])
        if n == 0:
            cotangent_rows()
    forward_norm(3)
    loads[6].wait()

    axes = {
        "y": (yn, ty, on_y),
        "x": (inner, bi, on_inner),
        "z": (OUTER, bo, on_outer),
    }
    half = C // 2

    def plan(u):
        return tuple(axes[name] for name in ORDERS[u])

    def out_rows(u, side, start, count):
        n, k = u // 3, u % 3
        base = k * C + side * half + start
        return wg_ref.at[n, pl.ds(pl.multiple_of(base, 16), count)]

    def slots(u):
        (k1, _, _), (k2, _, _), (k3, _, _) = plan(u)
        base = [0, 1, k1, k1 + k2 - 1]
        width = k1 + k2 + k3 - 2
        return base, width

    def reduce_step(u, s):
        (k1, m1, d1), (k2, m2, d2), (k3, m3, d3) = plan(u)
        base, width = slots(u)
        r1, r2, w3 = half // k1, half // k1 // k2, C // k3
        rcv3, acc4 = (rcv3z, acc4z) if ORDERS[u][2] == "z" else (rcv3o, acc4o)
        sems = lambda slot: (ws_sem.at[u, slot], wr_sem.at[u, slot])

        def band(ref, index, count):
            return ref.at[u, pl.ds(pl.multiple_of(index * count, 16), count)]

        def lanes(index):
            return pl.ds(pl.multiple_of(index * w3, WIDE), w3)

        def other(m, k, o):
            return lax.rem(m + o, k)

        def sums(own, k, first, landed, device):
            for o in range(1, k):
                remote(landed(o), landed(o), *sems(first + o - 1), device(o)).wait_recv()
                own = own + landed(o)[...].astype(F32)
            return own.astype(BF16)

        land1 = lambda o: rcv1.at[u, o - 1]
        land2 = lambda o: band(rcv2, o - 1, r2)
        land3 = lambda o: band(rcv3, o - 1, r2)
        row0 = m1 * r1 + m2 * r2
        if s == 0:
            send(wsnd.at[u], wrcv0.at[u], *sems(0), on_core())
        elif s == 1:
            remote(wsnd.at[u], wrcv0.at[u], *sems(0), on_core()).wait_recv()
            wkeep[u] = (wkeep[u].astype(F32) + wrcv0[u].astype(F32)).astype(BF16)
            for o in range(1, k1):
                send(band(wkeep, other(m1, k1, o), r1), land1(o), *sems(base[1] + o - 1), d1(o))
        elif s == 2:
            own = band(wkeep, m1, r1)[...].astype(F32)
            acc2[u] = sums(own, k1, base[1], land1, d1)
            for o in range(1, k2):
                send(band(acc2, other(m2, k2, o), r2), land2(o), *sems(base[2] + o - 1), d2(o))
        elif s == 3:
            own = band(acc2, m2, r2)[...].astype(F32)
            acc3[u, 0:r2] = sums(own, k2, base[2], land2, d2)
            for o in range(1, k3):
                piece = acc3.at[u, pl.ds(0, r2), lanes(other(m3, k3, o))]
                send(piece, land3(o), *sems(base[3] + o - 1), d3(o))
        elif s == 4:
            own = acc3[u, pl.ds(0, r2), lanes(m3)].astype(F32)
            acc4[u] = sums(own, k3, base[3], land3, d3)
            spot = out_rows(u, core, row0, r2).at[:, lanes(m3)]
            pltpu.make_async_copy(acc4.at[u], spot, csem.at[u]).start()
            for o in range(1, k3):
                send(acc4.at[u], spot, *sems(width + base[3] + o - 1), d3(o))
        elif s == 5:
            spot = out_rows(u, core, row0, r2)
            for o in range(1, k3):
                got = spot.at[:, lanes(other(m3, k3, k3 - o))]
                remote(got, got, *sems(width + base[3] + o - 1), d3(o)).wait_recv()
            pltpu.make_async_copy(acc4.at[u], spot.at[:, lanes(m3)], csem.at[u]).wait()
            for o in range(1, k2):
                send(spot, spot, *sems(width + base[2] + o - 1), d2(o))
        elif s == 6:
            for o in range(1, k2):
                got = out_rows(u, core, m1 * r1 + other(m2, k2, k2 - o) * r2, r2)
                remote(got, got, *sems(width + base[2] + o - 1), d2(o)).wait_recv()
            spot = out_rows(u, core, m1 * r1, r1)
            for o in range(1, k1):
                send(spot, spot, *sems(width + base[1] + o - 1), d1(o))
        elif s == 7:
            for o in range(1, k1):
                got = out_rows(u, core, other(m1, k1, k1 - o) * r1, r1)
                remote(got, got, *sems(width + base[1] + o - 1), d1(o)).wait_recv()
            spot = out_rows(u, core, 0, half)
            send(spot, spot, *sems(width), on_core())
        else:
            got = out_rows(u, 1 - core, 0, half)
            remote(got, got, *sems(width), on_core()).wait_recv()

    progress = {}

    def step(u):
        reduce_step(u, progress[u])
        progress[u] += 1

    schedule = iter(SCHEDULE)

    def slot():
        for u in next(schedule):
            step(u)

    def gather_step(n, s):
        sems = lambda slot: (gs_sem.at[n, slot], gr_sem.at[n, slot])
        if s == 0:
            own = gat_ref.at[n, bo, bi]
            for o in range(1, inner):
                send(own, own, *sems(o - 1), on_inner(o))
        elif s == 1:
            for o in range(1, inner):
                got = gat_ref.at[n, bo, lax.rem(bi + inner - o, inner)]
                remote(got, got, *sems(o - 1), on_inner(o)).wait_recv()
            own = gat_ref.at[n, bo]
            for o in range(1, OUTER):
                send(own, own, *sems(inner - 1 + o - 1), on_outer(o))
        else:
            for o in range(1, OUTER):
                got = gat_ref.at[n, lax.rem(bo + OUTER - o, OUTER)]
                remote(got, got, *sems(inner - 1 + o - 1), on_outer(o)).wait_recv()

    def backward_conv(n):
        st[...] = jnp.zeros_like(st)
        coef[0:32, 0 : 2 * C] = split3(jnp.concatenate([sv[n, 0], sv[n, 1]], axis=1))
        for i in range(T // R):
            slot()
            rows = pl.ds(i * R, R)
            if n < 3:
                shift_rows(i)
            da = (
                dot_back(x3[rows, 0:C], cw[n, 0:C, :])
                + dot_back(x3[rows, C : 2 * C], cw[n, C : 2 * C, :])
                + dot_back(x3[rows, 2 * C : 3 * C], cw[n, 2 * C : 3 * C, :])
            )
            spread_out = dot(mem[rows, :], coef[:, 0 : 2 * C])
            d = value(n, rows)
            h = spread_out[:, 0:C] * d + spread_out[:, C : 2 * C]
            th = jnp.tanh(h)
            dy = da * ((0.5 + 0.5 * th) * (1.0 + h - h * th))
            dyb[rows, :] = dy
            add_stats(rows, dy, dy * d)

    def backward_send(n):
        scale, mean = sv[n, 2], sv[n, 3]
        s1, s2 = st[0:8, 0:C], st[0:8, C : 2 * C]
        bx[n, time, 0:4, :] = (scale * (s2 - mean * s1))[0:4]
        bx[n, time, 4:8, :] = s1[0:4]
        bx[n, time, 8:9, :] = dyb[0:1, :]
        bx[n, time, 9:10, :] = dyb[T - 1 : T, :]
        bx[n, time, 10:11, :] = brow[0:1, :]
        bx[n, time, 11:16, :] = jnp.zeros((5, C), F32)
        exchange(bx.at[n], 4 + n, n % 2 == 1)

    def weight_grad(n):
        for side in range(2):
            lane = (core if side else 1 - core) * half
            left = asave[n, :, pl.ds(pl.multiple_of(lane, half), half)]
            for k in range(3):
                u = 3 * n + k
                g = dot_rows(left, x3[:, k * C : (k + 1) * C]).astype(BF16)
                if side:
                    wkeep[u] = g
                else:
                    wsnd[u] = g
                    progress[u] = 0
                    step(u)

    def backward_norm(n):
        exchanged(bx.at[n], 4 + n, n % 2 == 1)
        slot()
        zero4 = jnp.zeros((4, C), F32)
        dgain, dshift = jnp.zeros((4, C), F32), jnp.zeros((4, C), F32)
        bias_row = jnp.zeros((1, C), F32)
        for j in range(members):
            dgain = dgain + bx[n, j, 0:4, :]
            dshift = dshift + bx[n, j, 4:8, :]
            if n % 2 == 1:
                bias_row = bias_row + bx[n, j, 10:11, :]
        dmod = jnp.concatenate([dgain, dshift], axis=1)
        quarter = C // 2
        packet = [dmod[:, q * quarter : (q + 1) * quarter] for q in range(4)]
        packet += [bias_row[:, 0:quarter], bias_row[:, quarter:C]]
        packet += [
            jnp.concatenate([style_ref[0:1, :], style_ref[1:2, :]], axis=1),
            jnp.concatenate([style_ref[2:3, :], style_ref[3:4, :]], axis=1),
            jnp.zeros((12, quarter), F32),
        ]
        gat_ref[n, bo, bi] = jnp.concatenate(packet, axis=0).astype(BF16)
        gather_step(n, 0)
        dmod8 = jnp.concatenate([dmod, jnp.zeros((4, 2 * C), F32)], axis=0)
        part = dot_back(dmod8, fcw[n], highest)[0:UTT]
        if n == 3:
            styleg_ref[...] = part
        else:
            styleg_ref[...] += part
        scale, mean, gain = sv[n, 2], sv[n, 3], sv[n, 4]
        mean_dn = gain * jnp.concatenate([dshift, zero4], axis=0) * inv_totals
        mean_x = gain * jnp.concatenate([dgain, zero4], axis=0) * inv_totals
        alpha = scale * gain
        kappa = -(scale * scale) * mean_x
        delta = -scale * mean_dn - kappa * mean
        coef[0:32, 0 : 3 * C] = split3(jnp.concatenate([alpha, kappa, delta], axis=1))
        p = piv[8 * n : 8 * n + 1, :]

        def edge(dy, raw, own, cot_edge):
            out = (
                pick_row(alpha, own) * dy
                + pick_row(kappa, own) * (raw - p)
                + pick_row(delta, own)
            )
            if n == 2:
                out = (out + cot_edge * root_half) * root_half
            return out

        if n > 0:
            sh[7:8, :] = edge(
                bx[n, before_me, 9:10, :],
                fx[n, before_me, 9:10, :],
                first_own,
                fx[0, before_me, 11:12, :],
            )
            sh[T + 8 : T + 9, :] = edge(
                bx[n, after_me, 8:9, :],
                fx[n, after_me, 8:9, :],
                last_own,
                fx[0, after_me, 10:11, :],
            )
        if n == 2:
            brow[...] = jnp.zeros_like(brow)
        slot()

        @pl.loop(0, T // R)
        def _(i):
            r0 = pl.multiple_of(i * R, R)
            rows = pl.ds(r0, R)
            spread_out = dot(mem[rows, :], coef[...])
            dv = (
                spread_out[:, 0:C] * dyb[rows, :]
                + spread_out[:, C : 2 * C] * value(n, rows)
                + spread_out[:, 2 * C : 3 * C]
            )
            mid = pl.ds(pl.multiple_of(r0 + 8, 8), R)
            if n % 2 == 1:
                sh[mid, :] = dv
            elif n == 2:
                carried = (dv + cot[rows, :].astype(F32) * root_half) * root_half
                vs[2, rows, :] = carried
                sh[mid, :] = carried
                brow[0:1, :] += jnp.sum(carried, axis=0, keepdims=True)
            else:
                phon[rows, :] = (dv + vs[2, rows, :]).astype(BF16)

    for n in (3, 2, 1, 0):
        if n == 3:
            weight_grad(n)
        backward_conv(n)
        slot()
        backward_send(n)
        slot()
        if n == 3:
            forward_conv(n)
        else:
            weight_grad(n)
        slot()
        backward_norm(n)
        slot()
        if n < 3:
            gather_step(n + 1, 1)

    ph = PH // 2
    psnd, pkeep = x3.at[pl.ds(0, ph), 0:C], x3.at[pl.ds(0, ph), C : 2 * C]
    prcv1 = [asave.at[o, pl.ds(0, ph)] for o in range(1, yn)]
    psems = lambda slot: (ps_sem.at[slot], pr_sem.at[slot])
    for side in range(2):
        lane = pl.multiple_of((core if side else 1 - core) * ph, WIDE)
        block = 256

        @pl.loop(0, ph // block)
        def _(i):
            at = pl.multiple_of(i * block, block)
            lanes = pl.ds(pl.multiple_of(lane + at, WIDE), block)
            g = dot_rows(pick[:, lanes], phon[pl.ds(0, T), :])
            (pkeep if side else psnd)[pl.ds(at, block), :] = g.astype(BF16)

        if side == 0:
            send(psnd, prcv0, *psems(0), on_core())
        slot()
    remote(psnd, prcv0, *psems(0), on_core()).wait_recv()
    pkeep[...] = (pkeep[...].astype(F32) + prcv0[...].astype(F32)).astype(BF16)
    for o in range(1, yn):
        send(pkeep, prcv1[o - 1], *psems(o), on_y(o))
    slot()
    spot = pg_ref.at[pl.ds(pl.multiple_of(core * ph, WIDE), ph)]
    for u in next(schedule):
        if u >= 0:
            step(u)
            continue
        whole = pkeep[...].astype(F32)
        for o in range(1, yn):
            remote(pkeep, prcv1[o - 1], *psems(o), on_y(o)).wait_recv()
            whole = whole + prcv1[o - 1][...].astype(F32)
        spot[...] = whole.astype(BF16)
        send(spot, spot, *psems(yn), on_core())
        gather_step(0, 1)
    got = pg_ref.at[pl.ds(pl.multiple_of((1 - core) * ph, WIDE), ph)]
    remote(got, got, *psems(yn), on_core()).wait_recv()
    for n in range(4):
        gather_step(n, 2)
    drain()


def dot_general_exact(left, right):
    return jnp.dot(left, right, precision=highest, preferred_element_type=F32)


def finish(
    frames_in,
    pg_in,
    style_in,
    gat_in,
    wg_in,
    frames_out,
    pg_out,
    style_out,
    fcg_out,
    fcb_out,
    wg_out,
    bias_out,
    whigh,
    phigh,
    fcg,
    dm,
    styles,
    rsem,
    wsem,
):
    C = frames_in.shape[1]
    half = C // 2
    n_batch = gat_in.shape[1]
    units = [(n, k) for n in range(4) for k in range(3)]
    whole = pltpu.make_async_copy(frames_in, frames_out, rsem.at[0])
    stores = [
        pltpu.make_async_copy(whigh.at[u], wg_out.at[n, pl.ds(k * C, C)], wsem.at[u])
        for u, (n, k) in enumerate(units)
    ]
    pstore = pltpu.make_async_copy(phigh, pg_out, wsem.at[12])
    fstore = pltpu.make_async_copy(fcg, fcg_out, wsem.at[13])
    for u in range(12):
        n, k = units[u]
        whigh[u] = wg_in[n, k * C : (k + 1) * C, :].astype(F32)
        stores[u].start()
    phigh[...] = pg_in[...].astype(F32)
    pstore.start()
    whole.start()
    style_out[...] = style_in[...]
    bias = [jnp.zeros((1, C), F32), jnp.zeros((1, C), F32)]
    for b in range(n_batch):
        pack = gat_in[0, b].astype(F32)
        for side in range(2):
            styles[b * UTT + 2 * side : b * UTT + 2 * side + 1, :] = pack[18 + side : 19 + side, 0:half // 2]
            styles[b * UTT + 2 * side + 1 : b * UTT + 2 * side + 2, :] = pack[18 + side : 19 + side, half // 2 : half]
    for n in range(4):
        for b in range(n_batch):
            pack = gat_in[n, b].astype(F32)
            dm[b * UTT : (b + 1) * UTT, :] = jnp.concatenate(
                [pack[q * UTT : (q + 1) * UTT] for q in range(4)], axis=1
            )
            if n % 2 == 1:
                bias[n // 2] = bias[n // 2] + jnp.concatenate(
                    [pack[16:17], pack[17:18]], axis=1
                )
        fcg[n] = dot_rows(styles[...].astype(BF16), dm[...].astype(BF16))
        fcb_out[n : n + 1, :] = jnp.sum(dm[...], axis=0, keepdims=True)
    bias_out[...] = jnp.concatenate(bias, axis=0)
    fstore.start()
    whole.wait()
    for store in stores + [pstore, fstore]:
        store.wait()


def on_device(
    n_batch,
    members,
    phonemes,
    durations,
    utt_frames,
    style_codes,
    fc_weight,
    fc_bias,
    conv_weight,
    conv_bias,
    cotangent,
):
    T, C = cotangent.shape
    PH = phonemes.shape[0]
    inner = n_batch // OUTER
    yn = members // CORES
    assert inner == yn
    half = C // 2
    VM, ANY = pltpu.VMEM, pl.ANY
    vspec = pl.BlockSpec(memory_space=pltpu.VMEM)
    aspec = pl.BlockSpec(memory_space=pl.ANY)
    most = yn
    r1 = half // most
    nslots = 2 * (yn + inner + OUTER - 2)
    DMA = pltpu.SemaphoreType.DMA
    roomy = PH <= 1024 and members <= 4
    held = VM if roomy else jax.ShapeDtypeStruct
    scratch = [
        VM((PH, C), BF16),
        VM(fc_weight.shape, F32),
        VM(conv_weight.shape, BF16),
        VM((T, C), BF16),
        VM((T, PH), BF16),
        VM((T, WIDE), BF16),
        VM((16, T), BF16),
        VM((T, WIDE), F32),
        VM((T, WIDE), F32),
        VM((T, C), BF16),
        VM((3, T, C), F32),
        VM((32, C), F32),
        VM((4, T, C), BF16),
        VM((T + 16, C), F32),
        VM((T, 3 * C), BF16),
        VM((T, C), F32),
        VM((4, 8, 2 * C), F32),
        VM((4, 5, 8, C), F32),
        VM((WIDE, 3 * C), BF16),
        VM((16, 2 * C), F32),
        VM((8, C), F32),
        VM((4, members, 16, C), F32),
        VM((4, members, 16, C), F32),
        VM((PH // 2, C), BF16),
        VM((12, half, C), BF16),
        VM((12, half, C), BF16),
        VM((12, half, C), BF16),
        VM((12, most - 1, r1, C), BF16),
        VM((12, r1, C), BF16),
        VM((12, max((most - 1) * r1 // most, (OUTER - 1) * r1 // OUTER), C), BF16),
        VM((12, r1 // min(most, OUTER), C), BF16),
        VM((12, (OUTER - 1) * r1 // most, C // OUTER), BF16),
        VM((12, (most - 1) * r1 // OUTER, C // most), BF16),
        VM((12, r1 // most, C // OUTER), BF16),
        VM((12, r1 // OUTER, C // most), BF16),
        DMA((7,)),
        DMA((12,)),
        DMA((8, members)),
        DMA((8, members)),
        DMA((4, inner + OUTER)),
        DMA((4, inner + OUTER)),
        DMA((yn + 1,)),
        DMA((yn + 1,)),
        DMA((12, nslots)),
        DMA((12, nslots)),
    ]
    frames_out, pgrad, style_part, gathered, wgrad = pl.pallas_call(
        functools.partial(kernel, inner, members),
        out_shape=(
            held((T, C), BF16),
            held((PH, C), BF16),
            held(style_codes.shape, F32),
            held((4, OUTER, inner, 32, C // 2), BF16),
            held(conv_weight.shape, BF16),
        ),
        in_specs=[
            aspec,
            vspec,
            pl.BlockSpec(memory_space=pltpu.SMEM),
            vspec,
            aspec,
            vspec,
            aspec,
            vspec,
            aspec,
        ],
        out_specs=[vspec, vspec, vspec, vspec, vspec if roomy else aspec],
        scratch_shapes=scratch,
        compiler_params=pltpu.CompilerParams(
            collective_id=0, has_side_effects=True, vmem_limit_bytes=(54 if roomy else 63) * 1024 * 1024
        ),
    )(
        phonemes,
        durations,
        utt_frames,
        style_codes,
        fc_weight,
        fc_bias,
        conv_weight,
        conv_bias,
        cotangent,
    )
    utts = n_batch * UTT
    return pl.pallas_call(
        finish,
        out_shape=(
            jax.ShapeDtypeStruct((T, C), BF16),
            jax.ShapeDtypeStruct((PH, C), F32),
            jax.ShapeDtypeStruct(style_codes.shape, F32),
            jax.ShapeDtypeStruct(fc_weight.shape, F32),
            jax.ShapeDtypeStruct(fc_bias.shape, F32),
            jax.ShapeDtypeStruct(conv_weight.shape, F32),
            jax.ShapeDtypeStruct(conv_bias.shape, F32),
        ),
        in_specs=[vspec] * 5,
        out_specs=[aspec, aspec, vspec, aspec, vspec, aspec, vspec],
        scratch_shapes=[
            VM((12, C, C), F32),
            VM((PH, C), F32),
            VM(fc_weight.shape, F32),
            VM((utts, 2 * C), F32),
            VM((utts, style_codes.shape[1]), F32),
            DMA((1,)),
            DMA((14,)),
        ],
        compiler_params=pltpu.CompilerParams(vmem_limit_bytes=32 * 1024 * 1024),
    )(frames_out, pgrad, style_part, gathered.reshape(4, n_batch, 32, C // 2), wgrad)


def solution(mesh):
    return jax.shard_map(
        functools.partial(on_device, mesh.shape["batch"], mesh.shape["tm"]),
        mesh=mesh,
        in_specs=(
            P("batch", None),
            P("batch", None),
            P("batch", None),
            P("batch", None),
            P(),
            P(),
            P(),
            P(),
            P(("batch", "tm"), None),
        ),
        out_specs=(
            P(("batch", "tm"), None),
            P("batch", None),
            P("batch", None),
            P(),
            P(),
            P(),
            P(),
        ),
        check_vma=False,
    )
```

```python
import functools
import jax
import jax.numpy as jnp
from jax import lax
from jax.experimental import pallas as pl
from jax.experimental.pallas import tpu as pltpu
from jax.sharding import PartitionSpec as P

F32, BF16 = jnp.float32, jnp.bfloat16
MESH = pl.DeviceIdType.MESH
highest = lax.Precision.HIGHEST
norm_eps = 1e-05
root_half = 0.7071067811865476
UTT = 4
CORES = 2
OUTER = 4
WIDE = 128
ORDERS = ["xyz", "yxz", "yxz", "xyz", "xzy", "yxz", "xzy", "xzy", "yxz", "xzy", "xyz", "xzy"]
SCHEDULE = [
    [9, 10, 11],
    [],
    [],
    [9],
    [],
    [],
    [10],
    [],
    [],
    [11],
    [9],
    [10],
    [9],
    [],
    [6, 7, 8, 11, 10, 9],
    [],
    [],
    [],
    [],
    [6, 8, 10],
    [7, 11, 9],
    [],
    [3, 4, 5, 8, 11, 10],
    [6],
    [9],
    [7, 9],
    [],
    [3, 5, 8, 6],
    [4, 7, 11],
    [3, 6],
    [0, 1, 2, 5, 8, 7, 10],
    [],
    [11],
    [4, 10, 11],
    [3],
    [0],
    [1],
    [2, 0, 1, 2, 5, 4, 3, 8, 6, 7, 0, 1, 2, 5, 0, 4, -1, 1, 2, 3, 5, 6, 7, 8, 1, 0, 2, 4, 5, 3, 6, 7, 8, 5, 1, 0, 3, 1, 2, 4, 0, 2, 4],
]


def dot(left, right):
    return jnp.dot(left, right, preferred_element_type=F32)


def dot_rows(left, right):
    return lax.dot_general(left, right, (((0,), (0,)), ((), ())), preferred_element_type=F32)


def dot_back(left, right, precision=None):
    return lax.dot_general(
        left, right, (((1,), (1,)), ((), ())), precision=precision, preferred_element_type=F32
    )


def split3(values):
    high = values.astype(BF16).astype(F32)
    rest = values - high
    mid = rest.astype(BF16).astype(F32)
    return jnp.concatenate([high, mid, rest - mid, jnp.zeros_like(values)], axis=0).astype(BF16)


def kernel(
    inner,
    members,
    phon_hbm,
    dur_ref,
    utt_ref,
    style_ref,
    fcw_hbm,
    fcb_ref,
    cw_hbm,
    cb_ref,
    cot_hbm,
    frames_ref,
    pg_ref,
    styleg_ref,
    gat_ref,
    wg_ref,
    phon,
    fcw,
    cw,
    cot,
    pick,
    mem,
    memt,
    amask,
    bmask,
    x0,
    vs,
    piv,
    asave,
    sh,
    x3,
    dyb,
    mod,
    sv,
    coef,
    st,
    brow,
    fx,
    bx,
    prcv0,
    wsnd,
    wkeep,
    wrcv0,
    rcv1,
    acc2,
    rcv2,
    acc3,
    rcv3z,
    rcv3o,
    acc4z,
    acc4o,
    lsem,
    csem,
    xs_sem,
    xr_sem,
    gs_sem,
    gr_sem,
    ps_sem,
    pr_sem,
    ws_sem,
    wr_sem,
):
    T, C = cot_hbm.shape
    PH = phon_hbm.shape[0]
    yn = members // CORES
    batch = lax.axis_index("batch")
    time = lax.axis_index("tm")
    bo, bi = batch // inner, batch % inner
    ty, core = time // CORES, time % CORES
    R = 512
    t0 = time * T

    def at(i):
        return i * R if isinstance(i, int) else pl.multiple_of(i * R, R)

    loads = [
        pltpu.make_async_copy(phon_hbm, phon, lsem.at[0]),
        pltpu.make_async_copy(fcw_hbm, fcw, lsem.at[1]),
        pltpu.make_async_copy(cot_hbm, cot, lsem.at[2]),
    ] + [pltpu.make_async_copy(cw_hbm.at[n], cw.at[n], lsem.at[3 + n]) for n in range(4)]
    for i in (0, 1, 3, 2, 4, 5, 6):
        loads[i].start()

    def on_tm(o):
        return (batch, lax.rem(time + o, members))

    def on_core():
        return (batch, ty * CORES + (1 - core))

    def on_y(o):
        return (batch, lax.rem(ty + o, yn) * CORES + core)

    def on_inner(o):
        return (bo * inner + lax.rem(bi + o, inner), time)

    def on_outer(o):
        return (lax.rem(bo + o, OUTER) * inner + bi, time)

    partners = (
        [on_tm(o) for o in range(1, members)]
        + [on_inner(o) for o in range(1, inner)]
        + [on_outer(o) for o in range(1, OUTER)]
    )
    barrier = pltpu.get_barrier_semaphore()
    for partner in partners:
        pl.semaphore_signal(barrier, inc=1, device_id=partner, device_id_type=MESH)

    def remote(src, dst, sem, device):
        sent, landed, index = sem
        return pltpu.make_async_remote_copy(
            src_ref=src,
            dst_ref=dst,
            send_sem=sent.at[index],
            recv_sem=landed.at[index],
            device_id=device,
            device_id_type=MESH,
        )

    unsent = []

    def send(src, dst, sem, device, like=None):
        remote(src, dst, sem, device).start()
        unsent.append((like or (lambda: src), sem))

    def drain():
        for like, sem in unsent:
            remote(like(), like(), sem, on_core()).wait_send()
        unsent.clear()

    lens = [utt_ref[0, u] for u in range(UTT)]
    starts, ends, total = [], [], 0
    for u in range(UTT):
        starts.append(total)
        total = total + lens[u]
        ends.append(total)
    row8 = lax.broadcasted_iota(jnp.int32, (8, C), 0)

    def by_utt(values, other):
        out = jnp.full((8, C), other, F32)
        for u in range(UTT):
            out = jnp.where(row8 == u, values[u], out)
        return out

    def local_counts(j):
        return by_utt(
            [
                jnp.maximum(jnp.minimum(ends[u], (j + 1) * T) - jnp.maximum(starts[u], j * T), 0)
                .astype(F32)
                for u in range(UTT)
            ],
            0.0,
        )

    totals = by_utt([n.astype(F32) for n in lens], 1.0)
    inv_totals = 1.0 / totals
    mine = local_counts(time)
    inv_mine = 1.0 / jnp.maximum(mine, 1.0)

    def owner_rows(t):
        return [
            jnp.logical_and(t >= starts[u], t < ends[u]).astype(F32) for u in range(UTT)
        ]

    first_own, last_own = owner_rows(t0), owner_rows(t0 + T - 1)

    def pick_row(values, own):
        out = own[0] * values[0:1]
        for u in range(1, UTT):
            out = out + own[u] * values[u : u + 1]
        return out

    @pl.loop(0, T // WIDE)
    def _(i):
        r0 = pl.multiple_of(i * WIDE, WIDE)
        tt = lax.broadcasted_iota(jnp.int32, (16, WIDE), 1) + r0 + t0
        row = lax.broadcasted_iota(jnp.int32, (16, WIDE), 0)
        ownt = jnp.zeros((16, WIDE), F32)
        for u in range(UTT):
            inside = jnp.logical_and(tt >= starts[u], tt < ends[u])
            ownt = jnp.where(jnp.logical_and(inside, row == u), 1.0, ownt)
        memt[:, pl.ds(r0, WIDE)] = ownt.astype(BF16)

    tiles = PH // WIDE
    durs = jnp.concatenate(
        [dur_ref[0:1, j * WIDE : (j + 1) * WIDE] for j in range(tiles)], axis=0
    ).astype(F32)
    upper = (
        lax.broadcasted_iota(jnp.int32, (WIDE, WIDE), 0)
        <= lax.broadcasted_iota(jnp.int32, (WIDE, WIDE), 1)
    ).astype(BF16)
    within = dot(durs.astype(BF16), upper)
    so_far = jnp.zeros((1, 1), F32)
    for j in range(tiles):
        stop = within[j : j + 1] + so_far
        begin = (stop - durs[j : j + 1]).astype(jnp.int32)
        stop = stop.astype(jnp.int32)
        so_far = so_far + within[j : j + 1, WIDE - 1 : WIDE]
        t = lax.broadcasted_iota(jnp.int32, (T, WIDE), 0) + t0
        inside = jnp.logical_and(t >= begin, t < stop)
        pick[:, j * WIDE : (j + 1) * WIDE] = jnp.where(inside, 1.0, 0.0).astype(BF16)

    loads[0].wait()

    @pl.loop(0, T // R)
    def _(i):
        r0 = pl.multiple_of(i * R, R)
        x0[pl.ds(r0, R), :] = dot(pick[pl.ds(r0, R), :], phon[...]).astype(BF16)

    def value(n, rows):
        if n == 0:
            return x0[rows, :].astype(F32) - piv[0:1, :]
        return vs[n - 1, rows, :]

    def add_stats(rows, one, two):
        both = jnp.concatenate([one.astype(BF16), two.astype(BF16)], axis=1)
        st[...] += dot(memt[:, rows], both)

    st[...] = jnp.zeros_like(st)
    piv[0:8, :] = jnp.broadcast_to(x0[0:16, :].astype(F32)[0:1], (8, C))

    @pl.loop(0, T // R)
    def _(i):
        rows = pl.ds(pl.multiple_of(i * R, R), R)
        d = value(0, rows)
        add_stats(rows, d, d * d)

    pl.semaphore_wait(barrier, len(partners))

    def exchange(buf, phase, full):
        for o in range(1, members):
            rows = 16 if full or o in (1, members - 1) else 8
            send(
                buf.at[time, pl.ds(0, rows)],
                buf.at[time, pl.ds(0, rows)],
                (xs_sem, xr_sem, (phase, o)),
                on_tm(o),
            )

    def exchanged(buf, phase, full):
        for o in range(1, members):
            rows = 16 if full or o in (1, members - 1) else 8
            ref = buf.at[lax.rem(time + members - o, members), pl.ds(0, rows)]
            remote(ref, ref, (xs_sem, xr_sem, (phase, o)), on_tm(o)).wait_recv()

    before_me, after_me = lax.rem(time + members - 1, members), lax.rem(time + 1, members)

    def forward_send(n, first, last):
        p = piv[8 * n : 8 * n + 1, :]
        s1, s2 = st[0:8, 0:C], st[0:8, C : 2 * C]
        local = s1 * inv_mine
        fx[n, time, 0:4, :] = (local + p)[0:4]
        fx[n, time, 4:8, :] = (s2 - s1 * local)[0:4]
        fx[n, time, 8:9, :] = first + p
        fx[n, time, 9:10, :] = last + p
        if n == 1:
            loads[2].wait()
            fx[n, time, 10:11, :] = cot[0:16, :].astype(F32)[0:1]
            fx[n, time, 11:12, :] = cot[T - 16 : T, :].astype(F32)[15:16]
            fx[n, time, 12:16, :] = jnp.zeros((4, C), F32)
        else:
            fx[n, time, 10:16, :] = jnp.zeros((6, C), F32)
        exchange(fx.at[n], n, False)

    def forward_norm(n):
        exchanged(fx.at[n], n, False)
        p = piv[8 * n : 8 * n + 1, :]
        zero4 = jnp.zeros((4, C), F32)
        counts = [local_counts(j) for j in range(members)]
        means = [
            jnp.concatenate([fx[n, j, 0:4, :], zero4], axis=0) for j in range(members)
        ]
        mean = counts[0] * means[0]
        for j in range(1, members):
            mean = mean + counts[j] * means[j]
        mean = mean * inv_totals
        spread = jnp.zeros((8, C), F32)
        for j in range(members):
            off = means[j] - mean
            spread = spread + counts[j] * off * off + jnp.concatenate(
                [fx[n, j, 4:8, :], zero4], axis=0
            )
        scale = lax.rsqrt(jnp.maximum(spread * inv_totals, 0.0) + norm_eps)
        gain, shift = 1.0 + mod[n, :, 0:C], mod[n, :, C : 2 * C]
        slope = gain * scale
        mean = mean - p
        half_a, half_b = 0.5 * slope, 0.5 * (shift - slope * mean)
        sv[n, 0] = half_a
        sv[n, 1] = half_b
        sv[n, 2] = scale
        sv[n, 3] = mean
        sv[n, 4] = gain
        coef[0:32, 0 : 2 * C] = split3(jnp.concatenate([half_a, half_b], axis=1))

        def edge(raw, own):
            h = pick_row(half_a, own) * (raw - p) + pick_row(half_b, own)
            return h + h * jnp.tanh(h)

        sh[7:8, :] = edge(fx[n, before_me, 9:10, :], first_own)
        sh[T + 8 : T + 9, :] = edge(fx[n, after_me, 8:9, :], last_own)

        @pl.loop(0, T // R)
        def _(i):
            r0 = pl.multiple_of(i * R, R)
            rows = pl.ds(r0, R)
            spread_out = dot(mem[rows, :], coef[:, 0 : 2 * C])
            h = spread_out[:, 0:C] * value(n, rows) + spread_out[:, C : 2 * C]
            a = h + h * jnp.tanh(h)
            sh[pl.ds(pl.multiple_of(r0 + 8, 8), R), :] = a
            asave[n, rows, :] = a.astype(BF16)

    def shifted(r0):
        window = sh[pl.ds(r0, R + 16), :]
        rows = pl.ds(r0, R)
        bm = jnp.concatenate([bmask[rows, :]] * (C // WIDE), axis=1)
        am = jnp.concatenate([amask[rows, :]] * (C // WIDE), axis=1)
        return (
            (window[7 : 7 + R] * bm).astype(BF16),
            (window[9 : 9 + R] * am).astype(BF16),
            window[8 : 8 + R],
        )

    def forward_conv(n):
        st[...] = jnp.zeros_like(st)

        def chunk(i):
            r0 = at(i)
            rows = pl.ds(r0, R)
            prev, following, _ = shifted(r0)
            c = dot(jnp.concatenate([prev, asave[n, rows, :], following], axis=1), cw[n])
            if n % 2 == 1:
                b = n // 2
                kept = x0[rows, :].astype(F32) if n == 1 else vs[1, rows, :] + piv[16:17, :]
                c = (c + cb_ref[b : b + 1, :] + kept) * root_half
            if n == 3:
                frames_ref[rows, :] = c.astype(BF16)
                return

            @pl.when(i == 0)
            def _():
                m = jnp.mean(c, axis=0, keepdims=True)
                piv[8 * (n + 1) : 8 * (n + 2), :] = jnp.broadcast_to(m, (8, C))

            d = c - piv[8 * (n + 1) : 8 * (n + 1) + 1, :]
            vs[n, rows, :] = d
            add_stats(rows, d, d * d)

        if n < 3:
            loads[3 + n].wait()
            pl.loop(0, T // R)(chunk)
        else:
            @pl.loop(0, T // R)
            def _(i):
                slots_in(i)
                chunk(i)

    def shift_rows(i):
        r0 = at(i)
        rows = pl.ds(r0, R)
        prev, following, mid = shifted(r0)
        x3[rows, 0:C] = following
        x3[rows, C : 2 * C] = mid.astype(BF16)
        x3[rows, 2 * C : 3 * C] = prev

    def cotangent_rows():
        brow[...] = jnp.zeros_like(brow)

        @pl.loop(0, T // R)
        def _(i):
            r0 = pl.multiple_of(i * R, R)
            g = cot[pl.ds(r0, R), :].astype(F32) * root_half
            sh[pl.ds(pl.multiple_of(r0 + 8, 8), R), :] = g
            brow[0:1, :] += jnp.sum(g, axis=0, keepdims=True)

        sh[7:8, :] = fx[1, before_me, 11:12, :] * root_half
        sh[T + 8 : T + 9, :] = fx[1, after_me, 10:11, :] * root_half
        pl.loop(0, T // R)(shift_rows)

    first16 = x0[0:16, :].astype(F32)
    last16 = x0[T - 16 : T, :].astype(F32)
    p0 = piv[0:1, :]
    forward_send(0, first16[0:1] - p0, last16[15:16] - p0)

    coef[...] = jnp.zeros_like(coef)

    @pl.loop(0, T // WIDE)
    def _(i):
        r0 = pl.multiple_of(i * WIDE, WIDE)
        t = lax.broadcasted_iota(jnp.int32, (WIDE, WIDE), 0) + r0 + t0
        lane = lax.broadcasted_iota(jnp.int32, (WIDE, WIDE), 1)
        before, after = t >= 1, t >= 0
        own = jnp.zeros((WIDE, WIDE), F32)
        slot = lax.rem(lane, 8)
        for u in range(UTT):
            before = jnp.logical_and(before, t != starts[u])
            after = jnp.logical_and(after, t + 1 != ends[u])
            inside = jnp.logical_and(t >= starts[u], t < ends[u])
            own = jnp.where(jnp.logical_and(inside, slot == u), 1.0, own)
        own = jnp.where(lane < 24, own, 0.0)
        mem[pl.ds(r0, WIDE), :] = own.astype(BF16)
        bmask[pl.ds(r0, WIDE), :] = before.astype(F32)
        amask[pl.ds(r0, WIDE), :] = after.astype(F32)

    loads[1].wait()
    style8 = jnp.concatenate(
        [style_ref[...], jnp.zeros((8 - UTT, style_ref.shape[1]), F32)], axis=0
    )
    for n in range(4):
        mod[n] = dot_general_exact(style8, fcw[n]) + fcb_ref[n : n + 1, :]

    for n in range(3):
        forward_norm(n)
        forward_conv(n)
        forward_send(n + 1, vs[n, 0:1, :], vs[n, T - 1 : T, :])
        if n == 1:
            cotangent_rows()
    forward_norm(3)
    loads[6].wait()

    axes = {
        "y": (yn, ty, on_y),
        "x": (inner, bi, on_inner),
        "z": (OUTER, bo, on_outer),
    }
    half = C // 2

    def plan(u):
        return tuple(axes[name] for name in ORDERS[u])

    def out_rows(u, side, start, count):
        n, k = u // 3, u % 3
        base = k * C + side * half + start
        return wg_ref.at[n, pl.ds(pl.multiple_of(base, 16), count)]

    def slots(u):
        (k1, _, _), (k2, _, _), (k3, _, _) = plan(u)
        base = [0, 1, k1, k1 + k2 - 1]
        width = k1 + k2 + k3 - 2
        return base, width

    def reduce_step(u, s):
        (k1, m1, d1), (k2, m2, d2), (k3, m3, d3) = plan(u)
        base, width = slots(u)
        r1, r2, w3 = half // k1, half // k1 // k2, C // k3
        rcv3, acc4 = (rcv3z, acc4z) if ORDERS[u][2] == "z" else (rcv3o, acc4o)
        sems = lambda slot: (ws_sem, wr_sem, (u, slot))

        def band(ref, index, count):
            return ref.at[u, pl.ds(pl.multiple_of(index * count, 16), count)]

        def top(count):
            return lambda: wg_ref.at[u // 3, pl.ds(0, count)]

        def lanes(index):
            return pl.ds(pl.multiple_of(index * w3, WIDE), w3)

        def other(m, k, o):
            return lax.rem(m + o, k)

        def sums(own, k, first, landed, device):
            for o in range(1, k):
                remote(landed(o), landed(o), sems(first + o - 1), device(o)).wait_recv()
                own = own + landed(o)[...].astype(F32)
            return own.astype(BF16)

        land1 = lambda o: rcv1.at[u, o - 1]
        land2 = lambda o: band(rcv2, o - 1, r2)
        land3 = lambda o: band(rcv3, o - 1, r2)
        row0 = m1 * r1 + m2 * r2
        if s == 0:
            send(wsnd.at[u], wrcv0.at[u], sems(0), on_core(), lambda: wsnd.at[u])
        elif s == 1:
            remote(wsnd.at[u], wrcv0.at[u], sems(0), on_core()).wait_recv()
            wkeep[u] = (wkeep[u].astype(F32) + wrcv0[u].astype(F32)).astype(BF16)
            for o in range(1, k1):
                send(
                    band(wkeep, other(m1, k1, o), r1),
                    land1(o),
                    sems(base[1] + o - 1),
                    d1(o),
                    lambda: wkeep.at[u, pl.ds(0, r1)],
                )
        elif s == 2:
            own = band(wkeep, m1, r1)[...].astype(F32)
            acc2[u] = sums(own, k1, base[1], land1, d1)
            for o in range(1, k2):
                send(
                    band(acc2, other(m2, k2, o), r2),
                    land2(o),
                    sems(base[2] + o - 1),
                    d2(o),
                    lambda: acc2.at[u, pl.ds(0, r2)],
                )
        elif s == 3:
            own = band(acc2, m2, r2)[...].astype(F32)
            acc3[u, 0:r2] = sums(own, k2, base[2], land2, d2)
            for o in range(1, k3):
                piece = acc3.at[u, pl.ds(0, r2), lanes(other(m3, k3, o))]
                like = lambda: acc3.at[u, pl.ds(0, r2), pl.ds(0, w3)]
                send(piece, land3(o), sems(base[3] + o - 1), d3(o), like)
        elif s == 4:
            own = acc3[u, pl.ds(0, r2), lanes(m3)].astype(F32)
            acc4[u] = sums(own, k3, base[3], land3, d3)
            spot = out_rows(u, core, row0, r2).at[:, lanes(m3)]
            pltpu.make_async_copy(acc4.at[u], spot, csem.at[u]).start()
            for o in range(1, k3):
                send(acc4.at[u], spot, sems(width + base[3] + o - 1), d3(o), lambda: acc4.at[u])
        elif s == 5:
            spot = out_rows(u, core, row0, r2)
            for o in range(1, k3):
                got = spot.at[:, lanes(other(m3, k3, k3 - o))]
                remote(got, got, sems(width + base[3] + o - 1), d3(o)).wait_recv()
            pltpu.make_async_copy(acc4.at[u], spot.at[:, lanes(m3)], csem.at[u]).wait()
            for o in range(1, k2):
                send(spot, spot, sems(width + base[2] + o - 1), d2(o), top(r2))
        elif s == 6:
            for o in range(1, k2):
                got = out_rows(u, core, m1 * r1 + other(m2, k2, k2 - o) * r2, r2)
                remote(got, got, sems(width + base[2] + o - 1), d2(o)).wait_recv()
            spot = out_rows(u, core, m1 * r1, r1)
            for o in range(1, k1):
                send(spot, spot, sems(width + base[1] + o - 1), d1(o), top(r1))
        elif s == 7:
            for o in range(1, k1):
                got = out_rows(u, core, other(m1, k1, k1 - o) * r1, r1)
                remote(got, got, sems(width + base[1] + o - 1), d1(o)).wait_recv()
            spot = out_rows(u, core, 0, half)
            send(spot, spot, sems(width), on_core(), top(half))
        else:
            got = out_rows(u, 1 - core, 0, half)
            remote(got, got, sems(width), on_core()).wait_recv()

    progress = {}

    def step(u):
        reduce_step(u, progress[u])
        progress[u] += 1

    schedule = iter(SCHEDULE)

    def slot():
        for u in next(schedule):
            step(u)

    def slots_in(i):
        for q in range(T // R):
            units = next(schedule)
            if units:

                @pl.when(i == q)
                def _():
                    for u in units:
                        step(u)

    def gather_step(n, s):
        sems = lambda slot: (gs_sem, gr_sem, (n, slot))
        if s == 0:
            own = gat_ref.at[n, bo, bi]
            for o in range(1, inner):
                send(own, own, sems(o - 1), on_inner(o))
        elif s == 1:
            for o in range(1, inner):
                got = gat_ref.at[n, bo, lax.rem(bi + inner - o, inner)]
                remote(got, got, sems(o - 1), on_inner(o)).wait_recv()
            own = gat_ref.at[n, bo]
            for o in range(1, OUTER):
                send(own, own, sems(inner - 1 + o - 1), on_outer(o))
        else:
            for o in range(1, OUTER):
                got = gat_ref.at[n, lax.rem(bo + OUTER - o, OUTER)]
                remote(got, got, sems(inner - 1 + o - 1), on_outer(o)).wait_recv()

    def backward_conv(n):
        st[...] = jnp.zeros_like(st)
        coef[0:32, 0 : 2 * C] = split3(jnp.concatenate([sv[n, 0], sv[n, 1]], axis=1))
        @pl.loop(0, T // R)
        def _(i):
            slots_in(i)
            rows = pl.ds(at(i), R)
            if n < 3:
                shift_rows(i)
            da = (
                dot_back(x3[rows, 0:C], cw[n, 0:C, :])
                + dot_back(x3[rows, C : 2 * C], cw[n, C : 2 * C, :])
                + dot_back(x3[rows, 2 * C : 3 * C], cw[n, 2 * C : 3 * C, :])
            )
            spread_out = dot(mem[rows, :], coef[:, 0 : 2 * C])
            d = value(n, rows)
            h = spread_out[:, 0:C] * d + spread_out[:, C : 2 * C]
            th = jnp.tanh(h)
            dy = da * ((0.5 + 0.5 * th) * (1.0 + h - h * th))
            dyb[rows, :] = dy
            add_stats(rows, dy, dy * d)

    def backward_send(n):
        scale, mean = sv[n, 2], sv[n, 3]
        s1, s2 = st[0:8, 0:C], st[0:8, C : 2 * C]
        bx[n, time, 0:4, :] = (scale * (s2 - mean * s1))[0:4]
        bx[n, time, 4:8, :] = s1[0:4]
        bx[n, time, 8:9, :] = dyb[0:1, :]
        bx[n, time, 9:10, :] = dyb[T - 1 : T, :]
        bx[n, time, 10:11, :] = brow[0:1, :]
        bx[n, time, 11:16, :] = jnp.zeros((5, C), F32)
        exchange(bx.at[n], 4 + n, n % 2 == 1)

    def weight_grad(n):
        for side in range(2):
            lane = (core if side else 1 - core) * half
            left = asave[n, :, pl.ds(pl.multiple_of(lane, half), half)]
            for k in range(3):
                u = 3 * n + k
                g = dot_rows(left, x3[:, k * C : (k + 1) * C]).astype(BF16)
                if side:
                    wkeep[u] = g
                else:
                    wsnd[u] = g
                    progress[u] = 0
                    step(u)

    def backward_norm(n):
        exchanged(bx.at[n], 4 + n, n % 2 == 1)
        slot()
        zero4 = jnp.zeros((4, C), F32)
        dgain, dshift = jnp.zeros((4, C), F32), jnp.zeros((4, C), F32)
        bias_row = jnp.zeros((1, C), F32)
        for j in range(members):
            dgain = dgain + bx[n, j, 0:4, :]
            dshift = dshift + bx[n, j, 4:8, :]
            if n % 2 == 1:
                bias_row = bias_row + bx[n, j, 10:11, :]
        dmod = jnp.concatenate([dgain, dshift], axis=1)
        quarter = C // 2
        packet = [dmod[:, q * quarter : (q + 1) * quarter] for q in range(4)]
        packet += [bias_row[:, 0:quarter], bias_row[:, quarter:C]]
        packet += [
            jnp.concatenate([style_ref[0:1, :], style_ref[1:2, :]], axis=1),
            jnp.concatenate([style_ref[2:3, :], style_ref[3:4, :]], axis=1),
            jnp.zeros((12, quarter), F32),
        ]
        gat_ref[n, bo, bi] = jnp.concatenate(packet, axis=0).astype(BF16)
        gather_step(n, 0)
        dmod8 = jnp.concatenate([dmod, jnp.zeros((4, 2 * C), F32)], axis=0)
        part = dot_back(dmod8, fcw[n], highest)[0:UTT]
        if n == 3:
            styleg_ref[...] = part
        else:
            styleg_ref[...] += part
        scale, mean, gain = sv[n, 2], sv[n, 3], sv[n, 4]
        mean_dn = gain * jnp.concatenate([dshift, zero4], axis=0) * inv_totals
        mean_x = gain * jnp.concatenate([dgain, zero4], axis=0) * inv_totals
        alpha = scale * gain
        kappa = -(scale * scale) * mean_x
        delta = -scale * mean_dn - kappa * mean
        coef[0:32, 0 : 3 * C] = split3(jnp.concatenate([alpha, kappa, delta], axis=1))
        p = piv[8 * n : 8 * n + 1, :]

        def edge(dy, raw, own, cot_edge):
            out = (
                pick_row(alpha, own) * dy
                + pick_row(kappa, own) * (raw - p)
                + pick_row(delta, own)
            )
            if n == 2:
                out = (out + cot_edge * root_half) * root_half
            return out

        if n > 0:
            sh[7:8, :] = edge(
                bx[n, before_me, 9:10, :],
                fx[n, before_me, 9:10, :],
                first_own,
                fx[1, before_me, 11:12, :],
            )
            sh[T + 8 : T + 9, :] = edge(
                bx[n, after_me, 8:9, :],
                fx[n, after_me, 8:9, :],
                last_own,
                fx[1, after_me, 10:11, :],
            )
        if n == 2:
            brow[...] = jnp.zeros_like(brow)
        slot()

        @pl.loop(0, T // R)
        def _(i):
            r0 = pl.multiple_of(i * R, R)
            rows = pl.ds(r0, R)
            spread_out = dot(mem[rows, :], coef[...])
            dv = (
                spread_out[:, 0:C] * dyb[rows, :]
                + spread_out[:, C : 2 * C] * value(n, rows)
                + spread_out[:, 2 * C : 3 * C]
            )
            mid = pl.ds(pl.multiple_of(r0 + 8, 8), R)
            if n % 2 == 1:
                sh[mid, :] = dv
            elif n == 2:
                carried = (dv + cot[rows, :].astype(F32) * root_half) * root_half
                vs[2, rows, :] = carried
                sh[mid, :] = carried
                brow[0:1, :] += jnp.sum(carried, axis=0, keepdims=True)
            else:
                phon[rows, :] = (dv + vs[2, rows, :]).astype(BF16)

    for n in (3, 2, 1, 0):
        if n == 3:
            weight_grad(n)
        backward_conv(n)
        slot()
        backward_send(n)
        slot()
        if n == 3:
            forward_conv(n)
        else:
            weight_grad(n)
        slot()
        backward_norm(n)
        slot()
        if n < 3:
            gather_step(n + 1, 1)

    ph = PH // 2
    psnd, pkeep = x3.at[pl.ds(0, ph), 0:C], x3.at[pl.ds(0, ph), C : 2 * C]
    prcv1 = [asave.at[o, pl.ds(0, ph)] for o in range(1, yn)]
    psems = lambda slot: (ps_sem, pr_sem, (slot,))
    for side in range(2):
        lane = pl.multiple_of((core if side else 1 - core) * ph, WIDE)
        block = 256

        @pl.loop(0, ph // block)
        def _(i):
            at = pl.multiple_of(i * block, block)
            lanes = pl.ds(pl.multiple_of(lane + at, WIDE), block)
            g = dot_rows(pick[:, lanes], phon[pl.ds(0, T), :])
            (pkeep if side else psnd)[pl.ds(at, block), :] = g.astype(BF16)

        if side == 0:
            send(psnd, prcv0, psems(0), on_core())
        slot()
    remote(psnd, prcv0, psems(0), on_core()).wait_recv()
    pkeep[...] = (pkeep[...].astype(F32) + prcv0[...].astype(F32)).astype(BF16)
    for o in range(1, yn):
        send(pkeep, prcv1[o - 1], psems(o), on_y(o))
    slot()
    spot = pg_ref.at[pl.ds(pl.multiple_of(core * ph, WIDE), ph)]
    for u in next(schedule):
        if u >= 0:
            step(u)
            continue
        whole = pkeep[...].astype(F32)
        for o in range(1, yn):
            remote(pkeep, prcv1[o - 1], psems(o), on_y(o)).wait_recv()
            whole = whole + prcv1[o - 1][...].astype(F32)
        spot[...] = whole.astype(BF16)
        send(spot, spot, psems(yn), on_core())
        gather_step(0, 1)
    got = pg_ref.at[pl.ds(pl.multiple_of((1 - core) * ph, WIDE), ph)]
    remote(got, got, psems(yn), on_core()).wait_recv()
    for n in range(4):
        gather_step(n, 2)
    drain()


def dot_general_exact(left, right):
    return jnp.dot(left, right, precision=highest, preferred_element_type=F32)


def finish(
    frames_in,
    pg_in,
    style_in,
    gat_in,
    wg_in,
    frames_out,
    pg_out,
    style_out,
    fcg_out,
    fcb_out,
    wg_out,
    bias_out,
    whigh,
    phigh,
    fcg,
    dm,
    styles,
    rsem,
    wsem,
):
    C = frames_in.shape[1]
    half = C // 2
    n_batch = gat_in.shape[1]
    units = [(n, k) for n in range(4) for k in range(3)]
    whole = pltpu.make_async_copy(frames_in, frames_out, rsem.at[0])
    stores = [
        pltpu.make_async_copy(whigh.at[u], wg_out.at[n, pl.ds(k * C, C)], wsem.at[u])
        for u, (n, k) in enumerate(units)
    ]
    pstore = pltpu.make_async_copy(phigh, pg_out, wsem.at[12])
    fstore = pltpu.make_async_copy(fcg, fcg_out, wsem.at[13])
    for u in range(12):
        n, k = units[u]
        whigh[u] = wg_in[n, k * C : (k + 1) * C, :].astype(F32)
        stores[u].start()
    phigh[...] = pg_in[...].astype(F32)
    pstore.start()
    whole.start()
    style_out[...] = style_in[...]
    bias = [jnp.zeros((1, C), F32), jnp.zeros((1, C), F32)]
    for b in range(n_batch):
        pack = gat_in[0, b].astype(F32)
        for side in range(2):
            styles[b * UTT + 2 * side : b * UTT + 2 * side + 1, :] = pack[18 + side : 19 + side, 0:half // 2]
            styles[b * UTT + 2 * side + 1 : b * UTT + 2 * side + 2, :] = pack[18 + side : 19 + side, half // 2 : half]
    for n in range(4):
        for b in range(n_batch):
            pack = gat_in[n, b].astype(F32)
            dm[b * UTT : (b + 1) * UTT, :] = jnp.concatenate(
                [pack[q * UTT : (q + 1) * UTT] for q in range(4)], axis=1
            )
            if n % 2 == 1:
                bias[n // 2] = bias[n // 2] + jnp.concatenate(
                    [pack[16:17], pack[17:18]], axis=1
                )
        fcg[n] = dot_rows(styles[...].astype(BF16), dm[...].astype(BF16))
        fcb_out[n : n + 1, :] = jnp.sum(dm[...], axis=0, keepdims=True)
    bias_out[...] = jnp.concatenate(bias, axis=0)
    fstore.start()
    whole.wait()
    for store in stores + [pstore, fstore]:
        store.wait()


def on_device(
    n_batch,
    members,
    phonemes,
    durations,
    utt_frames,
    style_codes,
    fc_weight,
    fc_bias,
    conv_weight,
    conv_bias,
    cotangent,
):
    T, C = cotangent.shape
    PH = phonemes.shape[0]
    inner = n_batch // OUTER
    yn = members // CORES
    assert inner == yn
    half = C // 2
    VM, ANY = pltpu.VMEM, pl.ANY
    vspec = pl.BlockSpec(memory_space=pltpu.VMEM)
    aspec = pl.BlockSpec(memory_space=pl.ANY)
    most = yn
    r1 = half // most
    nslots = 2 * (yn + inner + OUTER - 2)
    DMA = pltpu.SemaphoreType.DMA
    roomy = PH <= 1024 and members <= 4
    held = VM if roomy else jax.ShapeDtypeStruct
    scratch = [
        VM((PH, C), BF16),
        VM(fc_weight.shape, F32),
        VM(conv_weight.shape, BF16),
        VM((T, C), BF16),
        VM((T, PH), BF16),
        VM((T, WIDE), BF16),
        VM((16, T), BF16),
        VM((T, WIDE), F32),
        VM((T, WIDE), F32),
        VM((T, C), BF16),
        VM((3, T, C), F32),
        VM((32, C), F32),
        VM((4, T, C), BF16),
        VM((T + 16, C), F32),
        VM((T, 3 * C), BF16),
        VM((T, C), F32),
        VM((4, 8, 2 * C), F32),
        VM((4, 5, 8, C), F32),
        VM((WIDE, 3 * C), BF16),
        VM((16, 2 * C), F32),
        VM((8, C), F32),
        VM((4, members, 16, C), F32),
        VM((4, members, 16, C), F32),
        VM((PH // 2, C), BF16),
        VM((12, half, C), BF16),
        VM((12, half, C), BF16),
        VM((12, half, C), BF16),
        VM((12, most - 1, r1, C), BF16),
        VM((12, r1, C), BF16),
        VM((12, max((most - 1) * r1 // most, (OUTER - 1) * r1 // OUTER), C), BF16),
        VM((12, r1 // min(most, OUTER), C), BF16),
        VM((12, (OUTER - 1) * r1 // most, C // OUTER), BF16),
        VM((12, (most - 1) * r1 // OUTER, C // most), BF16),
        VM((12, r1 // most, C // OUTER), BF16),
        VM((12, r1 // OUTER, C // most), BF16),
        DMA((7,)),
        DMA((12,)),
        DMA((8, members)),
        DMA((8, members)),
        DMA((4, inner + OUTER)),
        DMA((4, inner + OUTER)),
        DMA((yn + 1,)),
        DMA((yn + 1,)),
        DMA((12, nslots)),
        DMA((12, nslots)),
    ]
    frames_out, pgrad, style_part, gathered, wgrad = pl.pallas_call(
        functools.partial(kernel, inner, members),
        out_shape=(
            held((T, C), BF16),
            held((PH, C), BF16),
            held(style_codes.shape, F32),
            held((4, OUTER, inner, 32, C // 2), BF16),
            held(conv_weight.shape, BF16),
        ),
        in_specs=[
            aspec,
            vspec,
            pl.BlockSpec(memory_space=pltpu.SMEM),
            vspec,
            aspec,
            vspec,
            aspec,
            vspec,
            aspec,
        ],
        out_specs=[vspec, vspec, vspec, vspec, vspec if roomy else aspec],
        scratch_shapes=scratch,
        compiler_params=pltpu.CompilerParams(
            collective_id=0, has_side_effects=True, vmem_limit_bytes=(54 if roomy else 63) * 1024 * 1024
        ),
    )(
        phonemes,
        durations,
        utt_frames,
        style_codes,
        fc_weight,
        fc_bias,
        conv_weight,
        conv_bias,
        cotangent,
    )
    utts = n_batch * UTT
    return pl.pallas_call(
        finish,
        out_shape=(
            jax.ShapeDtypeStruct((T, C), BF16),
            jax.ShapeDtypeStruct((PH, C), F32),
            jax.ShapeDtypeStruct(style_codes.shape, F32),
            jax.ShapeDtypeStruct(fc_weight.shape, F32),
            jax.ShapeDtypeStruct(fc_bias.shape, F32),
            jax.ShapeDtypeStruct(conv_weight.shape, F32),
            jax.ShapeDtypeStruct(conv_bias.shape, F32),
        ),
        in_specs=[vspec] * 5,
        out_specs=[aspec, aspec, vspec, aspec, vspec, aspec, vspec],
        scratch_shapes=[
            VM((12, C, C), F32),
            VM((PH, C), F32),
            VM(fc_weight.shape, F32),
            VM((utts, 2 * C), F32),
            VM((utts, style_codes.shape[1]), F32),
            DMA((1,)),
            DMA((14,)),
        ],
        compiler_params=pltpu.CompilerParams(vmem_limit_bytes=32 * 1024 * 1024),
    )(frames_out, pgrad, style_part, gathered.reshape(4, n_batch, 32, C // 2), wgrad)


def solution(mesh):
    return jax.shard_map(
        functools.partial(on_device, mesh.shape["batch"], mesh.shape["tm"]),
        mesh=mesh,
        in_specs=(
            P("batch", None),
            P("batch", None),
            P("batch", None),
            P("batch", None),
            P(),
            P(),
            P(),
            P(),
            P(("batch", "tm"), None),
        ),
        out_specs=(
            P(("batch", "tm"), None),
            P("batch", None),
            P("batch", None),
            P(),
            P(),
            P(),
            P(),
        ),
        check_vma=False,
    )
```

```python
import functools
import jax
import jax.numpy as jnp
from jax import lax
from jax.experimental import pallas as pl
from jax.experimental.pallas import tpu as pltpu
from jax.sharding import PartitionSpec as P

F32, BF16 = jnp.float32, jnp.bfloat16
MESH = pl.DeviceIdType.MESH
highest = lax.Precision.HIGHEST
norm_eps = 1e-05
root_half = 0.7071067811865476
UTT = 4
CORES = 2
OUTER = 4
WIDE = 128
ORDERS = ["yxz", "yxz", "xyz", "xyz", "xyz", "xyz", "xyz", "xyz", "xyz", "xyz", "xyz", "xzy"]
SCHEDULE = [
    [9, 10, 11],
    [],
    [],
    [],
    [],
    [],
    [9],
    [],
    [],
    [],
    [],
    [10, 9],
    [11],
    [],
    [6, 7, 10, 8, 9],
    [],
    [],
    [],
    [],
    [11],
    [6, 10],
    [11, 9],
    [4, 7, 3, 6, 5],
    [8, 11, 10],
    [],
    [9],
    [],
    [4, 7],
    [6, 8, 10],
    [3],
    [0, 4, 1, 2, 7, 5, 11],
    [],
    [3, 6],
    [9],
    [8],
    [9],
    [0, 4, 10],
    [7, 10, 1, 3, 2, 5, 8, 6, 11, 4, 7, 11, 0, 2, 3, 1, 8, 5, -2, 4, 6, 3, 0, 6, 2, 7, 7, 1, 8, 5, 8, 0, 4, 2, 4, 1, 3, -1, 3, 0, 5, 2, 1, 0, 5, 0, 5, 1, 2, 1, 2],
]


def dot(left, right):
    return jnp.dot(left, right, preferred_element_type=F32)


def dot_rows(left, right):
    return lax.dot_general(left, right, (((0,), (0,)), ((), ())), preferred_element_type=F32)


def dot_back(left, right, precision=None):
    return lax.dot_general(
        left, right, (((1,), (1,)), ((), ())), precision=precision, preferred_element_type=F32
    )


def kernel(
    inner,
    members,
    phon_hbm,
    dur_ref,
    utt_ref,
    style_ref,
    fcw_hbm,
    fcb_ref,
    cw_hbm,
    cb_ref,
    cot_hbm,
    frames_ref,
    pg_ref,
    styleg_ref,
    gat_ref,
    wg_ref,
    phon,
    fcw,
    cw,
    cot,
    pick,
    uid,
    memt,
    amask,
    bmask,
    x0,
    vs,
    piv,
    asave,
    sh,
    x3,
    dyb,
    mod,
    sv,
    cf,
    st,
    brow,
    dmods,
    bias_rows,
    fx,
    bx,
    prcv0,
    wsnd,
    wkeep,
    wrcv0,
    rcv1,
    acc2,
    rcv2,
    acc3,
    rcv3z,
    rcv3o,
    acc4z,
    acc4o,
    lsem,
    csem,
    xs_sem,
    xr_sem,
    gs_sem,
    gr_sem,
    ps_sem,
    pr_sem,
    ws_sem,
    wr_sem,
):
    T, C = cot_hbm.shape
    PH = phon_hbm.shape[0]
    yn = members // CORES
    batch = lax.axis_index("batch")
    time = lax.axis_index("tm")
    bo, bi = batch // inner, batch % inner
    ty, core = time // CORES, time % CORES
    R, RS = 512, 256
    t0 = time * T

    def at(i):
        return i * R if isinstance(i, int) else pl.multiple_of(i * R, R)

    loads = [
        pltpu.make_async_copy(phon_hbm, phon, lsem.at[0]),
        pltpu.make_async_copy(fcw_hbm, fcw, lsem.at[1]),
        pltpu.make_async_copy(cot_hbm, cot, lsem.at[2]),
    ] + [pltpu.make_async_copy(cw_hbm.at[n], cw.at[n], lsem.at[3 + n]) for n in range(4)]
    for i in (0, 1, 3, 2, 4, 5, 6):
        loads[i].start()

    def on_tm(o):
        return (batch, lax.rem(time + o, members))

    def on_core():
        return (batch, ty * CORES + (1 - core))

    def on_y(o):
        return (batch, lax.rem(ty + o, yn) * CORES + core)

    def on_inner(o):
        return (bo * inner + lax.rem(bi + o, inner), time)

    def on_outer(o):
        return (lax.rem(bo + o, OUTER) * inner + bi, time)

    partners = (
        [on_tm(o) for o in range(1, members)]
        + [on_inner(o) for o in range(1, inner)]
        + [on_outer(o) for o in range(1, OUTER)]
    )
    barrier = pltpu.get_barrier_semaphore()
    for partner in partners:
        pl.semaphore_signal(barrier, inc=1, device_id=partner, device_id_type=MESH)

    def remote(src, dst, sem, device):
        sent, landed, index = sem
        return pltpu.make_async_remote_copy(
            src_ref=src,
            dst_ref=dst,
            send_sem=sent.at[index],
            recv_sem=landed.at[index],
            device_id=device,
            device_id_type=MESH,
        )

    unsent = []

    def send(src, dst, sem, device, like=None):
        remote(src, dst, sem, device).start()
        unsent.append((like or (lambda: src), sem))

    def drain():
        for like, sem in unsent:
            remote(like(), like(), sem, on_core()).wait_send()
        unsent.clear()

    lens = [utt_ref[0, u] for u in range(UTT)]
    starts, ends, total = [], [], 0
    for u in range(UTT):
        starts.append(total)
        total = total + lens[u]
        ends.append(total)
    row8 = lax.broadcasted_iota(jnp.int32, (8, C), 0)

    def by_utt(values, other):
        out = jnp.full((8, C), other, F32)
        for u in range(UTT):
            out = jnp.where(row8 == u, values[u], out)
        return out

    def local_counts(j):
        return by_utt(
            [
                jnp.maximum(jnp.minimum(ends[u], (j + 1) * T) - jnp.maximum(starts[u], j * T), 0)
                .astype(F32)
                for u in range(UTT)
            ],
            0.0,
        )

    totals = by_utt([n.astype(F32) for n in lens], 1.0)
    inv_totals = 1.0 / totals
    mine = local_counts(time)
    inv_mine = 1.0 / jnp.maximum(mine, 1.0)
    counts = [local_counts(j) for j in range(members)]

    def owner_rows(t):
        return [
            jnp.logical_and(t >= starts[u], t < ends[u]).astype(F32) for u in range(UTT)
        ]

    first_own, last_own = owner_rows(t0), owner_rows(t0 + T - 1)

    def pick_row(values, own):
        out = own[0] * values[0:1]
        for u in range(1, UTT):
            out = out + own[u] * values[u : u + 1]
        return out

    @pl.loop(0, T // WIDE)
    def _(i):
        r0 = pl.multiple_of(i * WIDE, WIDE)
        tt = lax.broadcasted_iota(jnp.int32, (16, WIDE), 1) + r0 + t0
        row = lax.broadcasted_iota(jnp.int32, (16, WIDE), 0)
        ownt = jnp.zeros((16, WIDE), F32)
        for u in range(UTT):
            inside = jnp.logical_and(tt >= starts[u], tt < ends[u])
            ownt = jnp.where(jnp.logical_and(inside, row == u), 1.0, ownt)
        memt[:, pl.ds(r0, WIDE)] = ownt.astype(BF16)

    tiles = PH // WIDE
    durs = jnp.concatenate(
        [dur_ref[0:1, j * WIDE : (j + 1) * WIDE] for j in range(tiles)], axis=0
    ).astype(F32)
    upper = (
        lax.broadcasted_iota(jnp.int32, (WIDE, WIDE), 0)
        <= lax.broadcasted_iota(jnp.int32, (WIDE, WIDE), 1)
    ).astype(BF16)
    within = dot(durs.astype(BF16), upper)
    so_far = jnp.zeros((1, 1), F32)
    for j in range(tiles):
        stop = within[j : j + 1] + so_far
        begin = (stop - durs[j : j + 1]).astype(jnp.int32)
        stop = stop.astype(jnp.int32)
        so_far = so_far + within[j : j + 1, WIDE - 1 : WIDE]
        t = lax.broadcasted_iota(jnp.int32, (T, WIDE), 0) + t0
        inside = jnp.logical_and(t >= begin, t < stop)
        pick[:, j * WIDE : (j + 1) * WIDE] = jnp.where(inside, 1.0, 0.0).astype(BF16)

    loads[0].wait()

    @pl.loop(0, T // R)
    def _(i):
        r0 = pl.multiple_of(i * R, R)
        x0[pl.ds(r0, R), :] = dot(pick[pl.ds(r0, R), :], phon[...]).astype(BF16)

    def value(n, rows, lanes=slice(None)):
        if n == 0:
            return x0[rows, lanes].astype(F32) - piv[0:1, lanes]
        return vs[n - 1, rows, lanes]

    LANES = [slice(j * WIDE, (j + 1) * WIDE) for j in range(C // WIDE)]

    def owners(rows):
        own = uid[rows, :]
        return [own < u + 0.5 for u in range(UTT - 1)]

    def by_row(own, table, lanes):
        out = table[UTT - 1 : UTT, lanes]
        for u in range(UTT - 2, -1, -1):
            out = jnp.where(own[u], table[u : u + 1, lanes], out)
        return out

    def add_stats(rows, one, two):
        both = jnp.concatenate([one.astype(BF16), two.astype(BF16)], axis=1)
        st[...] += dot(memt[:, rows], both)

    st[...] = jnp.zeros_like(st)
    piv[0:8, :] = jnp.broadcast_to(x0[0:16, :].astype(F32)[0:1], (8, C))

    @pl.loop(0, T // R)
    def _(i):
        rows = pl.ds(pl.multiple_of(i * R, R), R)
        d = value(0, rows)
        add_stats(rows, d, d * d)

    pl.semaphore_wait(barrier, len(partners))

    def exchange(buf, phase, full):
        for o in range(1, members):
            rows = 16 if full or o in (1, members - 1) else 8
            send(
                buf.at[time, pl.ds(0, rows)],
                buf.at[time, pl.ds(0, rows)],
                (xs_sem, xr_sem, (phase, o)),
                on_tm(o),
            )

    def exchanged(buf, phase, full):
        for o in range(1, members):
            rows = 16 if full or o in (1, members - 1) else 8
            ref = buf.at[lax.rem(time + members - o, members), pl.ds(0, rows)]
            remote(ref, ref, (xs_sem, xr_sem, (phase, o)), on_tm(o)).wait_recv()

    before_me, after_me = lax.rem(time + members - 1, members), lax.rem(time + 1, members)

    def forward_send(n, first, last):
        p = piv[8 * n : 8 * n + 1, :]
        s1, s2 = st[0:8, 0:C], st[0:8, C : 2 * C]
        local = s1 * inv_mine
        fx[n, time, 0:4, :] = (local + p)[0:4]
        fx[n, time, 4:8, :] = (s2 - s1 * local)[0:4]
        fx[n, time, 8:9, :] = first + p
        fx[n, time, 9:10, :] = last + p
        if n == 1:
            loads[2].wait()
            fx[n, time, 10:11, :] = cot[0:16, :].astype(F32)[0:1]
            fx[n, time, 11:12, :] = cot[T - 16 : T, :].astype(F32)[15:16]
            fx[n, time, 12:16, :] = jnp.zeros((4, C), F32)
        else:
            fx[n, time, 10:16, :] = jnp.zeros((6, C), F32)
        exchange(fx.at[n], n, False)

    def forward_norm(n):
        exchanged(fx.at[n], n, False)
        p = piv[8 * n : 8 * n + 1, :]
        zero4 = jnp.zeros((4, C), F32)
        means = [
            jnp.concatenate([fx[n, j, 0:4, :], zero4], axis=0) for j in range(members)
        ]
        mean = counts[0] * means[0]
        for j in range(1, members):
            mean = mean + counts[j] * means[j]
        mean = mean * inv_totals
        spread = jnp.zeros((8, C), F32)
        for j in range(members):
            off = means[j] - mean
            spread = spread + counts[j] * off * off + jnp.concatenate(
                [fx[n, j, 4:8, :], zero4], axis=0
            )
        scale = lax.rsqrt(jnp.maximum(spread * inv_totals, 0.0) + norm_eps)
        gain, shift = 1.0 + mod[n, :, 0:C], mod[n, :, C : 2 * C]
        slope = gain * scale
        mean = mean - p
        half_a, half_b = 0.5 * slope, 0.5 * (shift - slope * mean)
        sv[n, 0] = half_a
        sv[n, 1] = half_b
        sv[n, 2] = scale
        sv[n, 3] = mean
        sv[n, 4] = gain
        def edge(raw, own):
            h = pick_row(half_a, own) * (raw - p) + pick_row(half_b, own)
            return h + h * jnp.tanh(h)

        sh[7:8, :] = edge(fx[n, before_me, 9:10, :], first_own)
        sh[T + 8 : T + 9, :] = edge(fx[n, after_me, 8:9, :], last_own)

        @pl.loop(0, T // RS)
        def _(i):
            r0 = pl.multiple_of(i * RS, RS)
            rows = pl.ds(r0, RS)
            own = owners(rows)
            for lanes in LANES:
                h = by_row(own, sv.at[n, 0], lanes) * value(n, rows, lanes)
                h = h + by_row(own, sv.at[n, 1], lanes)
                a = h + h * jnp.tanh(h)
                sh[pl.ds(pl.multiple_of(r0 + 8, 8), RS), lanes] = a
                asave[n, rows, lanes] = a.astype(BF16)

    def shifted(r0):
        window = sh[pl.ds(r0, R + 16), :]
        rows = pl.ds(r0, R)
        bm = jnp.concatenate([bmask[rows, :]] * (C // WIDE), axis=1)
        am = jnp.concatenate([amask[rows, :]] * (C // WIDE), axis=1)
        return (
            (window[7 : 7 + R] * bm).astype(BF16),
            (window[9 : 9 + R] * am).astype(BF16),
            window[8 : 8 + R],
        )

    def forward_conv(n):
        st[...] = jnp.zeros_like(st)

        def chunk(i):
            r0 = at(i)
            rows = pl.ds(r0, R)
            prev, following, _ = shifted(r0)
            c = dot(jnp.concatenate([prev, asave[n, rows, :], following], axis=1), cw[n])
            if n % 2 == 1:
                b = n // 2
                kept = x0[rows, :].astype(F32) if n == 1 else vs[1, rows, :] + piv[16:17, :]
                c = (c + cb_ref[b : b + 1, :] + kept) * root_half
            if n == 3:
                frames_ref[rows, :] = c.astype(BF16)
                return

            @pl.when(i == 0)
            def _():
                m = jnp.mean(c, axis=0, keepdims=True)
                piv[8 * (n + 1) : 8 * (n + 2), :] = jnp.broadcast_to(m, (8, C))

            d = c - piv[8 * (n + 1) : 8 * (n + 1) + 1, :]
            vs[n, rows, :] = d
            add_stats(rows, d, d * d)

        if n < 3:
            loads[3 + n].wait()
            pl.loop(0, T // R)(chunk)
        else:
            @pl.loop(0, T // R)
            def _(i):
                slots_in(i)
                chunk(i)

    def shift_rows(i):
        r0 = at(i)
        rows = pl.ds(r0, R)
        prev, following, mid = shifted(r0)
        x3[rows, 0:C] = following
        x3[rows, C : 2 * C] = mid.astype(BF16)
        x3[rows, 2 * C : 3 * C] = prev

    def data_grad(n, rows):
        return (
            dot_back(x3[rows, 0:C], cw[n, 0:C, :])
            + dot_back(x3[rows, C : 2 * C], cw[n, C : 2 * C, :])
            + dot_back(x3[rows, 2 * C : 3 * C], cw[n, 2 * C : 3 * C, :])
        )

    def cotangent_rows():
        brow[...] = jnp.zeros_like(brow)

        @pl.loop(0, T // R)
        def _(i):
            r0 = pl.multiple_of(i * R, R)
            g = cot[pl.ds(r0, R), :].astype(F32) * root_half
            sh[pl.ds(pl.multiple_of(r0 + 8, 8), R), :] = g
            brow[0:1, :] += jnp.sum(g, axis=0, keepdims=True)

        sh[7:8, :] = fx[1, before_me, 11:12, :] * root_half
        sh[T + 8 : T + 9, :] = fx[1, after_me, 10:11, :] * root_half
        pl.loop(0, T // R)(shift_rows)

    first16 = x0[0:16, :].astype(F32)
    last16 = x0[T - 16 : T, :].astype(F32)
    p0 = piv[0:1, :]
    forward_send(0, first16[0:1] - p0, last16[15:16] - p0)

    dmods[...] = jnp.zeros_like(dmods)

    @pl.loop(0, T // WIDE)
    def _(i):
        r0 = pl.multiple_of(i * WIDE, WIDE)
        t = lax.broadcasted_iota(jnp.int32, (WIDE, WIDE), 0) + r0 + t0
        before, after = t >= 1, t >= 0
        own = jnp.zeros((WIDE, WIDE), F32)
        for u in range(UTT):
            before = jnp.logical_and(before, t != starts[u])
            after = jnp.logical_and(after, t + 1 != ends[u])
            own = jnp.where(t >= starts[u], float(u), own)
        uid[pl.ds(r0, WIDE), :] = own
        bmask[pl.ds(r0, WIDE), :] = before.astype(F32)
        amask[pl.ds(r0, WIDE), :] = after.astype(F32)

    loads[1].wait()
    style8 = jnp.concatenate(
        [style_ref[...], jnp.zeros((8 - UTT, style_ref.shape[1]), F32)], axis=0
    )
    for n in range(4):
        mod[n] = dot_general_exact(style8, fcw[n]) + fcb_ref[n : n + 1, :]

    for n in range(3):
        forward_norm(n)
        forward_conv(n)
        forward_send(n + 1, vs[n, 0:1, :], vs[n, T - 1 : T, :])
        if n == 1:
            cotangent_rows()
        if n == 2:
            loads[6].wait()

            @pl.loop(0, T // R)
            def _(i):
                rows = pl.ds(at(i), R)
                dyb[rows, :] = data_grad(3, rows)

    forward_norm(3)

    axes = {
        "y": (yn, ty, on_y),
        "x": (inner, bi, on_inner),
        "z": (OUTER, bo, on_outer),
    }
    half = C // 2

    def plan(u):
        return tuple(axes[name] for name in ORDERS[u])

    def out_rows(u, side, start, count):
        n, k = u // 3, u % 3
        base = k * C + side * half + start
        return wg_ref.at[n, pl.ds(pl.multiple_of(base, 16), count)]

    def slots(u):
        (k1, _, _), (k2, _, _), (k3, _, _) = plan(u)
        base = [0, 1, k1, k1 + k2 - 1]
        width = k1 + k2 + k3 - 2
        return base, width

    def reduce_step(u, s):
        (k1, m1, d1), (k2, m2, d2), (k3, m3, d3) = plan(u)
        base, width = slots(u)
        r1, r2, w3 = half // k1, half // k1 // k2, C // k3
        rcv3, acc4 = (rcv3z, acc4z) if ORDERS[u][2] == "z" else (rcv3o, acc4o)
        sems = lambda slot: (ws_sem, wr_sem, (u, slot))

        def band(ref, index, count):
            return ref.at[u, pl.ds(pl.multiple_of(index * count, 16), count)]

        def top(count):
            return lambda: wg_ref.at[u // 3, pl.ds(0, count)]

        def lanes(index):
            return pl.ds(pl.multiple_of(index * w3, WIDE), w3)

        def other(m, k, o):
            return lax.rem(m + o, k)

        def sums(own, k, first, landed, device):
            for o in range(1, k):
                remote(landed(o), landed(o), sems(first + o - 1), device(o)).wait_recv()
            if k == 2:
                return own + landed(1)[...]
            own = own.astype(F32)
            for o in range(1, k):
                own = own + landed(o)[...].astype(F32)
            return own.astype(BF16)

        land1 = lambda o: rcv1.at[u, o - 1]
        land2 = lambda o: band(rcv2, o - 1, r2)
        land3 = lambda o: band(rcv3, o - 1, r2)
        row0 = m1 * r1 + m2 * r2
        if s == 0:
            send(wsnd.at[u], wrcv0.at[u], sems(0), on_core(), lambda: wsnd.at[u])
        elif s == 1:
            remote(wsnd.at[u], wrcv0.at[u], sems(0), on_core()).wait_recv()
            wkeep[u] = wkeep[u] + wrcv0[u]
            for o in range(1, k1):
                send(
                    band(wkeep, other(m1, k1, o), r1),
                    land1(o),
                    sems(base[1] + o - 1),
                    d1(o),
                    lambda: wkeep.at[u, pl.ds(0, r1)],
                )
        elif s == 2:
            own = band(wkeep, m1, r1)[...]
            acc2[u] = sums(own, k1, base[1], land1, d1)
            for o in range(1, k2):
                send(
                    band(acc2, other(m2, k2, o), r2),
                    land2(o),
                    sems(base[2] + o - 1),
                    d2(o),
                    lambda: acc2.at[u, pl.ds(0, r2)],
                )
        elif s == 3:
            own = band(acc2, m2, r2)[...]
            acc3[u, 0:r2] = sums(own, k2, base[2], land2, d2)
            for o in range(1, k3):
                piece = acc3.at[u, pl.ds(0, r2), lanes(other(m3, k3, o))]
                like = lambda: acc3.at[u, pl.ds(0, r2), pl.ds(0, w3)]
                send(piece, land3(o), sems(base[3] + o - 1), d3(o), like)
        elif s == 4:
            own = acc3[u, pl.ds(0, r2), lanes(m3)]
            acc4[u] = sums(own, k3, base[3], land3, d3)
            spot = out_rows(u, core, row0, r2).at[:, lanes(m3)]
            pltpu.make_async_copy(acc4.at[u], spot, csem.at[u]).start()
            for o in range(1, k3):
                send(acc4.at[u], spot, sems(width + base[3] + o - 1), d3(o), lambda: acc4.at[u])
        elif s == 5:
            spot = out_rows(u, core, row0, r2)
            for o in range(1, k3):
                got = spot.at[:, lanes(other(m3, k3, k3 - o))]
                remote(got, got, sems(width + base[3] + o - 1), d3(o)).wait_recv()
            pltpu.make_async_copy(acc4.at[u], spot.at[:, lanes(m3)], csem.at[u]).wait()
            for o in range(1, k2):
                send(spot, spot, sems(width + base[2] + o - 1), d2(o), top(r2))
        elif s == 6:
            for o in range(1, k2):
                got = out_rows(u, core, m1 * r1 + other(m2, k2, k2 - o) * r2, r2)
                remote(got, got, sems(width + base[2] + o - 1), d2(o)).wait_recv()
            spot = out_rows(u, core, m1 * r1, r1)
            for o in range(1, k1):
                send(spot, spot, sems(width + base[1] + o - 1), d1(o), top(r1))
        elif s == 7:
            for o in range(1, k1):
                got = out_rows(u, core, other(m1, k1, k1 - o) * r1, r1)
                remote(got, got, sems(width + base[1] + o - 1), d1(o)).wait_recv()
            spot = out_rows(u, core, 0, half)
            send(spot, spot, sems(width), on_core(), top(half))
        else:
            got = out_rows(u, 1 - core, 0, half)
            remote(got, got, sems(width), on_core()).wait_recv()

    progress = {}

    def step(u):
        reduce_step(u, progress[u])
        progress[u] += 1

    schedule = iter(SCHEDULE)

    def slot():
        for u in next(schedule):
            step(u)

    def slots_in(i):
        for q in range(T // R):
            units = next(schedule)
            if units:

                @pl.when(i == q)
                def _():
                    for u in units:
                        step(u)

    def gather_step(n, s):
        sems = lambda slot: (gs_sem, gr_sem, (n, slot))
        if s == 0:
            own = gat_ref.at[n, bo, bi]
            for o in range(1, inner):
                send(own, own, sems(o - 1), on_inner(o))
        elif s == 1:
            for o in range(1, inner):
                got = gat_ref.at[n, bo, lax.rem(bi + inner - o, inner)]
                remote(got, got, sems(o - 1), on_inner(o)).wait_recv()
            own = gat_ref.at[n, bo]
            for o in range(1, OUTER):
                send(own, own, sems(inner - 1 + o - 1), on_outer(o))
        else:
            for o in range(1, OUTER):
                got = gat_ref.at[n, lax.rem(bo + OUTER - o, OUTER)]
                remote(got, got, sems(inner - 1 + o - 1), on_outer(o)).wait_recv()

    def backward_conv(n):
        st[...] = jnp.zeros_like(st)
        @pl.loop(0, T // R)
        def _(i):
            slots_in(i)
            rows = pl.ds(at(i), R)
            if n < 3:
                shift_rows(i)
            da = dyb if n == 3 else data_grad(n, rows)
            own = owners(rows)
            grads, crosses = [], []
            for lanes in LANES:
                d = value(n, rows, lanes)
                h = by_row(own, sv.at[n, 0], lanes) * d + by_row(own, sv.at[n, 1], lanes)
                th = jnp.tanh(h)
                back = da[rows, lanes] if n == 3 else da[:, lanes]
                dy = back * ((0.5 + 0.5 * th) * (1.0 + h - h * th))
                dyb[rows, lanes] = dy
                grads.append(dy.astype(BF16))
                crosses.append((dy * d).astype(BF16))
            st[...] += dot(memt[:, rows], jnp.concatenate(grads + crosses, axis=1))

    def backward_send(n):
        scale, mean = sv[n, 2], sv[n, 3]
        s1, s2 = st[0:8, 0:C], st[0:8, C : 2 * C]
        packet = [(scale * (s2 - mean * s1))[0:4], s1[0:4], dyb[0:1, :], dyb[T - 1 : T, :]]
        packet += [brow[0:1, :], jnp.zeros((5, C), F32)]
        bx[n, time] = jnp.concatenate(packet, axis=0).astype(BF16)
        exchange(bx.at[n], 4 + n, True)

    def weight_grad(n):
        for side in range(2):
            lane = (core if side else 1 - core) * half
            left = asave[n, :, pl.ds(pl.multiple_of(lane, half), half)]
            for k in range(3):
                u = 3 * n + k
                g = dot_rows(left, x3[:, k * C : (k + 1) * C]).astype(BF16)
                if side:
                    wkeep[u] = g
                else:
                    wsnd[u] = g
                    progress[u] = 0
                    step(u)

    def spread_dmod(n):
        dmod = dmods[n, 0:4, :]
        bias_row = bias_rows[4 * n : 4 * n + 1, :] if n % 2 == 1 else jnp.zeros((1, C), F32)
        quarter = C // 2
        packet = [dmod[:, q * quarter : (q + 1) * quarter] for q in range(4)]
        packet += [bias_row[:, 0:quarter], bias_row[:, quarter:C]]
        packet += [
            jnp.concatenate([style_ref[0:1, :], style_ref[1:2, :]], axis=1),
            jnp.concatenate([style_ref[2:3, :], style_ref[3:4, :]], axis=1),
            jnp.zeros((12, quarter), F32),
        ]
        gat_ref[n, bo, bi] = jnp.concatenate(packet, axis=0).astype(BF16)
        gather_step(n, 0)
        part = dot_back(dmods[n], fcw[n], highest)[0:UTT]
        if n == 3:
            styleg_ref[...] = part
        else:
            styleg_ref[...] += part

    def backward_norm(n):
        exchanged(bx.at[n], 4 + n, True)
        packets = [bx[n, j].astype(F32) for j in range(members)]
        slot()
        zero4 = jnp.zeros((4, C), F32)
        dgain, dshift = jnp.zeros((4, C), F32), jnp.zeros((4, C), F32)
        bias_row = jnp.zeros((1, C), F32)
        for packet in packets:
            dgain = dgain + packet[0:4]
            dshift = dshift + packet[4:8]
            bias_row = bias_row + packet[10:11]
        dmod = jnp.concatenate([dgain, dshift], axis=1)
        dmods[n, 0:4, :] = dmod
        if n % 2 == 1:
            bias_rows[4 * n : 4 * n + 1, :] = bias_row
        scale, mean, gain = sv[n, 2], sv[n, 3], sv[n, 4]
        mean_dn = gain * jnp.concatenate([dshift, zero4], axis=0) * inv_totals
        mean_x = gain * jnp.concatenate([dgain, zero4], axis=0) * inv_totals
        alpha = scale * gain
        kappa = -(scale * scale) * mean_x
        delta = -scale * mean_dn - kappa * mean
        cf[0], cf[1], cf[2] = alpha, kappa, delta
        p = piv[8 * n : 8 * n + 1, :]

        def edge(dy, raw, own, cot_edge):
            out = (
                pick_row(alpha, own) * dy
                + pick_row(kappa, own) * (raw - p)
                + pick_row(delta, own)
            )
            if n == 2:
                out = (out + cot_edge * root_half) * root_half
            return out

        if n > 0:
            sh[7:8, :] = edge(
                bx[n, before_me].astype(F32)[9:10],
                fx[n, before_me, 9:10, :],
                first_own,
                fx[1, before_me, 11:12, :],
            )
            sh[T + 8 : T + 9, :] = edge(
                bx[n, after_me].astype(F32)[8:9],
                fx[n, after_me, 8:9, :],
                last_own,
                fx[1, after_me, 10:11, :],
            )
        if n == 2:
            brow[...] = jnp.zeros_like(brow)
        slot()

        @pl.loop(0, T // RS)
        def _(i):
            r0 = pl.multiple_of(i * RS, RS)
            rows = pl.ds(r0, RS)
            mid = pl.ds(pl.multiple_of(r0 + 8, 8), RS)
            own = owners(rows)
            for lanes in LANES:
                dv = by_row(own, cf.at[0], lanes) * dyb[rows, lanes]
                dv = dv + by_row(own, cf.at[1], lanes) * value(n, rows, lanes)
                dv = dv + by_row(own, cf.at[2], lanes)
                if n % 2 == 1:
                    sh[mid, lanes] = dv
                elif n == 2:
                    carried = (dv + cot[rows, lanes].astype(F32) * root_half) * root_half
                    vs[2, rows, lanes] = carried
                    sh[mid, lanes] = carried
                    brow[0:1, lanes] += jnp.sum(carried, axis=0, keepdims=True)
                else:
                    phon[rows, lanes] = (dv + vs[2, rows, lanes]).astype(BF16)

    for n in (3, 2, 1, 0):
        if n == 3:
            weight_grad(n)
        backward_conv(n)
        slot()
        backward_send(n)
        slot()
        if n == 3:
            forward_conv(n)
        else:
            weight_grad(n)
            spread_dmod(n + 1)
            if n < 2:
                gather_step(n + 2, 1)
        slot()
        backward_norm(n)
        slot()

    ph = PH // 2
    psnd, pkeep = x3.at[pl.ds(0, ph), 0:C], x3.at[pl.ds(0, ph), C : 2 * C]
    prcv1 = [asave.at[o, pl.ds(0, ph)] for o in range(1, yn)]
    psems = lambda slot: (ps_sem, pr_sem, (slot,))
    for side in range(2):
        lane = pl.multiple_of((core if side else 1 - core) * ph, WIDE)
        block = 256

        @pl.loop(0, ph // block)
        def _(i):
            at = pl.multiple_of(i * block, block)
            lanes = pl.ds(pl.multiple_of(lane + at, WIDE), block)
            g = dot_rows(pick[:, lanes], phon[pl.ds(0, T), :])
            (pkeep if side else psnd)[pl.ds(at, block), :] = g.astype(BF16)

        if side == 0:
            send(psnd, prcv0, psems(0), on_core())
            gather_step(1, 1)
        slot()
    remote(psnd, prcv0, psems(0), on_core()).wait_recv()
    pkeep[...] = pkeep[...] + prcv0[...]
    spread_dmod(0)
    slot()
    spot = pg_ref.at[pl.ds(pl.multiple_of(core * ph, WIDE), ph)]
    for u in next(schedule):
        if u >= 0:
            step(u)
            continue
        if u == -2:
            for o in range(1, yn):
                send(pkeep, prcv1[o - 1], psems(o), on_y(o))
            continue
        whole = pkeep[...].astype(F32)
        for o in range(1, yn):
            remote(pkeep, prcv1[o - 1], psems(o), on_y(o)).wait_recv()
            whole = whole + prcv1[o - 1][...].astype(F32)
        spot[...] = whole.astype(BF16)
        send(spot, spot, psems(yn), on_core())
        gather_step(0, 1)
    got = pg_ref.at[pl.ds(pl.multiple_of((1 - core) * ph, WIDE), ph)]
    remote(got, got, psems(yn), on_core()).wait_recv()
    for n in range(4):
        gather_step(n, 2)
    drain()


def dot_general_exact(left, right):
    return jnp.dot(left, right, precision=highest, preferred_element_type=F32)


def finish(
    frames_in,
    pg_in,
    style_in,
    gat_in,
    wg_in,
    frames_out,
    pg_out,
    style_out,
    fcg_out,
    fcb_out,
    wg_out,
    bias_out,
    whigh,
    phigh,
    fcg,
    dm,
    styles,
    rsem,
    wsem,
):
    C = frames_in.shape[1]
    half = C // 2
    n_batch = gat_in.shape[1]
    units = [(n, k) for n in range(4) for k in range(3)]
    whole = pltpu.make_async_copy(frames_in, frames_out, rsem.at[0])
    stores = [
        pltpu.make_async_copy(whigh.at[u], wg_out.at[n, pl.ds(k * C, C)], wsem.at[u])
        for u, (n, k) in enumerate(units)
    ]
    pstore = pltpu.make_async_copy(phigh, pg_out, wsem.at[12])
    fstore = pltpu.make_async_copy(fcg, fcg_out, wsem.at[13])
    for u in range(12):
        n, k = units[u]
        whigh[u] = wg_in[n, k * C : (k + 1) * C, :].astype(F32)
        stores[u].start()
    phigh[...] = pg_in[...].astype(F32)
    pstore.start()
    whole.start()
    style_out[...] = style_in[...]
    bias = [jnp.zeros((1, C), F32), jnp.zeros((1, C), F32)]
    for b in range(n_batch):
        pack = gat_in[0, b].astype(F32)
        for side in range(2):
            styles[b * UTT + 2 * side : b * UTT + 2 * side + 1, :] = pack[18 + side : 19 + side, 0:half // 2]
            styles[b * UTT + 2 * side + 1 : b * UTT + 2 * side + 2, :] = pack[18 + side : 19 + side, half // 2 : half]
    for n in range(4):
        for b in range(n_batch):
            pack = gat_in[n, b].astype(F32)
            dm[b * UTT : (b + 1) * UTT, :] = jnp.concatenate(
                [pack[q * UTT : (q + 1) * UTT] for q in range(4)], axis=1
            )
            if n % 2 == 1:
                bias[n // 2] = bias[n // 2] + jnp.concatenate(
                    [pack[16:17], pack[17:18]], axis=1
                )
        fcg[n] = dot_rows(styles[...].astype(BF16), dm[...].astype(BF16))
        fcb_out[n : n + 1, :] = jnp.sum(dm[...], axis=0, keepdims=True)
    bias_out[...] = jnp.concatenate(bias, axis=0)
    fstore.start()
    whole.wait()
    for store in stores + [pstore, fstore]:
        store.wait()


def on_device(
    n_batch,
    members,
    phonemes,
    durations,
    utt_frames,
    style_codes,
    fc_weight,
    fc_bias,
    conv_weight,
    conv_bias,
    cotangent,
):
    T, C = cotangent.shape
    PH = phonemes.shape[0]
    inner = n_batch // OUTER
    yn = members // CORES
    assert inner == yn
    half = C // 2
    VM, ANY = pltpu.VMEM, pl.ANY
    vspec = pl.BlockSpec(memory_space=pltpu.VMEM)
    aspec = pl.BlockSpec(memory_space=pl.ANY)
    most = yn
    r1 = half // most
    nslots = 2 * (yn + inner + OUTER - 2)
    DMA = pltpu.SemaphoreType.DMA
    roomy = PH <= 1024 and members <= 4
    held = VM if roomy else jax.ShapeDtypeStruct
    scratch = [
        VM((PH, C), BF16),
        VM(fc_weight.shape, F32),
        VM(conv_weight.shape, BF16),
        VM((T, C), BF16),
        VM((T, PH), BF16),
        VM((T, WIDE), F32),
        VM((16, T), BF16),
        VM((T, WIDE), F32),
        VM((T, WIDE), F32),
        VM((T, C), BF16),
        VM((3, T, C), F32),
        VM((32, C), F32),
        VM((4, T, C), BF16),
        VM((T + 16, C), F32),
        VM((T, 3 * C), BF16),
        VM((T, C), F32),
        VM((4, 8, 2 * C), F32),
        VM((4, 5, 8, C), F32),
        VM((3, 8, C), F32),
        VM((16, 2 * C), F32),
        VM((8, C), F32),
        VM((4, 8, 2 * C), F32),
        VM((16, C), F32),
        VM((4, members, 16, C), F32),
        VM((4, members, 16, C), BF16),
        VM((PH // 2, C), BF16),
        VM((12, half, C), BF16),
        VM((12, half, C), BF16),
        VM((12, half, C), BF16),
        VM((12, most - 1, r1, C), BF16),
        VM((12, r1, C), BF16),
        VM((12, max((most - 1) * r1 // most, (OUTER - 1) * r1 // OUTER), C), BF16),
        VM((12, r1 // min(most, OUTER), C), BF16),
        VM((12, (OUTER - 1) * r1 // most, C // OUTER), BF16),
        VM((12, (most - 1) * r1 // OUTER, C // most), BF16),
        VM((12, r1 // most, C // OUTER), BF16),
        VM((12, r1 // OUTER, C // most), BF16),
        DMA((7,)),
        DMA((12,)),
        DMA((8, members)),
        DMA((8, members)),
        DMA((4, inner + OUTER)),
        DMA((4, inner + OUTER)),
        DMA((yn + 1,)),
        DMA((yn + 1,)),
        DMA((12, nslots)),
        DMA((12, nslots)),
    ]
    frames_out, pgrad, style_part, gathered, wgrad = pl.pallas_call(
        functools.partial(kernel, inner, members),
        out_shape=(
            held((T, C), BF16),
            held((PH, C), BF16),
            held(style_codes.shape, F32),
            held((4, OUTER, inner, 32, C // 2), BF16),
            held(conv_weight.shape, BF16),
        ),
        in_specs=[
            aspec,
            vspec,
            pl.BlockSpec(memory_space=pltpu.SMEM),
            vspec,
            aspec,
            vspec,
            aspec,
            vspec,
            aspec,
        ],
        out_specs=[vspec, vspec, vspec, vspec, vspec if roomy else aspec],
        scratch_shapes=scratch,
        compiler_params=pltpu.CompilerParams(
            collective_id=0, has_side_effects=True, vmem_limit_bytes=(54 if roomy else 63) * 1024 * 1024
        ),
    )(
        phonemes,
        durations,
        utt_frames,
        style_codes,
        fc_weight,
        fc_bias,
        conv_weight,
        conv_bias,
        cotangent,
    )
    utts = n_batch * UTT
    return pl.pallas_call(
        finish,
        out_shape=(
            jax.ShapeDtypeStruct((T, C), BF16),
            jax.ShapeDtypeStruct((PH, C), F32),
            jax.ShapeDtypeStruct(style_codes.shape, F32),
            jax.ShapeDtypeStruct(fc_weight.shape, F32),
            jax.ShapeDtypeStruct(fc_bias.shape, F32),
            jax.ShapeDtypeStruct(conv_weight.shape, F32),
            jax.ShapeDtypeStruct(conv_bias.shape, F32),
        ),
        in_specs=[vspec] * 5,
        out_specs=[aspec, aspec, vspec, aspec, vspec, aspec, vspec],
        scratch_shapes=[
            VM((12, C, C), F32),
            VM((PH, C), F32),
            VM(fc_weight.shape, F32),
            VM((utts, 2 * C), F32),
            VM((utts, style_codes.shape[1]), F32),
            DMA((1,)),
            DMA((14,)),
        ],
        compiler_params=pltpu.CompilerParams(vmem_limit_bytes=32 * 1024 * 1024),
    )(frames_out, pgrad, style_part, gathered.reshape(4, n_batch, 32, C // 2), wgrad)


def solution(mesh):
    return jax.shard_map(
        functools.partial(on_device, mesh.shape["batch"], mesh.shape["tm"]),
        mesh=mesh,
        in_specs=(
            P("batch", None),
            P("batch", None),
            P("batch", None),
            P("batch", None),
            P(),
            P(),
            P(),
            P(),
            P(("batch", "tm"), None),
        ),
        out_specs=(
            P(("batch", "tm"), None),
            P("batch", None),
            P("batch", None),
            P(),
            P(),
            P(),
            P(),
        ),
        check_vma=False,
    )
```

```python
import functools
import jax
import jax.numpy as jnp
from jax import lax
from jax.experimental import pallas as pl
from jax.experimental.pallas import tpu as pltpu
from jax.sharding import PartitionSpec as P

F32, BF16 = jnp.float32, jnp.bfloat16
MESH = pl.DeviceIdType.MESH
highest = lax.Precision.HIGHEST
norm_eps = 1e-05
root_half = 0.7071067811865476
UTT = 4
CORES = 2
OUTER = 4
WIDE = 128
ORDERS = ["yxz", "yxz", "xyz", "xyz", "xyz", "xyz", "xyz", "xyz", "xyz", "xyz", "xyz", "xzy"]
SCHEDULE = [
    [9, 10, 11],
    [],
    [],
    [],
    [],
    [],
    [9],
    [],
    [],
    [],
    [],
    [10, 9],
    [11],
    [],
    [6, 7, 10, 8, 9],
    [],
    [],
    [],
    [],
    [11],
    [6, 10],
    [11, 9],
    [4, 7, 3, 6, 5],
    [8, 11, 10],
    [],
    [9],
    [],
    [4, 7],
    [6, 8, 10],
    [3],
    [0, 4, 1, 2, 7, 5, 11],
    [],
    [3, 6],
    [9],
    [8],
    [9],
    [0, 4, 10],
    [7, 10, 1, 3, 2, 5, 8, 6, 11, 4, 7, 11, 0, 2, 3, 1, 8, 5, -2, 4, 6, 3, 0, 6, 2, 7, 7, 1, 8, 5, 8, 0, 4, 2, 4, 1, 3, -1, 3, 0, 5, 2, 1, 0, 5, 0, 5, 1, 2, 1, 2],
]


def dot(left, right):
    return jnp.dot(left, right, preferred_element_type=F32)


def dot_rows(left, right):
    return lax.dot_general(left, right, (((0,), (0,)), ((), ())), preferred_element_type=F32)


def dot_back(left, right, precision=None):
    return lax.dot_general(
        left, right, (((1,), (1,)), ((), ())), precision=precision, preferred_element_type=F32
    )


def kernel(
    inner,
    members,
    phon_hbm,
    dur_ref,
    utt_ref,
    style_ref,
    fcw_hbm,
    fcb_ref,
    cw_hbm,
    cb_ref,
    cot_hbm,
    frames_ref,
    pg_ref,
    styleg_ref,
    gat_ref,
    wg_ref,
    phon,
    fcw,
    cw,
    cot,
    pick,
    uid,
    memt,
    amask,
    bmask,
    x0,
    vs,
    piv,
    asave,
    sh,
    x3,
    dyb,
    mod,
    sv,
    cf,
    st,
    brow,
    dmods,
    bias_rows,
    fx,
    bx,
    prcv0,
    wsnd,
    wkeep,
    wrcv0,
    rcv1,
    acc2,
    rcv2,
    acc3,
    rcv3z,
    rcv3o,
    acc4z,
    acc4o,
    lsem,
    csem,
    xs_sem,
    xr_sem,
    gs_sem,
    gr_sem,
    ps_sem,
    pr_sem,
    ws_sem,
    wr_sem,
):
    T, C = cot_hbm.shape
    PH = phon_hbm.shape[0]
    yn = members // CORES
    batch = lax.axis_index("batch")
    time = lax.axis_index("tm")
    bo, bi = batch // inner, batch % inner
    ty, core = time // CORES, time % CORES
    R, RS = 512, 256
    t0 = time * T

    def at(i):
        return i * R if isinstance(i, int) else pl.multiple_of(i * R, R)

    loads = [
        pltpu.make_async_copy(phon_hbm, phon, lsem.at[0]),
        pltpu.make_async_copy(fcw_hbm, fcw, lsem.at[1]),
        pltpu.make_async_copy(cot_hbm, cot, lsem.at[2]),
    ] + [pltpu.make_async_copy(cw_hbm.at[n], cw.at[n], lsem.at[3 + n]) for n in range(4)]
    for i in (0, 1, 3, 2, 4, 5, 6):
        loads[i].start()

    def on_tm(o):
        return (batch, lax.rem(time + o, members))

    def on_core():
        return (batch, ty * CORES + (1 - core))

    def on_y(o):
        return (batch, lax.rem(ty + o, yn) * CORES + core)

    def on_inner(o):
        return (bo * inner + lax.rem(bi + o, inner), time)

    def on_outer(o):
        return (lax.rem(bo + o, OUTER) * inner + bi, time)

    partners = (
        [on_tm(o) for o in range(1, members)]
        + [on_inner(o) for o in range(1, inner)]
        + [on_outer(o) for o in range(1, OUTER)]
    )
    barrier = pltpu.get_barrier_semaphore()
    for partner in partners:
        pl.semaphore_signal(barrier, inc=1, device_id=partner, device_id_type=MESH)

    def remote(src, dst, sem, device):
        sent, landed, index = sem
        return pltpu.make_async_remote_copy(
            src_ref=src,
            dst_ref=dst,
            send_sem=sent.at[index],
            recv_sem=landed.at[index],
            device_id=device,
            device_id_type=MESH,
        )

    unsent = []

    def send(src, dst, sem, device, like=None):
        remote(src, dst, sem, device).start()
        unsent.append((like or (lambda: src), sem))

    def drain():
        for like, sem in unsent:
            remote(like(), like(), sem, on_core()).wait_send()
        unsent.clear()

    lens = [utt_ref[0, u] for u in range(UTT)]
    starts, ends, total = [], [], 0
    for u in range(UTT):
        starts.append(total)
        total = total + lens[u]
        ends.append(total)
    row8 = lax.broadcasted_iota(jnp.int32, (8, C), 0)

    def by_utt(values, other):
        out = jnp.full((8, C), other, F32)
        for u in range(UTT):
            out = jnp.where(row8 == u, values[u], out)
        return out

    def local_counts(j):
        return by_utt(
            [
                jnp.maximum(jnp.minimum(ends[u], (j + 1) * T) - jnp.maximum(starts[u], j * T), 0)
                .astype(F32)
                for u in range(UTT)
            ],
            0.0,
        )

    totals = by_utt([n.astype(F32) for n in lens], 1.0)
    inv_totals = 1.0 / totals
    mine = local_counts(time)
    inv_mine = 1.0 / jnp.maximum(mine, 1.0)
    counts = [local_counts(j) for j in range(members)]

    def owner_rows(t):
        return [
            jnp.logical_and(t >= starts[u], t < ends[u]).astype(F32) for u in range(UTT)
        ]

    first_own, last_own = owner_rows(t0), owner_rows(t0 + T - 1)

    def pick_row(values, own):
        out = own[0] * values[0:1]
        for u in range(1, UTT):
            out = out + own[u] * values[u : u + 1]
        return out

    @pl.loop(0, T // WIDE)
    def _(i):
        r0 = pl.multiple_of(i * WIDE, WIDE)
        tt = lax.broadcasted_iota(jnp.int32, (16, WIDE), 1) + r0 + t0
        row = lax.broadcasted_iota(jnp.int32, (16, WIDE), 0)
        ownt = jnp.zeros((16, WIDE), F32)
        for u in range(UTT):
            inside = jnp.logical_and(tt >= starts[u], tt < ends[u])
            ownt = jnp.where(jnp.logical_and(inside, row == u), 1.0, ownt)
        memt[:, pl.ds(r0, WIDE)] = ownt.astype(BF16)

    tiles = PH // WIDE
    durs = jnp.concatenate(
        [dur_ref[0:1, j * WIDE : (j + 1) * WIDE] for j in range(tiles)], axis=0
    ).astype(F32)
    upper = (
        lax.broadcasted_iota(jnp.int32, (WIDE, WIDE), 0)
        <= lax.broadcasted_iota(jnp.int32, (WIDE, WIDE), 1)
    ).astype(BF16)
    within = dot(durs.astype(BF16), upper)
    so_far = jnp.zeros((1, 1), F32)
    for j in range(tiles):
        stop = within[j : j + 1] + so_far
        begin = (stop - durs[j : j + 1]).astype(jnp.int32)
        stop = stop.astype(jnp.int32)
        so_far = so_far + within[j : j + 1, WIDE - 1 : WIDE]
        t = lax.broadcasted_iota(jnp.int32, (T, WIDE), 0) + t0
        inside = jnp.logical_and(t >= begin, t < stop)
        pick[:, j * WIDE : (j + 1) * WIDE] = jnp.where(inside, 1.0, 0.0).astype(BF16)

    loads[0].wait()

    @pl.loop(0, T // R)
    def _(i):
        r0 = pl.multiple_of(i * R, R)
        x0[pl.ds(r0, R), :] = dot(pick[pl.ds(r0, R), :], phon[...]).astype(BF16)

    def value(n, rows, lanes=slice(None)):
        if n == 0:
            return x0[rows, lanes].astype(F32) - piv[0:1, lanes]
        return vs[n - 1, rows, lanes]

    LANES = [slice(j * WIDE, (j + 1) * WIDE) for j in range(C // WIDE)]

    def owners(rows):
        own = uid[rows, :]
        return [own < u + 0.5 for u in range(UTT - 1)]

    def by_row(own, table, lanes):
        out = table[UTT - 1 : UTT, lanes]
        for u in range(UTT - 2, -1, -1):
            out = jnp.where(own[u], table[u : u + 1, lanes], out)
        return out

    def add_stats(rows, one, two):
        both = jnp.concatenate([one.astype(BF16), two.astype(BF16)], axis=1)
        st[...] += dot(memt[:, rows], both)

    st[...] = jnp.zeros_like(st)
    piv[0:8, :] = jnp.broadcast_to(x0[0:16, :].astype(F32)[0:1], (8, C))

    @pl.loop(0, T // R)
    def _(i):
        rows = pl.ds(pl.multiple_of(i * R, R), R)
        d = value(0, rows)
        add_stats(rows, d, d * d)

    pl.semaphore_wait(barrier, len(partners))

    def exchange(buf, phase, full):
        for o in sorted(range(1, members), key=lambda o: abs(2 * o - members)):
            rows = 16 if full or o in (1, members - 1) else 8
            send(
                buf.at[time, pl.ds(0, rows)],
                buf.at[time, pl.ds(0, rows)],
                (xs_sem, xr_sem, (phase, o)),
                on_tm(o),
            )

    def exchanged(buf, phase, full):
        for o in range(1, members):
            rows = 16 if full or o in (1, members - 1) else 8
            ref = buf.at[lax.rem(time + members - o, members), pl.ds(0, rows)]
            remote(ref, ref, (xs_sem, xr_sem, (phase, o)), on_tm(o)).wait_recv()

    before_me, after_me = lax.rem(time + members - 1, members), lax.rem(time + 1, members)

    def forward_send(n, first, last):
        p = piv[8 * n : 8 * n + 1, :]
        s1, s2 = st[0:8, 0:C], st[0:8, C : 2 * C]
        local = s1 * inv_mine
        fx[n, time, 0:4, :] = (local + p)[0:4]
        fx[n, time, 4:8, :] = (s2 - s1 * local)[0:4]
        fx[n, time, 8:9, :] = first + p
        fx[n, time, 9:10, :] = last + p
        if n == 1:
            loads[2].wait()
            fx[n, time, 10:11, :] = cot[0:16, :].astype(F32)[0:1]
            fx[n, time, 11:12, :] = cot[T - 16 : T, :].astype(F32)[15:16]
            fx[n, time, 12:16, :] = jnp.zeros((4, C), F32)
        else:
            fx[n, time, 10:16, :] = jnp.zeros((6, C), F32)
        exchange(fx.at[n], n, False)

    def forward_norm(n):
        exchanged(fx.at[n], n, False)
        p = piv[8 * n : 8 * n + 1, :]
        zero4 = jnp.zeros((4, C), F32)
        means = [
            jnp.concatenate([fx[n, j, 0:4, :], zero4], axis=0) for j in range(members)
        ]
        mean = counts[0] * means[0]
        for j in range(1, members):
            mean = mean + counts[j] * means[j]
        mean = mean * inv_totals
        spread = jnp.zeros((8, C), F32)
        for j in range(members):
            off = means[j] - mean
            spread = spread + counts[j] * off * off + jnp.concatenate(
                [fx[n, j, 4:8, :], zero4], axis=0
            )
        scale = lax.rsqrt(jnp.maximum(spread * inv_totals, 0.0) + norm_eps)
        gain, shift = 1.0 + mod[n, :, 0:C], mod[n, :, C : 2 * C]
        slope = gain * scale
        mean = mean - p
        half_a, half_b = 0.5 * slope, 0.5 * (shift - slope * mean)
        sv[n, 0] = half_a
        sv[n, 1] = half_b
        sv[n, 2] = scale
        sv[n, 3] = mean
        sv[n, 4] = gain
        def edge(raw, own):
            h = pick_row(half_a, own) * (raw - p) + pick_row(half_b, own)
            return h + h * jnp.tanh(h)

        sh[7:8, :] = edge(fx[n, before_me, 9:10, :], first_own)
        sh[T + 8 : T + 9, :] = edge(fx[n, after_me, 8:9, :], last_own)

        @pl.loop(0, T // RS)
        def _(i):
            r0 = pl.multiple_of(i * RS, RS)
            rows = pl.ds(r0, RS)
            own = owners(rows)
            for lanes in LANES:
                h = by_row(own, sv.at[n, 0], lanes) * value(n, rows, lanes)
                h = h + by_row(own, sv.at[n, 1], lanes)
                a = h + h * jnp.tanh(h)
                sh[pl.ds(pl.multiple_of(r0 + 8, 8), RS), lanes] = a
                asave[n, rows, lanes] = a.astype(BF16)

    def shifted(r0):
        window = sh[pl.ds(r0, R + 16), :]
        rows = pl.ds(r0, R)
        bm = jnp.concatenate([bmask[rows, :]] * (C // WIDE), axis=1)
        am = jnp.concatenate([amask[rows, :]] * (C // WIDE), axis=1)
        return (
            (window[7 : 7 + R] * bm).astype(BF16),
            (window[9 : 9 + R] * am).astype(BF16),
            window[8 : 8 + R],
        )

    def forward_conv(n):
        st[...] = jnp.zeros_like(st)

        def chunk(i):
            r0 = at(i)
            rows = pl.ds(r0, R)
            prev, following, _ = shifted(r0)
            c = dot(jnp.concatenate([prev, asave[n, rows, :], following], axis=1), cw[n])
            if n % 2 == 1:
                b = n // 2
                kept = x0[rows, :].astype(F32) if n == 1 else vs[1, rows, :] + piv[16:17, :]
                c = (c + cb_ref[b : b + 1, :] + kept) * root_half
            if n == 3:
                frames_ref[rows, :] = c.astype(BF16)
                return

            @pl.when(i == 0)
            def _():
                m = jnp.mean(c, axis=0, keepdims=True)
                piv[8 * (n + 1) : 8 * (n + 2), :] = jnp.broadcast_to(m, (8, C))

            d = c - piv[8 * (n + 1) : 8 * (n + 1) + 1, :]
            vs[n, rows, :] = d
            add_stats(rows, d, d * d)

        if n < 3:
            loads[3 + n].wait()
            pl.loop(0, T // R)(chunk)
        else:
            @pl.loop(0, T // R)
            def _(i):
                slots_in(i)
                chunk(i)

    def shift_rows(i):
        r0 = at(i)
        rows = pl.ds(r0, R)
        prev, following, mid = shifted(r0)
        x3[rows, 0:C] = following
        x3[rows, C : 2 * C] = mid.astype(BF16)
        x3[rows, 2 * C : 3 * C] = prev

    def data_grad(n, rows):
        return (
            dot_back(x3[rows, 0:C], cw[n, 0:C, :])
            + dot_back(x3[rows, C : 2 * C], cw[n, C : 2 * C, :])
            + dot_back(x3[rows, 2 * C : 3 * C], cw[n, 2 * C : 3 * C, :])
        )

    def cotangent_rows():
        brow[...] = jnp.zeros_like(brow)

        @pl.loop(0, T // R)
        def _(i):
            r0 = pl.multiple_of(i * R, R)
            g = cot[pl.ds(r0, R), :].astype(F32) * root_half
            sh[pl.ds(pl.multiple_of(r0 + 8, 8), R), :] = g
            brow[0:1, :] += jnp.sum(g, axis=0, keepdims=True)

        sh[7:8, :] = fx[1, before_me, 11:12, :] * root_half
        sh[T + 8 : T + 9, :] = fx[1, after_me, 10:11, :] * root_half
        pl.loop(0, T // R)(shift_rows)

    first16 = x0[0:16, :].astype(F32)
    last16 = x0[T - 16 : T, :].astype(F32)
    p0 = piv[0:1, :]
    forward_send(0, first16[0:1] - p0, last16[15:16] - p0)

    dmods[...] = jnp.zeros_like(dmods)

    @pl.loop(0, T // WIDE)
    def _(i):
        r0 = pl.multiple_of(i * WIDE, WIDE)
        t = lax.broadcasted_iota(jnp.int32, (WIDE, WIDE), 0) + r0 + t0
        before, after = t >= 1, t >= 0
        own = jnp.zeros((WIDE, WIDE), F32)
        for u in range(UTT):
            before = jnp.logical_and(before, t != starts[u])
            after = jnp.logical_and(after, t + 1 != ends[u])
            own = jnp.where(t >= starts[u], float(u), own)
        uid[pl.ds(r0, WIDE), :] = own
        bmask[pl.ds(r0, WIDE), :] = before.astype(F32)
        amask[pl.ds(r0, WIDE), :] = after.astype(F32)

    loads[1].wait()
    style8 = jnp.concatenate(
        [style_ref[...], jnp.zeros((8 - UTT, style_ref.shape[1]), F32)], axis=0
    )
    for n in range(4):
        mod[n] = dot_general_exact(style8, fcw[n]) + fcb_ref[n : n + 1, :]

    for n in range(3):
        forward_norm(n)
        forward_conv(n)
        forward_send(n + 1, vs[n, 0:1, :], vs[n, T - 1 : T, :])
        if n == 1:
            cotangent_rows()
        if n == 2:
            loads[6].wait()

            @pl.loop(0, T // R)
            def _(i):
                rows = pl.ds(at(i), R)
                dyb[rows, :] = data_grad(3, rows)

    forward_norm(3)

    axes = {
        "y": (yn, ty, on_y),
        "x": (inner, bi, on_inner),
        "z": (OUTER, bo, on_outer),
    }
    half = C // 2

    def plan(u):
        return tuple(axes[name] for name in ORDERS[u])

    def out_rows(u, side, start, count):
        n, k = u // 3, u % 3
        base = k * C + side * half + start
        return wg_ref.at[n, pl.ds(pl.multiple_of(base, 16), count)]

    def slots(u):
        (k1, _, _), (k2, _, _), (k3, _, _) = plan(u)
        base = [0, 1, k1, k1 + k2 - 1]
        width = k1 + k2 + k3 - 2
        return base, width

    def reduce_step(u, s):
        (k1, m1, d1), (k2, m2, d2), (k3, m3, d3) = plan(u)
        base, width = slots(u)
        r1, r2, w3 = half // k1, half // k1 // k2, C // k3
        rcv3, acc4 = (rcv3z, acc4z) if ORDERS[u][2] == "z" else (rcv3o, acc4o)
        sems = lambda slot: (ws_sem, wr_sem, (u, slot))

        def band(ref, index, count):
            return ref.at[u, pl.ds(pl.multiple_of(index * count, 16), count)]

        def top(count):
            return lambda: wg_ref.at[u // 3, pl.ds(0, count)]

        def lanes(index):
            return pl.ds(pl.multiple_of(index * w3, WIDE), w3)

        def other(m, k, o):
            return lax.rem(m + o, k)

        def sums(own, k, first, landed, device):
            for o in range(1, k):
                remote(landed(o), landed(o), sems(first + o - 1), device(o)).wait_recv()
            if k == 2:
                return own + landed(1)[...]
            own = own.astype(F32)
            for o in range(1, k):
                own = own + landed(o)[...].astype(F32)
            return own.astype(BF16)

        land1 = lambda o: rcv1.at[u, o - 1]
        land2 = lambda o: band(rcv2, o - 1, r2)
        land3 = lambda o: band(rcv3, o - 1, r2)
        row0 = m1 * r1 + m2 * r2
        if s == 0:
            send(wsnd.at[u], wrcv0.at[u], sems(0), on_core(), lambda: wsnd.at[u])
        elif s == 1:
            remote(wsnd.at[u], wrcv0.at[u], sems(0), on_core()).wait_recv()
            wkeep[u] = wkeep[u] + wrcv0[u]
            for o in range(1, k1):
                send(
                    band(wkeep, other(m1, k1, o), r1),
                    land1(o),
                    sems(base[1] + o - 1),
                    d1(o),
                    lambda: wkeep.at[u, pl.ds(0, r1)],
                )
        elif s == 2:
            own = band(wkeep, m1, r1)[...]
            acc2[u] = sums(own, k1, base[1], land1, d1)
            for o in range(1, k2):
                send(
                    band(acc2, other(m2, k2, o), r2),
                    land2(o),
                    sems(base[2] + o - 1),
                    d2(o),
                    lambda: acc2.at[u, pl.ds(0, r2)],
                )
        elif s == 3:
            own = band(acc2, m2, r2)[...]
            acc3[u, 0:r2] = sums(own, k2, base[2], land2, d2)
            for o in range(1, k3):
                piece = acc3.at[u, pl.ds(0, r2), lanes(other(m3, k3, o))]
                like = lambda: acc3.at[u, pl.ds(0, r2), pl.ds(0, w3)]
                send(piece, land3(o), sems(base[3] + o - 1), d3(o), like)
        elif s == 4:
            own = acc3[u, pl.ds(0, r2), lanes(m3)]
            acc4[u] = sums(own, k3, base[3], land3, d3)
            spot = out_rows(u, core, row0, r2).at[:, lanes(m3)]
            pltpu.make_async_copy(acc4.at[u], spot, csem.at[u]).start()
            for o in range(1, k3):
                send(acc4.at[u], spot, sems(width + base[3] + o - 1), d3(o), lambda: acc4.at[u])
        elif s == 5:
            spot = out_rows(u, core, row0, r2)
            for o in range(1, k3):
                got = spot.at[:, lanes(other(m3, k3, k3 - o))]
                remote(got, got, sems(width + base[3] + o - 1), d3(o)).wait_recv()
            pltpu.make_async_copy(acc4.at[u], spot.at[:, lanes(m3)], csem.at[u]).wait()
            for o in range(1, k2):
                send(spot, spot, sems(width + base[2] + o - 1), d2(o), top(r2))
        elif s == 6:
            for o in range(1, k2):
                got = out_rows(u, core, m1 * r1 + other(m2, k2, k2 - o) * r2, r2)
                remote(got, got, sems(width + base[2] + o - 1), d2(o)).wait_recv()
            spot = out_rows(u, core, m1 * r1, r1)
            for o in range(1, k1):
                send(spot, spot, sems(width + base[1] + o - 1), d1(o), top(r1))
        elif s == 7:
            for o in range(1, k1):
                got = out_rows(u, core, other(m1, k1, k1 - o) * r1, r1)
                remote(got, got, sems(width + base[1] + o - 1), d1(o)).wait_recv()
            spot = out_rows(u, core, 0, half)
            send(spot, spot, sems(width), on_core(), top(half))
        else:
            got = out_rows(u, 1 - core, 0, half)
            remote(got, got, sems(width), on_core()).wait_recv()

    progress = {}

    def step(u):
        reduce_step(u, progress[u])
        progress[u] += 1

    schedule = iter(SCHEDULE)

    def slot():
        for u in next(schedule):
            step(u)

    def slots_in(i):
        for q in range(T // R):
            units = next(schedule)
            if units:

                @pl.when(i == q)
                def _():
                    for u in units:
                        step(u)

    def gather_step(n, s):
        sems = lambda slot: (gs_sem, gr_sem, (n, slot))
        if s == 0:
            own = gat_ref.at[n, bo, bi]
            for o in range(1, inner):
                send(own, own, sems(o - 1), on_inner(o))
        elif s == 1:
            for o in range(1, inner):
                got = gat_ref.at[n, bo, lax.rem(bi + inner - o, inner)]
                remote(got, got, sems(o - 1), on_inner(o)).wait_recv()
            own = gat_ref.at[n, bo]
            for o in range(1, OUTER):
                send(own, own, sems(inner - 1 + o - 1), on_outer(o))
        else:
            for o in range(1, OUTER):
                got = gat_ref.at[n, lax.rem(bo + OUTER - o, OUTER)]
                remote(got, got, sems(inner - 1 + o - 1), on_outer(o)).wait_recv()

    def backward_conv(n):
        st[...] = jnp.zeros_like(st)
        @pl.loop(0, T // R)
        def _(i):
            slots_in(i)
            rows = pl.ds(at(i), R)
            if n < 3:
                shift_rows(i)
            da = dyb if n == 3 else data_grad(n, rows)
            own = owners(rows)
            grads, crosses = [], []
            for lanes in LANES:
                d = value(n, rows, lanes)
                h = by_row(own, sv.at[n, 0], lanes) * d + by_row(own, sv.at[n, 1], lanes)
                th = jnp.tanh(h)
                back = da[rows, lanes] if n == 3 else da[:, lanes]
                dy = back * ((0.5 + 0.5 * th) * (1.0 + h - h * th))
                dyb[rows, lanes] = dy
                grads.append(dy.astype(BF16))
                crosses.append((dy * d).astype(BF16))
            st[...] += dot(memt[:, rows], jnp.concatenate(grads + crosses, axis=1))

    def backward_send(n):
        scale, mean = sv[n, 2], sv[n, 3]
        s1, s2 = st[0:8, 0:C], st[0:8, C : 2 * C]
        packet = [(scale * (s2 - mean * s1))[0:4], s1[0:4], dyb[0:1, :], dyb[T - 1 : T, :]]
        packet += [brow[0:1, :], jnp.zeros((5, C), F32)]
        bx[n, time] = jnp.concatenate(packet, axis=0).astype(BF16)
        exchange(bx.at[n], 4 + n, True)

    def weight_grad(n):
        for side in range(2):
            lane = (core if side else 1 - core) * half
            left = asave[n, :, pl.ds(pl.multiple_of(lane, half), half)]
            for k in range(3):
                u = 3 * n + k
                g = dot_rows(left, x3[:, k * C : (k + 1) * C]).astype(BF16)
                if side:
                    wkeep[u] = g
                else:
                    wsnd[u] = g
                    progress[u] = 0
                    step(u)

    def spread_dmod(n):
        dmod = dmods[n, 0:4, :]
        bias_row = bias_rows[4 * n : 4 * n + 1, :] if n % 2 == 1 else jnp.zeros((1, C), F32)
        quarter = C // 2
        packet = [dmod[:, q * quarter : (q + 1) * quarter] for q in range(4)]
        packet += [bias_row[:, 0:quarter], bias_row[:, quarter:C]]
        packet += [
            jnp.concatenate([style_ref[0:1, :], style_ref[1:2, :]], axis=1),
            jnp.concatenate([style_ref[2:3, :], style_ref[3:4, :]], axis=1),
            jnp.zeros((12, quarter), F32),
        ]
        gat_ref[n, bo, bi] = jnp.concatenate(packet, axis=0).astype(BF16)
        gather_step(n, 0)
        part = dot_back(dmods[n], fcw[n], highest)[0:UTT]
        if n == 3:
            styleg_ref[...] = part
        else:
            styleg_ref[...] += part

    def backward_norm(n):
        exchanged(bx.at[n], 4 + n, True)
        packets = [bx[n, j].astype(F32) for j in range(members)]
        slot()
        zero4 = jnp.zeros((4, C), F32)
        dgain, dshift = jnp.zeros((4, C), F32), jnp.zeros((4, C), F32)
        bias_row = jnp.zeros((1, C), F32)
        for packet in packets:
            dgain = dgain + packet[0:4]
            dshift = dshift + packet[4:8]
            bias_row = bias_row + packet[10:11]
        dmod = jnp.concatenate([dgain, dshift], axis=1)
        dmods[n, 0:4, :] = dmod
        if n % 2 == 1:
            bias_rows[4 * n : 4 * n + 1, :] = bias_row
        scale, mean, gain = sv[n, 2], sv[n, 3], sv[n, 4]
        mean_dn = gain * jnp.concatenate([dshift, zero4], axis=0) * inv_totals
        mean_x = gain * jnp.concatenate([dgain, zero4], axis=0) * inv_totals
        alpha = scale * gain
        kappa = -(scale * scale) * mean_x
        delta = -scale * mean_dn - kappa * mean
        cf[0], cf[1], cf[2] = alpha, kappa, delta
        p = piv[8 * n : 8 * n + 1, :]

        def edge(dy, raw, own, cot_edge):
            out = (
                pick_row(alpha, own) * dy
                + pick_row(kappa, own) * (raw - p)
                + pick_row(delta, own)
            )
            if n == 2:
                out = (out + cot_edge * root_half) * root_half
            return out

        if n > 0:
            sh[7:8, :] = edge(
                bx[n, before_me].astype(F32)[9:10],
                fx[n, before_me, 9:10, :],
                first_own,
                fx[1, before_me, 11:12, :],
            )
            sh[T + 8 : T + 9, :] = edge(
                bx[n, after_me].astype(F32)[8:9],
                fx[n, after_me, 8:9, :],
                last_own,
                fx[1, after_me, 10:11, :],
            )
        if n == 2:
            brow[...] = jnp.zeros_like(brow)
        slot()

        @pl.loop(0, T // RS)
        def _(i):
            r0 = pl.multiple_of(i * RS, RS)
            rows = pl.ds(r0, RS)
            mid = pl.ds(pl.multiple_of(r0 + 8, 8), RS)
            own = owners(rows)
            for lanes in LANES:
                dv = by_row(own, cf.at[0], lanes) * dyb[rows, lanes]
                dv = dv + by_row(own, cf.at[1], lanes) * value(n, rows, lanes)
                dv = dv + by_row(own, cf.at[2], lanes)
                if n % 2 == 1:
                    sh[mid, lanes] = dv
                elif n == 2:
                    carried = (dv + cot[rows, lanes].astype(F32) * root_half) * root_half
                    vs[2, rows, lanes] = carried
                    sh[mid, lanes] = carried
                    brow[0:1, lanes] += jnp.sum(carried, axis=0, keepdims=True)
                else:
                    phon[rows, lanes] = (dv + vs[2, rows, lanes]).astype(BF16)

    for n in (3, 2, 1, 0):
        if n == 3:
            weight_grad(n)
        backward_conv(n)
        slot()
        backward_send(n)
        slot()
        if n == 3:
            forward_conv(n)
        else:
            weight_grad(n)
            spread_dmod(n + 1)
            if n < 2:
                gather_step(n + 2, 1)
        slot()
        backward_norm(n)
        slot()

    ph = PH // 2
    psnd, pkeep = x3.at[pl.ds(0, ph), 0:C], x3.at[pl.ds(0, ph), C : 2 * C]
    prcv1 = [asave.at[o, pl.ds(0, ph)] for o in range(1, yn)]
    psems = lambda slot: (ps_sem, pr_sem, (slot,))
    for side in range(2):
        lane = pl.multiple_of((core if side else 1 - core) * ph, WIDE)
        block = 256

        @pl.loop(0, ph // block)
        def _(i):
            at = pl.multiple_of(i * block, block)
            lanes = pl.ds(pl.multiple_of(lane + at, WIDE), block)
            g = dot_rows(pick[:, lanes], phon[pl.ds(0, T), :])
            (pkeep if side else psnd)[pl.ds(at, block), :] = g.astype(BF16)

        if side == 0:
            send(psnd, prcv0, psems(0), on_core())
            gather_step(1, 1)
        slot()
    remote(psnd, prcv0, psems(0), on_core()).wait_recv()
    pkeep[...] = pkeep[...] + prcv0[...]
    slot()
    spot = pg_ref.at[pl.ds(pl.multiple_of(core * ph, WIDE), ph)]
    for u in next(schedule):
        if u >= 0:
            step(u)
            continue
        if u == -2:
            for o in range(1, yn):
                send(pkeep, prcv1[o - 1], psems(o), on_y(o))
            spread_dmod(0)
            continue
        whole = pkeep[...].astype(F32)
        for o in range(1, yn):
            remote(pkeep, prcv1[o - 1], psems(o), on_y(o)).wait_recv()
            whole = whole + prcv1[o - 1][...].astype(F32)
        spot[...] = whole.astype(BF16)
        send(spot, spot, psems(yn), on_core())
        gather_step(0, 1)
    got = pg_ref.at[pl.ds(pl.multiple_of((1 - core) * ph, WIDE), ph)]
    remote(got, got, psems(yn), on_core()).wait_recv()
    for n in range(4):
        gather_step(n, 2)
    drain()


def dot_general_exact(left, right):
    return jnp.dot(left, right, precision=highest, preferred_element_type=F32)


def finish(
    frames_in,
    pg_in,
    style_in,
    gat_in,
    wg_in,
    frames_out,
    pg_out,
    style_out,
    fcg_out,
    fcb_out,
    wg_out,
    bias_out,
    whigh,
    phigh,
    fcg,
    dm,
    styles,
    rsem,
    wsem,
):
    C = frames_in.shape[1]
    half = C // 2
    n_batch = gat_in.shape[1]
    units = [(n, k) for n in range(4) for k in range(3)]
    whole = pltpu.make_async_copy(frames_in, frames_out, rsem.at[0])
    stores = [
        pltpu.make_async_copy(whigh.at[u], wg_out.at[n, pl.ds(k * C, C)], wsem.at[u])
        for u, (n, k) in enumerate(units)
    ]
    pstore = pltpu.make_async_copy(phigh, pg_out, wsem.at[12])
    fstore = pltpu.make_async_copy(fcg, fcg_out, wsem.at[13])
    for u in range(12):
        n, k = units[u]
        whigh[u] = wg_in[n, k * C : (k + 1) * C, :].astype(F32)
        stores[u].start()
    phigh[...] = pg_in[...].astype(F32)
    pstore.start()
    whole.start()
    style_out[...] = style_in[...]
    bias = [jnp.zeros((1, C), F32), jnp.zeros((1, C), F32)]
    for b in range(n_batch):
        pack = gat_in[0, b].astype(F32)
        for side in range(2):
            styles[b * UTT + 2 * side : b * UTT + 2 * side + 1, :] = pack[18 + side : 19 + side, 0:half // 2]
            styles[b * UTT + 2 * side + 1 : b * UTT + 2 * side + 2, :] = pack[18 + side : 19 + side, half // 2 : half]
    for n in range(4):
        for b in range(n_batch):
            pack = gat_in[n, b].astype(F32)
            dm[b * UTT : (b + 1) * UTT, :] = jnp.concatenate(
                [pack[q * UTT : (q + 1) * UTT] for q in range(4)], axis=1
            )
            if n % 2 == 1:
                bias[n // 2] = bias[n // 2] + jnp.concatenate(
                    [pack[16:17], pack[17:18]], axis=1
                )
        fcg[n] = dot_rows(styles[...].astype(BF16), dm[...].astype(BF16))
        fcb_out[n : n + 1, :] = jnp.sum(dm[...], axis=0, keepdims=True)
    bias_out[...] = jnp.concatenate(bias, axis=0)
    fstore.start()
    whole.wait()
    for store in stores + [pstore, fstore]:
        store.wait()


def on_device(
    n_batch,
    members,
    phonemes,
    durations,
    utt_frames,
    style_codes,
    fc_weight,
    fc_bias,
    conv_weight,
    conv_bias,
    cotangent,
):
    T, C = cotangent.shape
    PH = phonemes.shape[0]
    inner = n_batch // OUTER
    yn = members // CORES
    assert inner == yn
    half = C // 2
    VM, ANY = pltpu.VMEM, pl.ANY
    vspec = pl.BlockSpec(memory_space=pltpu.VMEM)
    aspec = pl.BlockSpec(memory_space=pl.ANY)
    most = yn
    r1 = half // most
    nslots = 2 * (yn + inner + OUTER - 2)
    DMA = pltpu.SemaphoreType.DMA
    roomy = PH <= 1024 and members <= 4
    held = VM if roomy else jax.ShapeDtypeStruct
    scratch = [
        VM((PH, C), BF16),
        VM(fc_weight.shape, F32),
        VM(conv_weight.shape, BF16),
        VM((T, C), BF16),
        VM((T, PH), BF16),
        VM((T, WIDE), F32),
        VM((16, T), BF16),
        VM((T, WIDE), F32),
        VM((T, WIDE), F32),
        VM((T, C), BF16),
        VM((3, T, C), F32),
        VM((32, C), F32),
        VM((4, T, C), BF16),
        VM((T + 16, C), F32),
        VM((T, 3 * C), BF16),
        VM((T, C), F32),
        VM((4, 8, 2 * C), F32),
        VM((4, 5, 8, C), F32),
        VM((3, 8, C), F32),
        VM((16, 2 * C), F32),
        VM((8, C), F32),
        VM((4, 8, 2 * C), F32),
        VM((16, C), F32),
        VM((4, members, 16, C), F32),
        VM((4, members, 16, C), BF16),
        VM((PH // 2, C), BF16),
        VM((12, half, C), BF16),
        VM((12, half, C), BF16),
        VM((12, half, C), BF16),
        VM((12, most - 1, r1, C), BF16),
        VM((12, r1, C), BF16),
        VM((12, max((most - 1) * r1 // most, (OUTER - 1) * r1 // OUTER), C), BF16),
        VM((12, r1 // min(most, OUTER), C), BF16),
        VM((12, (OUTER - 1) * r1 // most, C // OUTER), BF16),
        VM((12, (most - 1) * r1 // OUTER, C // most), BF16),
        VM((12, r1 // most, C // OUTER), BF16),
        VM((12, r1 // OUTER, C // most), BF16),
        DMA((7,)),
        DMA((12,)),
        DMA((8, members)),
        DMA((8, members)),
        DMA((4, inner + OUTER)),
        DMA((4, inner + OUTER)),
        DMA((yn + 1,)),
        DMA((yn + 1,)),
        DMA((12, nslots)),
        DMA((12, nslots)),
    ]
    frames_out, pgrad, style_part, gathered, wgrad = pl.pallas_call(
        functools.partial(kernel, inner, members),
        out_shape=(
            held((T, C), BF16),
            held((PH, C), BF16),
            held(style_codes.shape, F32),
            held((4, OUTER, inner, 32, C // 2), BF16),
            held(conv_weight.shape, BF16),
        ),
        in_specs=[
            aspec,
            vspec,
            pl.BlockSpec(memory_space=pltpu.SMEM),
            vspec,
            aspec,
            vspec,
            aspec,
            vspec,
            aspec,
        ],
        out_specs=[vspec, vspec, vspec, vspec, vspec if roomy else aspec],
        scratch_shapes=scratch,
        compiler_params=pltpu.CompilerParams(
            collective_id=0, has_side_effects=True, vmem_limit_bytes=(54 if roomy else 63) * 1024 * 1024
        ),
    )(
        phonemes,
        durations,
        utt_frames,
        style_codes,
        fc_weight,
        fc_bias,
        conv_weight,
        conv_bias,
        cotangent,
    )
    utts = n_batch * UTT
    return pl.pallas_call(
        finish,
        out_shape=(
            jax.ShapeDtypeStruct((T, C), BF16),
            jax.ShapeDtypeStruct((PH, C), F32),
            jax.ShapeDtypeStruct(style_codes.shape, F32),
            jax.ShapeDtypeStruct(fc_weight.shape, F32),
            jax.ShapeDtypeStruct(fc_bias.shape, F32),
            jax.ShapeDtypeStruct(conv_weight.shape, F32),
            jax.ShapeDtypeStruct(conv_bias.shape, F32),
        ),
        in_specs=[vspec] * 5,
        out_specs=[aspec, aspec, vspec, aspec, vspec, aspec, vspec],
        scratch_shapes=[
            VM((12, C, C), F32),
            VM((PH, C), F32),
            VM(fc_weight.shape, F32),
            VM((utts, 2 * C), F32),
            VM((utts, style_codes.shape[1]), F32),
            DMA((1,)),
            DMA((14,)),
        ],
        compiler_params=pltpu.CompilerParams(vmem_limit_bytes=32 * 1024 * 1024),
    )(frames_out, pgrad, style_part, gathered.reshape(4, n_batch, 32, C // 2), wgrad)


def solution(mesh):
    return jax.shard_map(
        functools.partial(on_device, mesh.shape["batch"], mesh.shape["tm"]),
        mesh=mesh,
        in_specs=(
            P("batch", None),
            P("batch", None),
            P("batch", None),
            P("batch", None),
            P(),
            P(),
            P(),
            P(),
            P(("batch", "tm"), None),
        ),
        out_specs=(
            P(("batch", "tm"), None),
            P("batch", None),
            P("batch", None),
            P(),
            P(),
            P(),
            P(),
        ),
        check_vma=False,
    )
```
